32 devices in a mesh: dp: 16 (over z, y, x), rep: 2 (over core).
Axes of the slice: x: 2, y: 2, z: 4, core: 2. Of those that a mesh axis runs over, the one named last changes fastest.
Arguments:
- event_ids: int32 [32, 12288], P('dp'), may hold values from 0 to 4095, as said below
- row_counts: int32 [32], P('dp'), may hold values from 2 to 4096
- table_slot: int32 [26], replicated, may hold values from 0 to 31, as said below
- dense_input: float32 [12288, 13], P(('dp', 'rep')), may hold values from -6 to 6
- labels: int32 [12288], P(('dp', 'rep')), may hold values 0 or 1
- tables: float32 [32, 4096, 39], P('dp'), may hold values from -3 to 3
- tables_m: float32 [32, 4096, 39], P('dp'), may hold values from -1.5258789e-05 to 1.5258789e-05
- tables_v: float32 [32, 4096, 39], P('dp'), may hold values from 5.9604643e-12 to 2.3841857e-11
- cross_uv: float32 [3, 2, 1027, 256], P(None, None, None, ('dp', 'rep')), may hold values from -0.375 to 0.375
- cross_m: float32 [3, 2, 1027, 256], P(None, None, None, ('dp', 'rep')), may hold values from -0.00010681152 to 0.00010681152
- cross_v: float32 [3, 2, 1027, 256], P(None, None, None, ('dp', 'rep')), may hold values from 3.2552083e-10 to 1.3020833e-09
- tower_in: float32 [1027, 1024], P(None, ('dp', 'rep')), may hold values from -0.1875 to 0.1875
- tower_in_m: float32 [1027, 1024], P(None, ('dp', 'rep')), may hold values from -0.00021362305 to 0.00021362305
- tower_in_v: float32 [1027, 1024], P(None, ('dp', 'rep')), may hold values from 1.3020833e-09 to 5.2083333e-09
- tower_mid: float32 [1024, 1024], P(None, ('dp', 'rep')), may hold values from -0.1875 to 0.1875
- tower_mid_m: float32 [1024, 1024], P(None, ('dp', 'rep')), may hold values from -0.0009765625 to 0.0009765625
- tower_mid_v: float32 [1024, 1024], P(None, ('dp', 'rep')), may hold values from 3.2552084e-08 to 5.2083334e-07
- head_weight: float32 [1024], P(('dp', 'rep')), may hold values from -0.1875 to 0.1875
- head_m: float32 [1024], P(('dp', 'rep')), may hold values from -0.0390625 to 0.0390625
- head_v: float32 [1024], P(('dp', 'rep')), may hold values from 3.98763e-05 to 0.0006380208
- biases: float32 [5130], replicated, may hold values from -0.625 to 0.625
- biases_m: float32 [5130], replicated, may hold values from -0.00030517578 to 0.00030517578
- biases_v: float32 [5130], replicated, may hold values from 2.9296876e-09 to 1.171875e-08
Outputs:
- loss_sum: float32 [], replicated
- new_tables: float32 [32, 4096, 39], P('dp')
- new_tables_m: float32 [32, 4096, 39], P('dp')
- new_tables_v: float32 [32, 4096, 39], P('dp')
- tables_low: bfloat16 [32, 4096, 39], P('dp')
- new_cross: float32 [3, 2, 1027, 256], P(None, None, None, ('dp', 'rep'))
- new_cross_m: float32 [3, 2, 1027, 256], P(None, None, None, ('dp', 'rep'))
- new_cross_v: float32 [3, 2, 1027, 256], P(None, None, None, ('dp', 'rep'))
- cross_low: bfloat16 [3, 2, 1027, 256], P(None, None, None, ('dp', 'rep'))
- new_tower_in: float32 [1027, 1024], P(None, ('dp', 'rep'))
- new_tower_in_m: float32 [1027, 1024], P(None, ('dp', 'rep'))
- new_tower_in_v: float32 [1027, 1024], P(None, ('dp', 'rep'))
- tower_in_low: bfloat16 [1027, 1024], P(None, ('dp', 'rep'))
- new_tower_mid: float32 [1024, 1024], P(None, ('dp', 'rep'))
- new_tower_mid_m: float32 [1024, 1024], P(None, ('dp', 'rep'))
- new_tower_mid_v: float32 [1024, 1024], P(None, ('dp', 'rep'))
- tower_mid_low: bfloat16 [1024, 1024], P(None, ('dp', 'rep'))
- new_head: float32 [1024], P(('dp', 'rep'))
- new_head_m: float32 [1024], P(('dp', 'rep'))
- new_head_v: float32 [1024], P(('dp', 'rep'))
- head_low: bfloat16 [1024], P(('dp', 'rep'))
- new_biases: float32 [5130], replicated
- new_biases_m: float32 [5130], replicated
- new_biases_v: float32 [5130], replicated
- biases_low: bfloat16 [5130], replicated
The draws below stay inside these ranges and needn't reach their ends.
Inputs may be any that keep to these rules, and one draw needn't show every extreme that they name: event_ids[s, e] is below row_counts[s]; small ids are rare and ids near the table's end common. `table_slot`: all 26 entries differ.
All inputs are finite; a program needn't handle non-finite values. No bound on the sum of `labels` on one device may be relied on, other than what follows from the above.
Results may differ from the reference program's by a relative error of at most 0.012.
The reference program's roundings to bfloat16 on the way count: a program that leaves them out, or rounds other values in their place, can miss the bound.
Values may be sent and summed in bfloat16 or wider, within the bound.
A program may use at most 128 MiB of HBM per device.

```python
import math
import jax
import jax.numpy as jnp
from jax import lax

TABLES = 26
EMB = 39
DENSE = 13
RANK = 256
HIDDEN_SIZE = 1024
LAYERS = 3
ROWS = 4096
EV_MB = 128
STEP = 5
WIDTH = 1027
BIAS_LEN = 5130
SLOTS_ALL = 32
EVENTS = 12288
N_DP = 16
N_REP = 2


def common_counts(key):
    shift_key, pick_key = jax.random.split(jax.random.fold_in(key, 101))
    shifts = jax.random.randint(shift_key, (SLOTS_ALL,), 0, 6)
    counts = jnp.maximum(ROWS // jnp.left_shift(1, shifts), 2)
    chosen = jax.random.randint(pick_key, (), 0, SLOTS_ALL)
    return jnp.where(jnp.arange(SLOTS_ALL) == chosen, ROWS, counts).astype(jnp.int32)


def draw_row_counts(key, part):
    counts = common_counts(key)
    return counts


def draw_event_ids(key, part):
    counts = common_counts(key)[:, None]
    key = jax.random.fold_in(key, 5)
    left_key, right_key = jax.random.split(key)
    left_draw = jax.random.randint(left_key, (SLOTS_ALL, EVENTS), 0, counts)
    right_draw = jax.random.randint(right_key, (SLOTS_ALL, EVENTS), 0, counts)
    return (counts - 1 - left_draw * right_draw // counts).astype(jnp.int32)


def draw_table_slot(key, part):
    key = jax.random.fold_in(key, 7)
    return jax.random.permutation(key, SLOTS_ALL)[:TABLES].astype(jnp.int32)


def plant(array, own_key, low, high):
    dims = array.shape
    index_at = [jax.random.randint(jax.random.fold_in(own_key, axis), (), 0, dims[axis]) for axis in range(len(dims))]
    array = array.at[tuple(index_at)].set(low)
    longest = dims.index(max(dims))
    index_at[longest] = (index_at[longest] + 1) % dims[longest]
    return array.at[tuple(index_at)].set(high)


def steps_of(key, extent, pieces, least, top_value):
    factor_of, own = 1.0, jax.random.fold_in(key, 6)
    for dim, shards_of in pieces:
        draws = jnp.exp(jax.random.uniform(jax.random.fold_in(own, dim), (shards_of,), jnp.float32, least / len(pieces), top_value / len(pieces)))
        factor_of = factor_of * jnp.repeat(draws, extent[dim] // shards_of).reshape([-1 if axis == dim else 1 for axis in range(len(extent))])
    return factor_of


def bell_draw(stream_key, dims, scale, bound, shards=(), kind=jnp.bfloat16):
    result = jax.random.normal(stream_key, dims, jnp.float32) * scale
    if len(shards) > 0:
        result = steps_of(stream_key, dims, shards, -0.22, 0.18) * result
    return jnp.clip(result, min=-bound, max=bound).astype(kind)


def setup_inputs(seed: int = 0) -> dict:
    keys = jax.random.split(jax.random.key(seed), 24)
    return {
        "event_ids": draw_event_ids(jax.random.fold_in(keys[23], 71), 0),
        "row_counts": draw_row_counts(jax.random.fold_in(keys[23], 71), 0),
        "table_slot": draw_table_slot(jax.random.fold_in(keys[23], 71), 0),
        "dense_input": bell_draw(keys[3], (EVENTS, DENSE), 1.0, 6.0, ((0, 32),), jnp.float32),
        "labels": plant((jax.random.randint(keys[4], (EVENTS,), 0, 4) < 1).astype(jnp.int32), jax.random.fold_in(keys[4], 1), 0, 1),
        "tables": bell_draw(keys[5], (SLOTS_ALL, ROWS, EMB), 0.5, 3.0, ((0, 16),), jnp.float32),
        "tables_m": bell_draw(keys[6], (SLOTS_ALL, ROWS, EMB), (0.03 * EVENTS ** -1), 1.52587890625e-05, ((0, 16),), jnp.float32),
        "tables_v": jnp.clip(jnp.exp(math.log(2.384185730786026e-11) - 1.3862944 * jax.random.uniform(keys[7], (SLOTS_ALL, ROWS, EMB), jnp.float32) ** steps_of(keys[7], (SLOTS_ALL, ROWS, EMB), ((0, 16),), -0.2, 0.2)), 5.960464326965065e-12, 2.384185730786026e-11),
        "cross_uv": bell_draw(keys[8], (LAYERS, 2, WIDTH, RANK), RANK ** -0.5, 0.375, ((3, 32),), jnp.float32),
        "cross_m": bell_draw(keys[9], (LAYERS, 2, WIDTH, RANK), (0.002 * EVENTS ** -0.5), 0.00010681152, ((3, 32),), jnp.float32),
        "cross_v": jnp.clip(jnp.exp(math.log(1.302083330045889e-09) - 1.3862944 * jax.random.uniform(keys[10], (LAYERS, 2, WIDTH, RANK), jnp.float32) ** steps_of(keys[10], (LAYERS, 2, WIDTH, RANK), ((3, 32),), -0.2, 0.2)), 3.2552083251147224e-10, 1.302083330045889e-09),
        "tower_in": bell_draw(keys[11], (WIDTH, HIDDEN_SIZE), WIDTH ** -0.5, 0.1875, ((1, 32),), jnp.float32),
        "tower_in_m": bell_draw(keys[12], (WIDTH, HIDDEN_SIZE), (0.004 * EVENTS ** -0.5), 0.00021362305, ((1, 32),), jnp.float32),
        "tower_in_v": jnp.clip(jnp.exp(math.log(5.208333320183556e-09) - 1.3862944 * jax.random.uniform(keys[13], (WIDTH, HIDDEN_SIZE), jnp.float32) ** steps_of(keys[13], (WIDTH, HIDDEN_SIZE), ((1, 32),), -0.2, 0.2)), 1.302083330045889e-09, 5.208333320183556e-09),
        "tower_mid": bell_draw(keys[14], (HIDDEN_SIZE, HIDDEN_SIZE), HIDDEN_SIZE ** -0.5, 0.1875, ((1, 32),), jnp.float32),
        "tower_mid_m": bell_draw(keys[15], (HIDDEN_SIZE, HIDDEN_SIZE), (0.02 * EVENTS ** -0.5), 0.0009765625, ((1, 32),), jnp.float32),
        "tower_mid_v": jnp.clip(jnp.exp(math.log(5.208333391237829e-07) - 2.7725887 * jax.random.uniform(keys[16], (HIDDEN_SIZE, HIDDEN_SIZE), jnp.float32) ** steps_of(keys[16], (HIDDEN_SIZE, HIDDEN_SIZE), ((1, 32),), -0.2, 0.2)), 3.2552083695236433e-08, 5.208333391237829e-07),
        "head_weight": bell_draw(keys[17], (HIDDEN_SIZE,), HIDDEN_SIZE ** -0.5, 0.1875, ((0, 32),), jnp.float32),
        "head_m": bell_draw(keys[18], (HIDDEN_SIZE,), (0.7 * EVENTS ** -0.5), 0.0390625, ((0, 32),), jnp.float32),
        "head_v": jnp.clip(jnp.exp(math.log(0.0006380208) - 2.7725887 * jax.random.uniform(keys[19], (HIDDEN_SIZE,), jnp.float32) ** steps_of(keys[19], (HIDDEN_SIZE,), ((0, 32),), -0.2, 0.2)), 3.9876300434116274e-05, 0.0006380208),
        "biases": bell_draw(keys[20], (BIAS_LEN,), 0.1, 0.625, (), jnp.float32),
        "biases_m": bell_draw(keys[21], (BIAS_LEN,), (0.006 * EVENTS ** -0.5), 0.00030517578, (), jnp.float32),
        "biases_v": jnp.clip(jnp.exp(jax.random.uniform(keys[22], (BIAS_LEN,), jnp.float32, math.log(2.9296876036255526e-09), math.log(1.171875041450221e-08))), 2.9296876036255526e-09, 1.171875041450221e-08),
    }


BETA_ONE = 0.5
BETA_TWO = 0.5
EPSILON = 1e-10
WEIGHT_DECAY = 0.01
RATE_DENSE = 0.01
RATE_BIAS = 0.05
RATE_TABLE = 0.2
HIGHEST_PRECISION = lax.Precision.HIGHEST

@jax.custom_vjp
def low(v):
    return lax.optimization_barrier(v.astype(jnp.bfloat16)).astype(jnp.float32)

@jax.custom_vjp
def low_back(v):
    return v

def low_keep(v):
    return (low(v), None)

def low_pass(kept, grad):
    return (grad,)

def back_keep(v):
    return (v, None)

def back_low(kept, grad):
    return (low(grad),)
low.defvjp(low_keep, low_pass)
low_back.defvjp(back_keep, back_low)

def matmul(left_side, right_side):
    return jnp.dot(left_side, right_side, precision=HIGHEST_PRECISION, preferred_element_type=jnp.float32)

def block_loss(weight_set, sel_tables, sel_ids, dense_input, labels, offset, block_rows):
    cross_uv, tower_in, tower_mid, head_weight, biases = weight_set
    row_index = lax.dynamic_slice_in_dim(sel_ids, offset, block_rows, 1)
    looked = jax.vmap(lambda lookup_table, positions: jnp.take(lookup_table, positions, axis=0))(sel_tables, row_index)
    embedded = low_back(looked)
    emb_flat = jnp.transpose(embedded, (1, 0, 2)).reshape(block_rows, TABLES * EMB)
    dense_rows = low(lax.dynamic_slice_in_dim(dense_input, offset, block_rows, 0))
    anchor = jnp.concatenate([emb_flat, dense_rows], axis=1)
    layer_bias = biases[:LAYERS * WIDTH].reshape(LAYERS, WIDTH)
    bias_one = biases[LAYERS * WIDTH:LAYERS * WIDTH + HIDDEN_SIZE]
    bias_two = biases[LAYERS * WIDTH + HIDDEN_SIZE:LAYERS * WIDTH + 2 * HIDDEN_SIZE]
    bias_out = biases[LAYERS * WIDTH + 2 * HIDDEN_SIZE]
    carried = anchor
    for which_layer in range(LAYERS):
        project = low_back(matmul(low(carried), cross_uv[which_layer, 0]))
        crossed = low_back(matmul(low(project), cross_uv[which_layer, 1].T))
        carried = anchor * (crossed + layer_bias[which_layer]) + carried
    pre_one = low_back(matmul(low(carried), tower_in) + bias_one)
    pre_two = low_back(matmul(low(jax.nn.silu(pre_one)), tower_mid) + bias_two)
    logits = matmul(low(jax.nn.silu(pre_two)), head_weight) + bias_out
    target = lax.dynamic_slice_in_dim(labels, offset, block_rows, 0).astype(jnp.float32)
    return jnp.sum(jax.nn.softplus(logits) - target * logits)

def total_loss(weight_set, table_set, event_ids, table_slot, dense_input, labels):
    low_weights = tuple((low(piece) for piece in weight_set[:4])) + (weight_set[4],)
    sel_tables = low(jnp.take(table_set, table_slot, axis=0))
    sel_ids = jnp.take(event_ids, table_slot, axis=0)
    events = labels.shape[0]
    block_rows = EV_MB * N_REP * math.gcd(N_DP, 8)
    starts = jnp.arange(events // block_rows, dtype=jnp.int32) * block_rows

    def add_block(running, offset):
        return (running + block_loss(low_weights, sel_tables, sel_ids, dense_input, labels, offset, block_rows), None)
    summed, unused = lax.scan(jax.checkpoint(add_block), jnp.zeros((), jnp.float32), starts)
    return (summed / events, summed)

def adamw_update(weight, moment_one, moment_two, gradient, step_rate):
    moment_new = BETA_ONE * moment_one + (1 - BETA_ONE) * gradient
    second = BETA_TWO * moment_two + (1 - BETA_TWO) * gradient * gradient
    scaled_one = moment_new / (1 - BETA_ONE ** STEP)
    scaled_two = second / (1 - BETA_TWO ** STEP)
    fresh = weight - step_rate * (scaled_one / (jnp.sqrt(scaled_two) + EPSILON) + WEIGHT_DECAY * weight)
    return (fresh, moment_new, second)

def reference(event_ids, row_counts, table_slot, dense_input, labels, tables, tables_m, tables_v, cross_uv, cross_m, cross_v, tower_in, tower_in_m, tower_in_v, tower_mid, tower_mid_m, tower_mid_v, head_weight, head_m, head_v, biases, biases_m, biases_v):

    def loss_of(weight_set, table_set):
        return total_loss(weight_set, table_set, event_ids, table_slot, dense_input, labels)
    weight_set = (cross_uv, tower_in, tower_mid, head_weight, biases)
    mean_loss, pullback, loss_sum = jax.vjp(loss_of, weight_set, tables, has_aux=True)
    grads, table_grad = pullback(jnp.ones_like(mean_loss))
    fresh_tab, fresh_tab_m, fresh_tab_v = adamw_update(tables, tables_m, tables_v, table_grad, RATE_TABLE)
    in_use = (jnp.arange(ROWS, dtype=jnp.int32)[None, :] < row_counts[:, None])[:, :, None]
    fresh_tab = jnp.where(in_use, fresh_tab, tables)
    fresh_tab_m = jnp.where(in_use, fresh_tab_m, tables_m)
    fresh_tab_v = jnp.where(in_use, fresh_tab_v, tables_v)
    states = ((cross_m, cross_v, RATE_DENSE), (tower_in_m, tower_in_v, RATE_DENSE), (tower_mid_m, tower_mid_v, RATE_DENSE), (head_m, head_v, RATE_DENSE), (biases_m, biases_v, RATE_BIAS))
    results = []
    for weight, gradient, state in zip(weight_set, grads, states):
        fresh, moment_new, second = adamw_update(weight, state[0], state[1], gradient, state[2])
        results.append((fresh, moment_new, second, fresh.astype(jnp.bfloat16)))
    return (loss_sum, fresh_tab, fresh_tab_m, fresh_tab_v, fresh_tab.astype(jnp.bfloat16), results[0][0], results[0][1], results[0][2], results[0][3], results[1][0], results[1][1], results[1][2], results[1][3], results[2][0], results[2][1], results[2][2], results[2][3], results[3][0], results[3][1], results[3][2], results[3][3], results[4][0], results[4][1], results[4][2], results[4][3])
```

```python
import functools
import math

import jax
import jax.numpy as jnp
from jax import lax
from jax.experimental import pallas as pl
from jax.experimental.pallas import tpu as pltpu
from jax.sharding import PartitionSpec as P

TABLES = 26
EMB = 39
HIDDEN_SIZE = 1024
LAYERS = 3
MICRO = 3
STEP = 5
WIDTH = 1027


BETA_ONE = 0.5
BETA_TWO = 0.5
EPSILON = 1e-10
WEIGHT_DECAY = 0.01
RATE_DENSE = 0.01
RATE_BIAS = 0.05
RATE_TABLE = 0.2
HIGHEST_PRECISION = lax.Precision.HIGHEST


def adamw_update(weight, moment_one, moment_two, gradient, step_rate):
    moment_new = BETA_ONE * moment_one + (1 - BETA_ONE) * gradient
    second = BETA_TWO * moment_two + (1 - BETA_TWO) * gradient * gradient
    scaled_one = moment_new / (1 - BETA_ONE**STEP)
    scaled_two = second / (1 - BETA_TWO**STEP)
    fresh = weight - step_rate * (
        scaled_one / (jnp.sqrt(scaled_two) + EPSILON) + WEIGHT_DECAY * weight
    )
    return (fresh, moment_new, second)


def silu_slope(pre_value):
    sigmoid_value = jax.nn.sigmoid(pre_value)
    return sigmoid_value * (1.0 + pre_value * (1.0 - sigmoid_value))


def contract_rows(left_side, right_side):
    return lax.dot_general(
        left_side, right_side, (((0,), (0,)), ((), ())), preferred_element_type=jnp.float32
    )


def contract_cols(left_side, right_side):
    return lax.dot_general(
        left_side, right_side, (((1,), (1,)), ((), ())), preferred_element_type=jnp.float32
    )


def one_hot_rows(positions, row_total):
    return (positions[:, None] == jnp.arange(row_total, dtype=jnp.int32)[None, :]).astype(
        jnp.bfloat16
    )


def lookup_rows(table_piece, positions):
    count = positions.shape[0]
    block = math.gcd(count, 512)
    blocks = positions.reshape(count // block, block)

    def one_block(block_ids):
        return jnp.dot(
            one_hot_rows(block_ids, table_piece.shape[0]),
            table_piece,
            preferred_element_type=jnp.float32,
        ).astype(jnp.bfloat16)

    return lax.map(one_block, blocks).reshape(count, table_piece.shape[1])


def accumulate_rows(entry_rows, positions, row_total):
    count = positions.shape[0]
    block = math.gcd(count, 512)
    blocks = positions.reshape(count // block, block)
    entry_blocks = entry_rows.reshape(count // block, block, entry_rows.shape[1])

    def add_block(running, pair):
        block_ids, block_rows = pair
        return (running + contract_rows(one_hot_rows(block_ids, row_total), block_rows), None)

    start = jnp.zeros((row_total, entry_rows.shape[1]), jnp.float32)
    summed, unused = lax.scan(add_block, start, (blocks, entry_blocks))
    return summed


def cross_forward(anchor, carried, cross_full, layer_bias, which_layer):
    carried_low = carried.astype(jnp.bfloat16)
    project = jnp.dot(
        carried_low, cross_full[which_layer, 0], preferred_element_type=jnp.float32
    ).astype(jnp.bfloat16)
    crossed = contract_cols(project, cross_full[which_layer, 1])
    return (anchor * (crossed + layer_bias[which_layer]) + carried, (carried_low, project, crossed))


def cross_backward(anchor, grad_carried, saved_values, cross_full, layer_bias, which_layer):
    carried_low, project, crossed = saved_values
    grad_cross = grad_carried * anchor
    bias_grad = jnp.sum(grad_cross, axis=0)
    grad_cross_low = grad_cross.astype(jnp.bfloat16)
    grad_up = contract_rows(grad_cross_low, project)
    grad_project = jnp.dot(
        grad_cross_low, cross_full[which_layer, 1], preferred_element_type=jnp.float32
    ).astype(jnp.bfloat16)
    grad_down = contract_rows(carried_low, grad_project)
    grad_input = contract_cols(grad_project, cross_full[which_layer, 0]) + grad_carried
    extra_grad = grad_carried * (crossed + layer_bias[which_layer])
    return (grad_input, extra_grad, jnp.stack([grad_down, grad_up]), bias_grad)


def micro_step(gathered, biases, emb_flat, dense_rows, target, total_events):
    cross_full, tower_full, mid_full, head_full = gathered
    layer_bias = biases[: LAYERS * WIDTH].reshape(LAYERS, WIDTH)
    bias_one = biases[LAYERS * WIDTH : LAYERS * WIDTH + HIDDEN_SIZE]
    bias_two = biases[LAYERS * WIDTH + HIDDEN_SIZE : LAYERS * WIDTH + 2 * HIDDEN_SIZE]
    bias_out = biases[LAYERS * WIDTH + 2 * HIDDEN_SIZE]
    dense_low = lax.optimization_barrier(dense_rows.astype(jnp.bfloat16)).astype(jnp.float32)
    anchor = jnp.concatenate([emb_flat.astype(jnp.float32), dense_low], axis=1)
    carried = anchor
    saved_all = []
    for which_layer in range(LAYERS):
        carried, saved_values = cross_forward(anchor, carried, cross_full, layer_bias, which_layer)
        saved_all.append(saved_values)
    carried_low = carried.astype(jnp.bfloat16)
    pre_one = jnp.dot(carried_low, tower_full, preferred_element_type=jnp.float32) + bias_one
    hidden_one = jax.nn.silu(pre_one).astype(jnp.bfloat16)
    pre_two = jnp.dot(hidden_one, mid_full, preferred_element_type=jnp.float32) + bias_two
    hidden_two = jax.nn.silu(pre_two).astype(jnp.bfloat16)
    logits = jnp.dot(hidden_two, head_full, preferred_element_type=jnp.float32) + bias_out
    loss_part = jnp.sum(jax.nn.softplus(logits) - target * logits)
    grad_logits = (jax.nn.sigmoid(logits) - target) / total_events
    grad_head = jnp.dot(grad_logits, hidden_two.astype(jnp.float32), precision=HIGHEST_PRECISION)
    grad_hidden_two = grad_logits[:, None] * head_full.astype(jnp.float32)[None, :]
    grad_pre_two = (grad_hidden_two * silu_slope(pre_two)).astype(jnp.bfloat16)
    grad_mid = contract_rows(hidden_one, grad_pre_two)
    grad_hidden_one = contract_cols(grad_pre_two, mid_full)
    grad_pre_one = (grad_hidden_one * silu_slope(pre_one)).astype(jnp.bfloat16)
    grad_tower = contract_rows(carried_low, grad_pre_one)
    grad_carried = contract_cols(grad_pre_one, tower_full)
    grad_anchor = jnp.zeros_like(anchor)
    cross_grads = [None] * LAYERS
    layer_grads = [None] * LAYERS
    for which_layer in reversed(range(LAYERS)):
        grad_carried, extra_grad, grad_pair, bias_grad = cross_backward(
            anchor, grad_carried, saved_all[which_layer], cross_full, layer_bias, which_layer
        )
        grad_anchor = grad_anchor + extra_grad
        cross_grads[which_layer] = grad_pair
        layer_grads[which_layer] = bias_grad
    grad_anchor = grad_anchor + grad_carried
    grad_emb = grad_anchor[:, : TABLES * EMB].astype(jnp.bfloat16)
    bias_grads = jnp.concatenate(
        [
            jnp.stack(layer_grads).reshape(-1),
            jnp.sum(grad_pre_one.astype(jnp.float32), axis=0),
            jnp.sum(grad_pre_two.astype(jnp.float32), axis=0),
            jnp.sum(grad_logits)[None],
        ]
    )
    dense_grads = (jnp.stack(cross_grads), grad_tower, grad_mid, grad_head)
    return (loss_part, grad_emb, dense_grads, bias_grads)


def shards(
    event_ids,
    row_counts,
    table_slot,
    dense_input,
    labels,
    tables,
    tables_m,
    tables_v,
    cross_uv,
    cross_m,
    cross_v,
    tower_in,
    tower_in_m,
    tower_in_v,
    tower_mid,
    tower_mid_m,
    tower_mid_v,
    head_weight,
    head_m,
    head_v,
    biases,
    biases_m,
    biases_v,
):
    dp_count = lax.axis_size("dp")
    rep_count = lax.axis_size("rep")
    rep_index = lax.axis_index("rep")
    slot_count = tables.shape[0]
    row_total = tables.shape[1]
    device_events = labels.shape[0]
    micro_events = device_events // MICRO
    total_events = float(device_events * dp_count * rep_count)
    shard_set = (cross_uv, tower_in, tower_mid, head_weight)
    shard_low = tuple((shard_piece.astype(jnp.bfloat16) for shard_piece in shard_set))
    event_grid = event_ids.reshape(slot_count, dp_count, rep_count, MICRO, micro_events)
    own_ids = lax.dynamic_index_in_dim(event_grid, rep_index, 2, keepdims=False)
    table_low = tables.astype(jnp.bfloat16)
    selector = (
        table_slot[:, None] == jnp.arange(dp_count * slot_count, dtype=jnp.int32)[None, :]
    ).astype(jnp.bfloat16)
    loss_total = jnp.zeros((), jnp.float32)
    bias_total = jnp.zeros(biases.shape, jnp.float32)
    table_grad = jnp.zeros(tables.shape, jnp.float32)
    dense_total = None
    for micro_index in range(MICRO):
        gathered = (
            lax.all_gather(shard_low[0], ("dp", "rep"), axis=3, tiled=True),
            lax.all_gather(shard_low[1], ("dp", "rep"), axis=1, tiled=True),
            lax.all_gather(shard_low[2], ("dp", "rep"), axis=1, tiled=True),
            lax.all_gather(shard_low[3], ("dp", "rep"), axis=0, tiled=True),
        )
        micro_ids = own_ids[:, :, micro_index, :].reshape(slot_count, dp_count * micro_events)
        looked = jax.vmap(lookup_rows)(table_low, micro_ids)
        outgoing = jnp.transpose(
            looked.reshape(slot_count, dp_count, micro_events, EMB), (1, 0, 2, 3)
        )
        arrived = lax.all_to_all(outgoing, "dp", split_axis=0, concat_axis=0, tiled=True)
        by_slot = arrived.reshape(dp_count * slot_count, micro_events, EMB)
        picked = jnp.einsum(
            "ts,sec->tec", selector, by_slot, preferred_element_type=jnp.float32
        ).astype(jnp.bfloat16)
        emb_flat = jnp.transpose(picked, (1, 0, 2)).reshape(micro_events, TABLES * EMB)
        row_lo = micro_index * micro_events
        dense_rows = dense_input[row_lo : row_lo + micro_events]
        target = labels[row_lo : row_lo + micro_events].astype(jnp.float32)
        loss_part, grad_emb, dense_grads, bias_grads = micro_step(
            gathered, biases, emb_flat, dense_rows, target, total_events
        )
        loss_total = loss_total + loss_part
        bias_total = bias_total + bias_grads
        if micro_index == 0:
            dense_total = dense_grads
        else:
            dense_total = tuple(
                (running + fresh_part for running, fresh_part in zip(dense_total, dense_grads))
            )
        grad_tables = jnp.transpose(grad_emb.reshape(micro_events, TABLES, EMB), (1, 0, 2))
        slot_grads = jnp.einsum(
            "ts,tec->sec", selector, grad_tables, preferred_element_type=jnp.float32
        ).astype(jnp.bfloat16)
        returned = lax.all_to_all(
            slot_grads.reshape(dp_count, slot_count, micro_events, EMB),
            "dp",
            split_axis=0,
            concat_axis=0,
            tiled=True,
        )
        entries = jnp.transpose(returned, (1, 0, 2, 3)).reshape(
            slot_count, dp_count * micro_events, EMB
        )
        table_grad = table_grad + jax.vmap(
            lambda entry_rows, positions: accumulate_rows(entry_rows, positions, row_total)
        )(entries, micro_ids)
    dense_total = (
        lax.psum_scatter(dense_total[0], ("dp", "rep"), scatter_dimension=3, tiled=True),
        lax.psum_scatter(dense_total[1], ("dp", "rep"), scatter_dimension=1, tiled=True),
        lax.psum_scatter(dense_total[2], ("dp", "rep"), scatter_dimension=1, tiled=True),
        lax.psum_scatter(dense_total[3], ("dp", "rep"), scatter_dimension=0, tiled=True),
    )
    table_grad = lax.psum(table_grad, "rep")
    bias_total, loss_total = lax.psum((bias_total, loss_total), ("dp", "rep"))
    fresh_tab, fresh_tab_m, fresh_tab_v = adamw_update(
        tables, tables_m, tables_v, table_grad, RATE_TABLE
    )
    in_use = (jnp.arange(row_total, dtype=jnp.int32)[None, :] < row_counts[:, None])[:, :, None]
    fresh_tab = jnp.where(in_use, fresh_tab, tables)
    fresh_tab_m = jnp.where(in_use, fresh_tab_m, tables_m)
    fresh_tab_v = jnp.where(in_use, fresh_tab_v, tables_v)
    weight_set = shard_set + (biases,)
    grad_set = tuple(dense_total) + (bias_total,)
    states = (
        (cross_m, cross_v, RATE_DENSE),
        (tower_in_m, tower_in_v, RATE_DENSE),
        (tower_mid_m, tower_mid_v, RATE_DENSE),
        (head_m, head_v, RATE_DENSE),
        (biases_m, biases_v, RATE_BIAS),
    )
    results = []
    for weight, gradient, state in zip(weight_set, grad_set, states):
        fresh, moment_new, second = adamw_update(weight, state[0], state[1], gradient, state[2])
        results.append((fresh, moment_new, second, fresh.astype(jnp.bfloat16)))
    return (
        loss_total,
        fresh_tab,
        fresh_tab_m,
        fresh_tab_v,
        fresh_tab.astype(jnp.bfloat16),
        results[0][0],
        results[0][1],
        results[0][2],
        results[0][3],
        results[1][0],
        results[1][1],
        results[1][2],
        results[1][3],
        results[2][0],
        results[2][1],
        results[2][2],
        results[2][3],
        results[3][0],
        results[3][1],
        results[3][2],
        results[3][3],
        results[4][0],
        results[4][1],
        results[4][2],
        results[4][3],
    )


MESH = pl.DeviceIdType.MESH
F32 = jnp.float32
BF = jnp.bfloat16
LN=1152; RB=112; ZN,YN,XN=4,2,2

def k1_body(ids_ref, tab_ref, cr_ref, ti_ref, tm_ref, hd_ref, G, E, tabr, eout, ss, rs, ess, ers):
    me=lax.axis_index("dp"); r=lax.axis_index("rep")
    x=me%2; y=(me//2)%2; z=me//4
    dev=lambda zz,yy,xx: zz*4+yy*2+xx
    zp=[z+1-2*(z%2),(z+2)%4,3-z]
    own=me*2+r
    bar=pltpu.get_barrier_semaphore()
    for i in range(1,16):
        pl.semaphore_signal(bar,inc=1,device_id=((me+i)%16,r),device_id_type=MESH)
    pl.semaphore_signal(bar,inc=1,device_id=(me,1-r),device_id_type=MESH)
    G[own,0:48,0:1024]=cr_ref[:,0:1024].astype(BF)
    G[own,0:48,1024:LN]=jnp.concatenate([cr_ref[:,1024:1027],jnp.zeros((48,125),F32)],axis=1).astype(BF)
    G[own,48:80,0:1024]=ti_ref[:,0:1024].astype(BF)
    G[own,48:80,1024:LN]=jnp.concatenate([ti_ref[:,1024:1027],jnp.zeros((32,125),F32)],axis=1).astype(BF)
    G[own,80:112,0:1024]=tm_ref[...].astype(BF)
    hcol=jnp.sum(jnp.where(lax.broadcasted_iota(jnp.int32,(32,32),0)==lax.broadcasted_iota(jnp.int32,(32,32),1),jnp.broadcast_to(hd_ref[...],(32,32)),0.0),axis=1,keepdims=True)
    G[own,80:112,1024:LN]=jnp.broadcast_to(hcol,(32,128)).astype(BF)
    pl.semaphore_wait(bar,16)
    parts=((0,48),(48,64))
    cnt=[0,0]; sends=[]
    def mk(p,k,dst,si):
        lo,n=parts[p]
        return pltpu.make_async_remote_copy(src_ref=G.at[k,pl.ds(lo,n)],dst_ref=G.at[k,pl.ds(lo,n)],
            send_sem=ss.at[p,si],recv_sem=rs.at[p,k],device_id=dst,device_id_type=MESH)
    def send(p,k,dst):
        c=mk(p,k,dst,cnt[p]); cnt[p]+=1; c.start(); sends.append(c)
    def wait(p,k): mk(p,k,(me,1-r),0).wait_recv()
    xpeer=(dev(z,y,1-x),r); ypeer=(dev(z,1-y,x),r); core=(me,1-r)
    p1=(ypeer,xpeer); p2=(xpeer,ypeer)
    key=lambda zz,yy,xx: dev(zz,yy,xx)*2+r
    for p in (0,1):
        send(p,own,p1[p]); send(p,own,p2[p])
    for q in zp:
        for p in (0,1): send(p,own,(dev(q,y,x),r))
    for p in (0,1): send(p,own,core)
    for s in range(2):
        for j in range(32):
            g,h=j//4,j%4
            t=tab_ref[pl.ds(2*j+s,39,stride=64),:]
            tabr[s,g*40:(g+1)*40,h*128:(h+1)*128]=jnp.concatenate([t,jnp.zeros((1,128),F32)],axis=0).astype(BF)
    def look(i,_):
        d=(me+i)%16
        off=pl.multiple_of((d*2+r)*384,128)
        idv=ids_ref[:,pl.ds(off,384)]
        outs=[]
        for s in range(2):
            ids=idv[s:s+1]
            lo=ids%512; hi=ids//512
            oh=(lax.broadcasted_iota(jnp.int32,(512,384),0)==lo).astype(F32).astype(BF)
            R=jnp.dot(tabr[s],oh,preferred_element_type=F32)
            e=jnp.zeros((40,384),F32)
            for g in range(8):
                e=e+jnp.where(hi==g,R[g*40:(g+1)*40],0.0)
            outs.append(e)
        eout[d]=jnp.concatenate(outs,axis=0).astype(BF)
        return 0
    def ecopy(i):
        d=(me+i)%16
        return pltpu.make_async_remote_copy(src_ref=eout.at[d],dst_ref=E.at[me],send_sem=ess.at[d],recv_sem=ers.at[me],device_id=(d,r),device_id_type=MESH)
    def step(i,_):
        look(i,0)
        ecopy(i).start()
        return 0
    lax.fori_loop(1,16,step,0)
    look(0,0)
    E[me]=eout[me]
    for q in zp:
        for p in (0,1):
            k=key(q,y,x); wait(p,k)
            send(p,k,p1[p]); send(p,k,p2[p]); send(p,k,core)
    k1f=(lambda zz:key(zz,1-y,x), lambda zz:key(zz,y,1-x))
    for q in [z]+zp:
        for p in (0,1):
            k=k1f[p](q); wait(p,k); send(p,k,p2[p]); send(p,k,core)
    k2f=(lambda zz,o:key(zz,(y+o)%2,1-x), lambda zz,o:key(zz,1-y,(x+o)%2))
    for q in [z]+zp:
        for o in (0,1):
            for p in (0,1):
                k=k2f[p](q,o); wait(p,k); send(p,k,core)
    def ew(i,_):
        d=(me+i)%16
        pltpu.make_async_remote_copy(src_ref=eout.at[d],dst_ref=E.at[d],send_sem=ess.at[d],recv_sem=ers.at[d],device_id=(d,r),device_id_type=MESH).wait()
        return 0
    lax.fori_loop(1,16,ew,0)
    def cw(i,_):
        for p in (0,1): wait(p,i*2+(1-r))
        return 0
    lax.fori_loop(0,16,cw,0)
    for c in sends: c.wait_send()

def k1(ids,tab,cr,ti,tm,hd):
    vm=pl.BlockSpec(memory_space=pltpu.VMEM)
    return pl.pallas_call(k1_body,name="k_one",
        out_shape=(jax.ShapeDtypeStruct((32,RB,LN),BF),jax.ShapeDtypeStruct((16,80,384),BF)),
        in_specs=[vm]*6,out_specs=(vm,vm),
        scratch_shapes=[pltpu.VMEM((2,320,512),BF),pltpu.VMEM((16,80,384),BF),
            pltpu.SemaphoreType.DMA((2,32)),pltpu.SemaphoreType.DMA((2,32)),pltpu.SemaphoreType.DMA((16,)),pltpu.SemaphoreType.DMA((16,))],
        compiler_params=pltpu.CompilerParams(collective_id=0,has_side_effects=True,vmem_limit_bytes=48<<20))(ids,tab,cr,ti,tm,hd)

def tab_view(t):
    S,R,C=t.shape
    return jnp.transpose(jnp.transpose(t,(2,0,1)).reshape(C,S,R//128,128),(0,2,1,3)).reshape(C*S*R//128,128)
def tab_unview(v,S=2,R=4096,C=39):
    return jnp.transpose(jnp.transpose(v.reshape(C,R//128,S,128),(0,2,1,3)).reshape(C,S,R),(1,2,0))
CH=[(0,256),(256,256),(512,256),(768,256),(1024,128)]
def nt(a,b): return lax.dot_general(a,b,(((1,),(1,)),((),())),preferred_element_type=F32)
def nn(a,b): return lax.dot_general(a,b,(((1,),(0,)),((),())),preferred_element_type=F32)
def tn(a,b): return lax.dot_general(a,b,(((0,),(0,)),((),())),preferred_element_type=F32)
def sig(v): return 1.0/(1.0+jnp.exp(-v))
def slope(v):
    s=sig(v); return s*(1.0+v*(1.0-s))

def k2_body(total, ts, G, E, dns, lab, bia, GA, GB, DE, M,
            xT, x0, xr, xl, qc, pr, VT, UT, a1, a2, h1, h2, d1, d2, dx, d0, dql, dpr):
    for t in range(26):
        s=ts[t]
        blk=E[s//2].astype(F32)
        e=jnp.where(s%2==1,blk[40:80],blk[0:40])
        xT[39*t:39*t+39,:]=e[0:39]
    xT[1014:1027,:]=dns[...].astype(BF).astype(F32)
    xT[1027:LN,:]=jnp.zeros((LN-1027,384),F32)
    for i in range(9):
        v=xT[128*i:128*i+128,:].T
        x0[:,128*i:128*i+128]=v
        xl[0,:,128*i:128*i+128]=v.astype(BF)
    for l in range(3):
        for lo,n in CH:
            w=G[:,16*l:16*l+16,lo:lo+n].astype(F32).reshape(32,2,8,n)
            VT[l,:,lo:lo+n]=w[:,0].reshape(256,n).astype(BF)
            UT[l,:,lo:lo+n]=w[:,1].reshape(256,n).astype(BF)
    for l in range(3):
        pr[l]=nt(xl[l],VT[l]).astype(BF)
        src=x0 if l==0 else xr
        for lo,n in CH:
            q=nn(pr[l],UT[l,:,lo:lo+n])+bia[l:l+1,lo:lo+n]
            qc[l,:,lo:lo+n]=q
            v=x0[:,lo:lo+n]*q+src[:,lo:lo+n]
            if l<2: xr[:,lo:lo+n]=v
            xl[l+1,:,lo:lo+n]=v.astype(BF)
    for n in range(4):
        c=slice(256*n,256*n+256)
        a=nt(xl[3],G[8*n:8*n+8,48:80,:].reshape(256,LN))+bia[3:4,c]
        a1[:,c]=a; h1[:,c]=(a*sig(a)).astype(BF)
    for n in range(4):
        c=slice(256*n,256*n+256)
        a=nt(h1[...],G[8*n:8*n+8,80:112,0:1024].reshape(256,1024))+bia[4:5,c]
        a2[:,c]=a; h2[:,c]=(a*sig(a)).astype(BF)
    hc=G[:,80:112,1024:LN].reshape(1024,128)
    z=nn(h2[...],hc)+bia[5:6,0:128]
    y=jnp.broadcast_to(lab[...].astype(F32),(128,384)).T
    lossv=jnp.maximum(z,0.0)+jnp.log1p(jnp.exp(-jnp.abs(z)))-y*z
    dz=(sig(z)-y)/total
    M[...]=jnp.zeros_like(M)
    M[6:7,0:128]=jnp.sum(lossv,axis=0,keepdims=True)
    M[7:8,0:128]=jnp.sum(dz,axis=0,keepdims=True)
    hrow=hc.astype(F32).T[0:1]
    for n in range(8):
        c=slice(128*n,128*n+128)
        M[5:6,c]=jnp.sum(dz*h2[:,c].astype(F32),axis=0,keepdims=True)
        g=(dz*hrow[:,c]*slope(a2[:,c])).astype(BF)
        d2[:,c]=g
        M[4:5,c]=jnp.sum(g.astype(F32),axis=0,keepdims=True)
    def put(ref,rows,base,nb,g):
        for i in range(g.shape[0]//nb):
            k=base+i; rep=k%2; d=k//2; zz,yy,xx=d//4,(d//2)%2,d%2
            ref[rep,yy,xx,zz,rows:rows+nb,0:g.shape[1]]=g[i*nb:i*nb+nb].astype(BF)
    for n in range(4):
        put(GB,32,8*n,32,tn(d2[:,256*n:256*n+256],h1[...]))
    GB[:,:,:,:,32:64,1024:LN]=jnp.zeros((2,2,2,4,32,LN-1024),BF)
    for n in range(4):
        c=slice(256*n,256*n+256)
        g=(nn(d2[...],G[:,80:112,c].reshape(1024,256))*slope(a1[:,c])).astype(BF)
        d1[:,c]=g
        M[3:4,c]=jnp.sum(g.astype(F32),axis=0,keepdims=True)
    for n in range(4):
        put(GB,0,8*n,32,tn(d1[:,256*n:256*n+256],xl[3]))
    for lo,n in CH:
        dx[:,lo:lo+n]=nn(d1[...],G[:,48:80,lo:lo+n].reshape(1024,n))
    for l in (2,1,0):
        for lo,n in CH:
            g=dx[:,lo:lo+n]; dq=g*x0[:,lo:lo+n]
            M[l:l+1,lo:lo+n]=jnp.sum(dq,axis=0,keepdims=True)
            dql[:,lo:lo+n]=dq.astype(BF)
            e=g*qc[l,:,lo:lo+n]
            d0[:,lo:lo+n]=e if l==2 else d0[:,lo:lo+n]+e
        dpr[...]=nt(dql[...],UT[l]).astype(BF)
        for lo,n in CH:
            gu=tn(pr[l],dql[:,lo:lo+n]).reshape(32,8,n)
            gv=tn(dpr[...],xl[l,:,lo:lo+n]).reshape(32,8,n)
            gg=jnp.concatenate([gv,gu],axis=1).astype(BF)
            for k in range(32):
                rep=k%2; d=k//2; zz,yy,xx=d//4,(d//2)%2,d%2
                GA[rep,xx,yy,zz,16*l:16*l+16,lo:lo+n]=gg[k]
            v=dx[:,lo:lo+n]+nn(dpr[...],VT[l,:,lo:lo+n])
            if l: dx[:,lo:lo+n]=v
            else: d0[:,lo:lo+n]=d0[:,lo:lo+n]+v
    for i in range(9):
        xT[128*i:128*i+128,:]=d0[:,128*i:128*i+128].T
    for t in range(26):
        DE[t]=jnp.concatenate([xT[39*t:39*t+39,:],jnp.zeros((1,384),F32)],axis=0)
    DE[26]=jnp.zeros((40,384),F32)

def k2(total,ts,G,E,dns,lab,bia):
    vm=pl.BlockSpec(memory_space=pltpu.VMEM)
    V=pltpu.VMEM
    return pl.pallas_call(functools.partial(k2_body,total),name="k_two",
        out_shape=(jax.ShapeDtypeStruct((2,2,2,4,48,LN),BF),jax.ShapeDtypeStruct((2,2,2,4,64,LN),BF),jax.ShapeDtypeStruct((27,40,384),F32),jax.ShapeDtypeStruct((8,LN),F32)),
        in_specs=[pl.BlockSpec(memory_space=pltpu.SMEM)]+[vm]*5,out_specs=(vm,)*4,
        scratch_shapes=[V((LN,384),F32),V((384,LN),F32),V((384,LN),F32),V((4,384,LN),BF),V((3,384,LN),F32),V((3,384,256),BF),
          V((3,256,LN),BF),V((3,256,LN),BF),V((384,1024),F32),V((384,1024),F32),V((384,1024),BF),V((384,1024),BF),V((384,1024),BF),V((384,1024),BF),
          V((384,LN),F32),V((384,LN),F32),V((384,LN),BF),V((384,256),BF)],
        compiler_params=pltpu.CompilerParams(vmem_limit_bytes=60<<20))(ts,G,E,dns,lab,bia)
B1=0.5; C5=1-0.5**5; EPS=1e-10
def adamw(w,m,v,g,rate):
    mn=0.5*m+0.5*g
    vn=0.5*v+0.5*g*g
    return w-rate*((mn/C5)/(jnp.sqrt(vn/C5)+EPS)+0.01*w),mn,vn

def k3_body(inv, rc, ids_ref, GA, GB, DE, M, tw, tm_, tv, crw,crm,crv, tiw,tim,tiv, tmw,tmm,tmv,
        ow,om,ov,ol, cow,com,cov,col, iow,iom,iov,iol, mow,mom,mov,mol, MO,
        eout, D, R, gt, gtc, CA, CB, SA, SB, KA, KB, RA, RB_, SA2, SB2, RA2, RB2, KA2,KB2, SA3,SB3, RA3,RB3, MC, MS, MX, MZ,
        ss, rs, ess, ers):
    me=lax.axis_index("dp"); r=lax.axis_index("rep")
    x=me%2; y=(me//2)%2; z=me//4
    dev=lambda zz,yy,xx: zz*4+yy*2+xx
    zp=[z+1-2*(z%2),(z+2)%4,3-z]
    bar=pltpu.get_barrier_semaphore()
    for i in range(1,16):
        pl.semaphore_signal(bar,inc=1,device_id=((me+i)%16,r),device_id_type=MESH)
    pl.semaphore_signal(bar,inc=1,device_id=(me,1-r),device_id_type=MESH)
    pl.semaphore_wait(bar,16)
    xpeer=(dev(z,y,1-x),r); ypeer=(dev(z,1-y,x),r); core=(me,1-r)
    sends=[]
    def cp(src,dst,i,dev_):
        return pltpu.make_async_remote_copy(src_ref=src,dst_ref=dst,send_sem=ss.at[i],recv_sem=rs.at[i],device_id=dev_,device_id_type=MESH)
    def go(src,dst,i,dev_):
        c=cp(src,dst,i,dev_); c.start(); sends.append(c); return c
    cB=go(GB.at[1-r],CB,0,core)
    cA=go(GA.at[1-r],CA,1,core)
    cM=go(M,MC,2,core)
    def blk(d):
        return jnp.concatenate([DE[inv[2*d]],DE[inv[2*d+1]]],axis=0).astype(BF)
    def ec(d,land):
        return pltpu.make_async_remote_copy(src_ref=eout.at[d],dst_ref=D.at[land],send_sem=ess.at[d],recv_sem=ers.at[land],device_id=(d,r),device_id_type=MESH)
    def estep(i,_):
        d=(me+i)%16
        eout[d]=blk(d)
        ec(d,me).start()
        return 0
    lax.fori_loop(1,16,estep,0)
    D[me]=blk(me)
    cB.wait_recv()
    SB[...]=(GB[r,1-y].astype(F32)+CB[1-y].astype(F32)).astype(BF)
    b1=go(SB,RB_,3,ypeer)
    cA.wait_recv()
    SA[...]=(GA[r,1-x].astype(F32)+CA[1-x].astype(F32)).astype(BF)
    a1=go(SA,RA,4,xpeer)
    cM.wait_recv()
    MS[...]=M[...]+MC[...]
    m1=go(MS,MX.at[0],5,xpeer)
    KB[...]=GB[r,y].astype(F32)+CB[y].astype(F32)
    KA[...]=GA[r,x].astype(F32)+CA[x].astype(F32)
    m1.wait_recv()
    MZ[0]=MS[...]+MX[0]
    m2=go(MZ.at[0],MX.at[1],6,ypeer)
    m2.wait_recv()
    MX[2]=MZ[0]+MX[1]
    ms=[]
    for i,q in enumerate(zp):
        ms.append(go(MX.at[2],MX.at[3+i],7+i,(dev(q,y,x),r)))
    def onehot_parts(i,s):
        d=(me+i)%16
        ids=ids_ref[:,pl.ds(pl.multiple_of((d*2+r)*384,128),384)][s:s+1]
        lo=ids%512; hi=ids//512
        oh=(lax.broadcasted_iota(jnp.int32,(512,384),0)==lo).astype(F32).astype(BF)
        e=D[d].astype(F32)[40*s:40*s+40]
        lhs=jnp.concatenate([jnp.where(hi==g,e,0.0) for g in range(8)],axis=0).astype(BF)
        return lhs,oh
    R[...]=jnp.zeros_like(R)
    def acc(i2,_):
        for j in range(2):
            i=2*i2+j
            d=(me+i)%16
            @pl.when(i>0)
            def _(): ec(d,d).wait_recv()
        for s in range(2):
            p0=onehot_parts(2*i2,s); p1=onehot_parts(2*i2+1,s)
            R[s]+=nt(jnp.concatenate([p0[0],p1[0]],axis=1),jnp.concatenate([p0[1],p1[1]],axis=1))
        return 0
    lax.fori_loop(0,8,acc,0)
    for s in range(2):
        for j in range(32):
            g,h=j//4,j%4
            gt[pl.ds(2*j+s,39,stride=64),:]=R[s,g*40:g*40+39,h*128:(h+1)*128]
    cG=go(gt,gtc,10,core)
    b1.wait_recv()
    SB2[...]=(KB[1-x]+RB_[1-x].astype(F32)).astype(BF)
    b2=go(SB2,RB2,11,xpeer)
    KB2[...]=KB[x]+RB_[x].astype(F32)
    a1.wait_recv()
    SA2[...]=(KA[1-y]+RA[1-y].astype(F32)).astype(BF)
    a2=go(SA2,RA2,12,ypeer)
    KA2[...]=KA[y]+RA[y].astype(F32)
    cG.wait_recv()
    rowsel=lax.broadcasted_iota(jnp.int32,(64,128),0)
    lane=lax.broadcasted_iota(jnp.int32,(64,128),1)
    use=((rowsel//2)*128+lane)<jnp.where(rowsel%2==0,rc[0],rc[1])
    def tab(c,_):
        q=pl.ds(pl.multiple_of(c*64,64),64)
        w=tw[q,:]; m=tm_[q,:]; v=tv[q,:]; g=gt[q,:]+gtc[q,:]
        nw,nm,nv=adamw(w,m,v,g,0.2)
        nw=jnp.where(use,nw,w)
        ow[q,:]=nw; om[q,:]=jnp.where(use,nm,m); ov[q,:]=jnp.where(use,nv,v); ol[q,:]=nw.astype(BF)
        return 0
    lax.fori_loop(0,39,tab,0)
    b2.wait_recv()
    SB3[...]=(KB2[...]+RB2[...].astype(F32)).astype(BF)
    bz=[go(SB3.at[q],RB3.at[i],13+i,(dev(q,y,x),r)) for i,q in enumerate(zp)]
    a2.wait_recv()
    SA3[...]=(KA2[...]+RA2[...].astype(F32)).astype(BF)
    az=[go(SA3.at[q],RA3.at[i],16+i,(dev(q,y,x),r)) for i,q in enumerate(zp)]
    for c in ms: c.wait_recv()
    pos=[MX[2],MX[3],MX[4],MX[5]]
    zb=z%2; zh=z//2
    e0=jnp.where(zb==0,pos[0],pos[1]); e1=jnp.where(zb==0,pos[1],pos[0])
    f0=jnp.where(zb==0,pos[2],pos[3]); f1=jnp.where(zb==0,pos[3],pos[2])
    lo_=e0+e1; hi_=f0+f1
    MO[...]=jnp.where(zh==0,lo_,hi_)+jnp.where(zh==0,hi_,lo_)
    for c in bz: c.wait_recv()
    gB=KB2[z]+RB2[z].astype(F32)+(RB3[0].astype(F32)+RB3[1].astype(F32)+RB3[2].astype(F32))
    g=gB[0:32,0:1027]
    w,m,v=adamw(tiw[...],tim[...],tiv[...],g,0.01)
    iow[...]=w; iom[...]=m; iov[...]=v; iol[...]=w.astype(BF)
    g=gB[32:64,0:1024]
    w,m,v=adamw(tmw[...],tmm[...],tmv[...],g,0.01)
    mow[...]=w; mom[...]=m; mov[...]=v; mol[...]=w.astype(BF)
    for c in az: c.wait_recv()
    g=(KA2[z]+RA2[z].astype(F32)+(RA3[0].astype(F32)+RA3[1].astype(F32)+RA3[2].astype(F32)))[:,0:1027]
    w,m,v=adamw(crw[...],crm[...],crv[...],g,0.01)
    cow[...]=w; com[...]=m; cov[...]=v; col[...]=w.astype(BF)
    def ew(i,_):
        d=(me+i)%16
        ec(d,d).wait_send()
        return 0
    lax.fori_loop(1,16,ew,0)
    for c in sends: c.wait_send()

def k3(inv,rc,ids,GA,GB,DE,M,tabs,crs,tis,tms):
    vm=pl.BlockSpec(memory_space=pltpu.VMEM); sm=pl.BlockSpec(memory_space=pltpu.SMEM)
    V=pltpu.VMEM; S=jax.ShapeDtypeStruct
    quad=lambda a:[S(a.shape,F32)]*3+[S(a.shape,BF)]
    outs=quad(tabs[0])+quad(crs[0])+quad(tis[0])+quad(tms[0])+[S((8,LN),F32)]
    return pl.pallas_call(k3_body,name="k_three",out_shape=tuple(outs),
        in_specs=[sm,sm]+[vm]*17,out_specs=(vm,)*len(outs),
        scratch_shapes=[V((16,80,384),BF),V((16,80,384),BF),V((2,320,512),F32),V((2496,128),F32),V((2496,128),F32),
          V((2,2,4,48,LN),BF),V((2,2,4,64,LN),BF), V((2,4,48,LN),BF),V((2,4,64,LN),BF), V((2,4,48,LN),F32),V((2,4,64,LN),F32),
          V((2,4,48,LN),BF),V((2,4,64,LN),BF), V((4,48,LN),BF),V((4,64,LN),BF),V((4,48,LN),BF),V((4,64,LN),BF),
          V((4,48,LN),F32),V((4,64,LN),F32), V((4,48,LN),BF),V((4,64,LN),BF),V((3,48,LN),BF),V((3,64,LN),BF),
          V((8,LN),F32),V((8,LN),F32),V((6,8,LN),F32),V((1,8,LN),F32),
          pltpu.SemaphoreType.DMA((20,)),pltpu.SemaphoreType.DMA((20,)),pltpu.SemaphoreType.DMA((16,)),pltpu.SemaphoreType.DMA((16,))],
        compiler_params=pltpu.CompilerParams(collective_id=1,has_side_effects=True,vmem_limit_bytes=60<<20))(
        inv,rc,ids,GA,GB,DE,M,*tabs,*crs,*tis,*tms)

def fast_shards(
    event_ids, row_counts, table_slot, dense_input, labels,
    tables, tables_m, tables_v, cross_uv, cross_m, cross_v,
    tower_in, tower_in_m, tower_in_v, tower_mid, tower_mid_m, tower_mid_v,
    head_weight, head_m, head_v, biases, biases_m, biases_v,
):
    total = float(labels.shape[0] * lax.axis_size("dp") * lax.axis_size("rep"))
    turn = lambda a: jnp.transpose(a, (0, 1, 3, 2)).reshape(48, WIDTH)
    back = lambda a: jnp.transpose(a.reshape(LAYERS, 2, 8, WIDTH), (0, 1, 3, 2))
    tabs = [tab_view(a) for a in (tables, tables_m, tables_v)]
    crs = [turn(a) for a in (cross_uv, cross_m, cross_v)]
    tis = [a.T for a in (tower_in, tower_in_m, tower_in_v)]
    tms = [a.T for a in (tower_mid, tower_mid_m, tower_mid_v)]
    hits = (table_slot[None, :] == jnp.arange(32, dtype=jnp.int32)[:, None])
    inv = TABLES - jnp.sum(hits * (TABLES - jnp.arange(TABLES, dtype=jnp.int32))[None, :], axis=1)
    wide = lambda v: jnp.pad(v, (0, LN - v.shape[0]))
    at = LAYERS * WIDTH
    bia = jnp.stack(
        [wide(biases[WIDTH * i : WIDTH * i + WIDTH]) for i in range(3)]
        + [wide(biases[at : at + 1024]), wide(biases[at + 1024 : at + 2048]),
           jnp.broadcast_to(biases[at + 2048], (LN,)), jnp.zeros((LN,), F32), jnp.zeros((LN,), F32)]
    )
    G, E = k1(event_ids, tabs[0], crs[0], tis[0], tms[0], head_weight.reshape(1, 32))
    GA, GB, DE, M = k2(total, table_slot, G, E, dense_input.T, labels.reshape(1, 384), bia)
    o = k3(inv, row_counts, event_ids, GA, GB, DE, M, tabs, crs, tis, tms)
    MO = o[16]
    loss = MO[6, 0]
    g_bias = jnp.concatenate([MO[0, :WIDTH], MO[1, :WIDTH], MO[2, :WIDTH], MO[3, :1024], MO[4, :1024], MO[7, :1]])
    k = lax.axis_index("dp") * 2 + lax.axis_index("rep")
    g_head = lax.dynamic_slice(MO[5], (k * 32,), (32,))
    tail = []
    for w, m, v, g, rate in ((head_weight, head_m, head_v, g_head, RATE_DENSE), (biases, biases_m, biases_v, g_bias, RATE_BIAS)):
        a, b, c = adamw_update(w, m, v, g, rate)
        tail += [a, b, c, a.astype(BF)]
    return (
        loss,
        *[tab_unview(a) for a in o[0:4]],
        *[back(a) for a in o[4:8]],
        *[a.T for a in o[8:12]],
        *[a.T for a in o[12:16]],
        *tail,
    )


def solution(mesh):
    placed = (
        P("dp", None),
        P("dp"),
        P(),
        P(("dp", "rep"), None),
        P(("dp", "rep")),
        P("dp", None, None),
        P("dp", None, None),
        P("dp", None, None),
        P(None, None, None, ("dp", "rep")),
        P(None, None, None, ("dp", "rep")),
        P(None, None, None, ("dp", "rep")),
        P(None, ("dp", "rep")),
        P(None, ("dp", "rep")),
        P(None, ("dp", "rep")),
        P(None, ("dp", "rep")),
        P(None, ("dp", "rep")),
        P(None, ("dp", "rep")),
        P(("dp", "rep")),
        P(("dp", "rep")),
        P(("dp", "rep")),
        P(),
        P(),
        P(),
    )
    fits = mesh.shape["dp"] == 16 and mesh.shape["rep"] == 2
    return jax.shard_map(
        fast_shards if fits else shards,
        mesh=mesh,
        in_specs=placed,
        out_specs=(
            P(),
            P("dp", None, None),
            P("dp", None, None),
            P("dp", None, None),
            P("dp", None, None),
            P(None, None, None, ("dp", "rep")),
            P(None, None, None, ("dp", "rep")),
            P(None, None, None, ("dp", "rep")),
            P(None, None, None, ("dp", "rep")),
            P(None, ("dp", "rep")),
            P(None, ("dp", "rep")),
            P(None, ("dp", "rep")),
            P(None, ("dp", "rep")),
            P(None, ("dp", "rep")),
            P(None, ("dp", "rep")),
            P(None, ("dp", "rep")),
            P(None, ("dp", "rep")),
            P(("dp", "rep")),
            P(("dp", "rep")),
            P(("dp", "rep")),
            P(("dp", "rep")),
            P(),
            P(),
            P(),
            P(),
        ),
        check_vma=False,
    )
```

```python
import functools
import math

import jax
import jax.numpy as jnp
from jax import lax
from jax.experimental import pallas as pl
from jax.experimental.pallas import tpu as pltpu
from jax.sharding import PartitionSpec as P

TABLES = 26
EMB = 39
HIDDEN_SIZE = 1024
LAYERS = 3
MICRO = 3
STEP = 5
WIDTH = 1027


BETA_ONE = 0.5
BETA_TWO = 0.5
EPSILON = 1e-10
WEIGHT_DECAY = 0.01
RATE_DENSE = 0.01
RATE_BIAS = 0.05
RATE_TABLE = 0.2
HIGHEST_PRECISION = lax.Precision.HIGHEST


def adamw_update(weight, moment_one, moment_two, gradient, step_rate):
    moment_new = BETA_ONE * moment_one + (1 - BETA_ONE) * gradient
    second = BETA_TWO * moment_two + (1 - BETA_TWO) * gradient * gradient
    scaled_one = moment_new / (1 - BETA_ONE**STEP)
    scaled_two = second / (1 - BETA_TWO**STEP)
    fresh = weight - step_rate * (
        scaled_one / (jnp.sqrt(scaled_two) + EPSILON) + WEIGHT_DECAY * weight
    )
    return (fresh, moment_new, second)


def silu_slope(pre_value):
    sigmoid_value = jax.nn.sigmoid(pre_value)
    return sigmoid_value * (1.0 + pre_value * (1.0 - sigmoid_value))


def contract_rows(left_side, right_side):
    return lax.dot_general(
        left_side, right_side, (((0,), (0,)), ((), ())), preferred_element_type=jnp.float32
    )


def contract_cols(left_side, right_side):
    return lax.dot_general(
        left_side, right_side, (((1,), (1,)), ((), ())), preferred_element_type=jnp.float32
    )


def one_hot_rows(positions, row_total):
    return (positions[:, None] == jnp.arange(row_total, dtype=jnp.int32)[None, :]).astype(
        jnp.bfloat16
    )


def lookup_rows(table_piece, positions):
    count = positions.shape[0]
    block = math.gcd(count, 512)
    blocks = positions.reshape(count // block, block)

    def one_block(block_ids):
        return jnp.dot(
            one_hot_rows(block_ids, table_piece.shape[0]),
            table_piece,
            preferred_element_type=jnp.float32,
        ).astype(jnp.bfloat16)

    return lax.map(one_block, blocks).reshape(count, table_piece.shape[1])


def accumulate_rows(entry_rows, positions, row_total):
    count = positions.shape[0]
    block = math.gcd(count, 512)
    blocks = positions.reshape(count // block, block)
    entry_blocks = entry_rows.reshape(count // block, block, entry_rows.shape[1])

    def add_block(running, pair):
        block_ids, block_rows = pair
        return (running + contract_rows(one_hot_rows(block_ids, row_total), block_rows), None)

    start = jnp.zeros((row_total, entry_rows.shape[1]), jnp.float32)
    summed, unused = lax.scan(add_block, start, (blocks, entry_blocks))
    return summed


def cross_forward(anchor, carried, cross_full, layer_bias, which_layer):
    carried_low = carried.astype(jnp.bfloat16)
    project = jnp.dot(
        carried_low, cross_full[which_layer, 0], preferred_element_type=jnp.float32
    ).astype(jnp.bfloat16)
    crossed = contract_cols(project, cross_full[which_layer, 1])
    return (anchor * (crossed + layer_bias[which_layer]) + carried, (carried_low, project, crossed))


def cross_backward(anchor, grad_carried, saved_values, cross_full, layer_bias, which_layer):
    carried_low, project, crossed = saved_values
    grad_cross = grad_carried * anchor
    bias_grad = jnp.sum(grad_cross, axis=0)
    grad_cross_low = grad_cross.astype(jnp.bfloat16)
    grad_up = contract_rows(grad_cross_low, project)
    grad_project = jnp.dot(
        grad_cross_low, cross_full[which_layer, 1], preferred_element_type=jnp.float32
    ).astype(jnp.bfloat16)
    grad_down = contract_rows(carried_low, grad_project)
    grad_input = contract_cols(grad_project, cross_full[which_layer, 0]) + grad_carried
    extra_grad = grad_carried * (crossed + layer_bias[which_layer])
    return (grad_input, extra_grad, jnp.stack([grad_down, grad_up]), bias_grad)


def micro_step(gathered, biases, emb_flat, dense_rows, target, total_events):
    cross_full, tower_full, mid_full, head_full = gathered
    layer_bias = biases[: LAYERS * WIDTH].reshape(LAYERS, WIDTH)
    bias_one = biases[LAYERS * WIDTH : LAYERS * WIDTH + HIDDEN_SIZE]
    bias_two = biases[LAYERS * WIDTH + HIDDEN_SIZE : LAYERS * WIDTH + 2 * HIDDEN_SIZE]
    bias_out = biases[LAYERS * WIDTH + 2 * HIDDEN_SIZE]
    dense_low = lax.optimization_barrier(dense_rows.astype(jnp.bfloat16)).astype(jnp.float32)
    anchor = jnp.concatenate([emb_flat.astype(jnp.float32), dense_low], axis=1)
    carried = anchor
    saved_all = []
    for which_layer in range(LAYERS):
        carried, saved_values = cross_forward(anchor, carried, cross_full, layer_bias, which_layer)
        saved_all.append(saved_values)
    carried_low = carried.astype(jnp.bfloat16)
    pre_one = jnp.dot(carried_low, tower_full, preferred_element_type=jnp.float32) + bias_one
    hidden_one = jax.nn.silu(pre_one).astype(jnp.bfloat16)
    pre_two = jnp.dot(hidden_one, mid_full, preferred_element_type=jnp.float32) + bias_two
    hidden_two = jax.nn.silu(pre_two).astype(jnp.bfloat16)
    logits = jnp.dot(hidden_two, head_full, preferred_element_type=jnp.float32) + bias_out
    loss_part = jnp.sum(jax.nn.softplus(logits) - target * logits)
    grad_logits = (jax.nn.sigmoid(logits) - target) / total_events
    grad_head = jnp.dot(grad_logits, hidden_two.astype(jnp.float32), precision=HIGHEST_PRECISION)
    grad_hidden_two = grad_logits[:, None] * head_full.astype(jnp.float32)[None, :]
    grad_pre_two = (grad_hidden_two * silu_slope(pre_two)).astype(jnp.bfloat16)
    grad_mid = contract_rows(hidden_one, grad_pre_two)
    grad_hidden_one = contract_cols(grad_pre_two, mid_full)
    grad_pre_one = (grad_hidden_one * silu_slope(pre_one)).astype(jnp.bfloat16)
    grad_tower = contract_rows(carried_low, grad_pre_one)
    grad_carried = contract_cols(grad_pre_one, tower_full)
    grad_anchor = jnp.zeros_like(anchor)
    cross_grads = [None] * LAYERS
    layer_grads = [None] * LAYERS
    for which_layer in reversed(range(LAYERS)):
        grad_carried, extra_grad, grad_pair, bias_grad = cross_backward(
            anchor, grad_carried, saved_all[which_layer], cross_full, layer_bias, which_layer
        )
        grad_anchor = grad_anchor + extra_grad
        cross_grads[which_layer] = grad_pair
        layer_grads[which_layer] = bias_grad
    grad_anchor = grad_anchor + grad_carried
    grad_emb = grad_anchor[:, : TABLES * EMB].astype(jnp.bfloat16)
    bias_grads = jnp.concatenate(
        [
            jnp.stack(layer_grads).reshape(-1),
            jnp.sum(grad_pre_one.astype(jnp.float32), axis=0),
            jnp.sum(grad_pre_two.astype(jnp.float32), axis=0),
            jnp.sum(grad_logits)[None],
        ]
    )
    dense_grads = (jnp.stack(cross_grads), grad_tower, grad_mid, grad_head)
    return (loss_part, grad_emb, dense_grads, bias_grads)


def shards(
    event_ids,
    row_counts,
    table_slot,
    dense_input,
    labels,
    tables,
    tables_m,
    tables_v,
    cross_uv,
    cross_m,
    cross_v,
    tower_in,
    tower_in_m,
    tower_in_v,
    tower_mid,
    tower_mid_m,
    tower_mid_v,
    head_weight,
    head_m,
    head_v,
    biases,
    biases_m,
    biases_v,
):
    dp_count = lax.axis_size("dp")
    rep_count = lax.axis_size("rep")
    rep_index = lax.axis_index("rep")
    slot_count = tables.shape[0]
    row_total = tables.shape[1]
    device_events = labels.shape[0]
    micro_events = device_events // MICRO
    total_events = float(device_events * dp_count * rep_count)
    shard_set = (cross_uv, tower_in, tower_mid, head_weight)
    shard_low = tuple((shard_piece.astype(jnp.bfloat16) for shard_piece in shard_set))
    event_grid = event_ids.reshape(slot_count, dp_count, rep_count, MICRO, micro_events)
    own_ids = lax.dynamic_index_in_dim(event_grid, rep_index, 2, keepdims=False)
    table_low = tables.astype(jnp.bfloat16)
    selector = (
        table_slot[:, None] == jnp.arange(dp_count * slot_count, dtype=jnp.int32)[None, :]
    ).astype(jnp.bfloat16)
    loss_total = jnp.zeros((), jnp.float32)
    bias_total = jnp.zeros(biases.shape, jnp.float32)
    table_grad = jnp.zeros(tables.shape, jnp.float32)
    dense_total = None
    for micro_index in range(MICRO):
        gathered = (
            lax.all_gather(shard_low[0], ("dp", "rep"), axis=3, tiled=True),
            lax.all_gather(shard_low[1], ("dp", "rep"), axis=1, tiled=True),
            lax.all_gather(shard_low[2], ("dp", "rep"), axis=1, tiled=True),
            lax.all_gather(shard_low[3], ("dp", "rep"), axis=0, tiled=True),
        )
        micro_ids = own_ids[:, :, micro_index, :].reshape(slot_count, dp_count * micro_events)
        looked = jax.vmap(lookup_rows)(table_low, micro_ids)
        outgoing = jnp.transpose(
            looked.reshape(slot_count, dp_count, micro_events, EMB), (1, 0, 2, 3)
        )
        arrived = lax.all_to_all(outgoing, "dp", split_axis=0, concat_axis=0, tiled=True)
        by_slot = arrived.reshape(dp_count * slot_count, micro_events, EMB)
        picked = jnp.einsum(
            "ts,sec->tec", selector, by_slot, preferred_element_type=jnp.float32
        ).astype(jnp.bfloat16)
        emb_flat = jnp.transpose(picked, (1, 0, 2)).reshape(micro_events, TABLES * EMB)
        row_lo = micro_index * micro_events
        dense_rows = dense_input[row_lo : row_lo + micro_events]
        target = labels[row_lo : row_lo + micro_events].astype(jnp.float32)
        loss_part, grad_emb, dense_grads, bias_grads = micro_step(
            gathered, biases, emb_flat, dense_rows, target, total_events
        )
        loss_total = loss_total + loss_part
        bias_total = bias_total + bias_grads
        if micro_index == 0:
            dense_total = dense_grads
        else:
            dense_total = tuple(
                (running + fresh_part for running, fresh_part in zip(dense_total, dense_grads))
            )
        grad_tables = jnp.transpose(grad_emb.reshape(micro_events, TABLES, EMB), (1, 0, 2))
        slot_grads = jnp.einsum(
            "ts,tec->sec", selector, grad_tables, preferred_element_type=jnp.float32
        ).astype(jnp.bfloat16)
        returned = lax.all_to_all(
            slot_grads.reshape(dp_count, slot_count, micro_events, EMB),
            "dp",
            split_axis=0,
            concat_axis=0,
            tiled=True,
        )
        entries = jnp.transpose(returned, (1, 0, 2, 3)).reshape(
            slot_count, dp_count * micro_events, EMB
        )
        table_grad = table_grad + jax.vmap(
            lambda entry_rows, positions: accumulate_rows(entry_rows, positions, row_total)
        )(entries, micro_ids)
    dense_total = (
        lax.psum_scatter(dense_total[0], ("dp", "rep"), scatter_dimension=3, tiled=True),
        lax.psum_scatter(dense_total[1], ("dp", "rep"), scatter_dimension=1, tiled=True),
        lax.psum_scatter(dense_total[2], ("dp", "rep"), scatter_dimension=1, tiled=True),
        lax.psum_scatter(dense_total[3], ("dp", "rep"), scatter_dimension=0, tiled=True),
    )
    table_grad = lax.psum(table_grad, "rep")
    bias_total, loss_total = lax.psum((bias_total, loss_total), ("dp", "rep"))
    fresh_tab, fresh_tab_m, fresh_tab_v = adamw_update(
        tables, tables_m, tables_v, table_grad, RATE_TABLE
    )
    in_use = (jnp.arange(row_total, dtype=jnp.int32)[None, :] < row_counts[:, None])[:, :, None]
    fresh_tab = jnp.where(in_use, fresh_tab, tables)
    fresh_tab_m = jnp.where(in_use, fresh_tab_m, tables_m)
    fresh_tab_v = jnp.where(in_use, fresh_tab_v, tables_v)
    weight_set = shard_set + (biases,)
    grad_set = tuple(dense_total) + (bias_total,)
    states = (
        (cross_m, cross_v, RATE_DENSE),
        (tower_in_m, tower_in_v, RATE_DENSE),
        (tower_mid_m, tower_mid_v, RATE_DENSE),
        (head_m, head_v, RATE_DENSE),
        (biases_m, biases_v, RATE_BIAS),
    )
    results = []
    for weight, gradient, state in zip(weight_set, grad_set, states):
        fresh, moment_new, second = adamw_update(weight, state[0], state[1], gradient, state[2])
        results.append((fresh, moment_new, second, fresh.astype(jnp.bfloat16)))
    return (
        loss_total,
        fresh_tab,
        fresh_tab_m,
        fresh_tab_v,
        fresh_tab.astype(jnp.bfloat16),
        results[0][0],
        results[0][1],
        results[0][2],
        results[0][3],
        results[1][0],
        results[1][1],
        results[1][2],
        results[1][3],
        results[2][0],
        results[2][1],
        results[2][2],
        results[2][3],
        results[3][0],
        results[3][1],
        results[3][2],
        results[3][3],
        results[4][0],
        results[4][1],
        results[4][2],
        results[4][3],
    )


MESH = pl.DeviceIdType.MESH
F32 = jnp.float32
BF = jnp.bfloat16
LN = 1152
RB = 112
CH = [(0, 256), (256, 256), (512, 256), (768, 256), (1024, 128)]
ITEMS = {"m": (32, 1024, True), "i": (32, LN, False), "c2": (16, LN, True), "c1": (16, LN, False), "c0": (16, LN, True)}
ORDER = ["m", "i", "c2", "c1", "c0"]


def nt(a, b):
    return lax.dot_general(a, b, (((1,), (1,)), ((), ())), preferred_element_type=F32)


def nn(a, b):
    return lax.dot_general(a, b, (((1,), (0,)), ((), ())), preferred_element_type=F32)


def tn(a, b):
    return lax.dot_general(a, b, (((0,), (0,)), ((), ())), preferred_element_type=F32)


def sig(v):
    return 1.0 / (1.0 + jnp.exp(-v))


def slope(v):
    s = sig(v)
    return s * (1.0 + v * (1.0 - s))


def place(k):
    rep, d = k % 2, k // 2
    return rep, d % 2, (d // 2) % 2, d // 4


def mega_body(total, names_in, names_out, names_scr, *refs):
    it = iter(refs)
    R_ = {n: next(it) for n in names_in + names_out + names_scr}
    ts, inv = R_["ts"], R_["inv"]
    G, E, D, eout, tabr = R_["G"], R_["E"], R_["D"], R_["eout"], R_["tabr"]
    xT, dx, xl, qc, pr = R_["xT"], R_["dx"], R_["xl"], R_["qc"], R_["pr"]
    VT, UT, a1, a2, h1, h2 = R_["VT"], R_["UT"], R_["a1"], R_["a2"], R_["h1"], R_["h2"]
    d0, dql, dpr, DE, M, R = R_["d0"], R_["dql"], R_["dpr"], R_["DE"], R_["M"], R_["R"]
    ids_ref, tab_ref, bia = R_["ids_v"], R_["tab_v"], R_["bia"]
    xr, d1, d2 = dx, h1, h2
    gt, gtc, MO = R_["gt"], R_["gtc"], R_["MO"]
    me = lax.axis_index("dp")
    r = lax.axis_index("rep")
    x, y, z = me % 2, (me // 2) % 2, me // 4
    dev = lambda zz, yy, xx: zz * 4 + yy * 2 + xx
    zp = [z + 1 - 2 * (z % 2), (z + 2) % 4, 3 - z]
    own = me * 2 + r
    xpeer, ypeer, core = (dev(z, y, 1 - x), r), (dev(z, 1 - y, x), r), (me, 1 - r)
    zpeer = [(dev(q, y, x), r) for q in zp]

    loads = {}
    for i, n in enumerate(["cr", "ti", "tm", "hd", "tab", "ids", "dns", "lab"]):
        c = pltpu.make_async_copy(R_[n], R_[n + "_v"], R_["lsem"].at[i])
        c.start()
        loads[n] = c
    bar = pltpu.get_barrier_semaphore()
    for i in range(1, 16):
        pl.semaphore_signal(bar, inc=1, device_id=((me + i) % 16, r), device_id_type=MESH)
    pl.semaphore_signal(bar, inc=1, device_id=core, device_id_type=MESH)

    cr, ti, tm, hd = R_["cr_v"], R_["ti_v"], R_["tm_v"], R_["hd_v"]
    for n in ("cr", "ti", "tm", "hd"):
        loads[n].wait()
    G[own, 0:48, 0:1024] = cr[:, 0:1024].astype(BF)
    G[own, 0:48, 1024:LN] = jnp.concatenate([cr[:, 1024:1027], jnp.zeros((48, 125), F32)], axis=1).astype(BF)
    G[own, 48:80, 0:1024] = ti[:, 0:1024].astype(BF)
    G[own, 48:80, 1024:LN] = jnp.concatenate([ti[:, 1024:1027], jnp.zeros((32, 125), F32)], axis=1).astype(BF)
    G[own, 80:112, 0:1024] = tm[...].astype(BF)
    eye = lax.broadcasted_iota(jnp.int32, (32, 32), 0) == lax.broadcasted_iota(jnp.int32, (32, 32), 1)
    hcol = jnp.sum(jnp.where(eye, jnp.broadcast_to(hd[...], (32, 32)), 0.0), axis=1, keepdims=True)
    G[own, 80:112, 1024:LN] = jnp.broadcast_to(hcol, (32, 128)).astype(BF)
    pl.semaphore_wait(bar, 16)

    parts = ((0, 48), (48, 64))
    cnt = [0, 0]
    sends = []

    def wcopy(p, k, dst, si):
        lo, n = parts[p]
        return pltpu.make_async_remote_copy(
            src_ref=G.at[k, pl.ds(lo, n)], dst_ref=G.at[k, pl.ds(lo, n)],
            send_sem=R_["wss"].at[p, si], recv_sem=R_["wrs"].at[p, k], device_id=dst, device_id_type=MESH)

    def wsend(p, k, dst):
        c = wcopy(p, k, dst, cnt[p])
        cnt[p] += 1
        c.start()
        sends.append(c)

    def wwait(p, k):
        wcopy(p, k, core, 0).wait_recv()

    p1, p2 = (ypeer, xpeer), (xpeer, ypeer)
    key = lambda zz, yy, xx: dev(zz, yy, xx) * 2 + r
    for p in (0, 1):
        wsend(p, own, p1[p])
        wsend(p, own, p2[p])
    for q in zpeer:
        for p in (0, 1):
            wsend(p, own, q)
    for p in (0, 1):
        wsend(p, own, core)

    def fwd_z(p, i):
        k = key(zp[i], y, x)
        wwait(p, k)
        wsend(p, k, p1[p])
        wsend(p, k, p2[p])
        wsend(p, k, core)

    def fwd_1(p, i):
        q = z if i < 0 else zp[i]
        k = key(q, 1 - y, x) if p == 0 else key(q, y, 1 - x)
        wwait(p, k)
        wsend(p, k, p2[p])
        wsend(p, k, core)

    def fwd_2(p, i, o):
        q = z if i < 0 else zp[i]
        k = key(q, (y + o) % 2, 1 - x) if p == 0 else key(q, 1 - y, (x + o) % 2)
        wwait(p, k)
        wsend(p, k, core)

    def core_wait(p):
        def cw(i, _):
            wwait(p, i * 2 + (1 - r))
            return 0
        lax.fori_loop(0, 16, cw, 0)

    loads["tab"].wait()
    loads["ids"].wait()
    for s in range(2):
        for j in range(32):
            g, h = j // 4, j % 4
            t = tab_ref[pl.ds(2 * j + s, 39, stride=64), :]
            tabr[s, g * 40 : (g + 1) * 40, h * 128 : (h + 1) * 128] = jnp.concatenate([t, jnp.zeros((1, 128), F32)], axis=0).astype(BF)

    def id_rows(d):
        return ids_ref[:, pl.ds(pl.multiple_of((d * 2 + r) * 384, 128), 384)]

    def one_hot(lo):
        return (lax.broadcasted_iota(jnp.int32, (512, 384), 0) == lo).astype(F32).astype(BF)

    def look(d):
        idv = id_rows(d)
        outs = []
        for s in range(2):
            ids = idv[s : s + 1]
            lo, hi = ids % 512, ids // 512
            res = nn(tabr[s], one_hot(lo))
            e = jnp.zeros((40, 384), F32)
            for g in range(8):
                e = e + jnp.where(hi == g, res[g * 40 : (g + 1) * 40], 0.0)
            outs.append(e)
        return jnp.concatenate(outs, axis=0).astype(BF)

    def ecopy(d, land):
        return pltpu.make_async_remote_copy(
            src_ref=eout.at[d], dst_ref=E.at[land], send_sem=R_["ess"].at[d], recv_sem=R_["ers"].at[land], device_id=(d, r), device_id_type=MESH)

    def dcopy(d, land):
        return pltpu.make_async_remote_copy(
            src_ref=eout.at[d], dst_ref=D.at[land], send_sem=R_["dss"].at[d], recv_sem=R_["drs"].at[land], device_id=(d, r), device_id_type=MESH)

    def looks(a, b):
        def step(i, _):
            d = (me + i) % 16
            eout[d] = look(d)
            ecopy(d, me).start()
            return 0
        lax.fori_loop(a, b, step, 0)

    looks(1, 8)
    fwd_1(0, -1)
    fwd_1(1, -1)
    looks(8, 12)
    fwd_z(0, 0)
    fwd_z(1, 0)
    looks(12, 16)
    E[me] = look(me)
    for i in (1, 2):
        for p in (0, 1):
            fwd_z(p, i)
    for i in (0, 1, 2):
        for p in (0, 1):
            fwd_1(p, i)
    for i in (-1, 0, 1, 2):
        for o in (0, 1):
            fwd_2(0, i, o)

    def ew(i, _):
        d = (me + i) % 16
        ecopy(d, d).wait()
        return 0

    lax.fori_loop(1, 16, ew, 0)
    loads["dns"].wait()
    loads["lab"].wait()
    for t in range(26):
        s = ts[t]
        blk = E[s // 2].astype(F32)
        e = jnp.where(s % 2 == 1, blk[40:80], blk[0:40])
        xT[39 * t : 39 * t + 39, :] = e[0:39]
    xT[1014:1027, :] = R_["dns_v"][...].astype(BF).astype(F32)
    xT[1027:LN, :] = jnp.zeros((LN - 1027, 384), F32)
    for i in range(9):
        c = slice(128 * i, 128 * i + 128)
        xl[0, :, c] = xT[c, :].T.astype(BF)
    x0 = lambda lo, n: xl[0, :, lo : lo + n].astype(F32)
    core_wait(0)
    for l in range(3):
        for lo, n in CH:
            w = G[:, 16 * l : 16 * l + 16, lo : lo + n].astype(F32).reshape(32, 2, 8, n)
            VT[l, :, lo : lo + n] = w[:, 0].reshape(256, n).astype(BF)
            UT[l, :, lo : lo + n] = w[:, 1].reshape(256, n).astype(BF)
    for l in range(3):
        pr[l] = nt(xl[l], VT[l]).astype(BF)
        for lo, n in CH:
            q = nn(pr[l], UT[l, :, lo : lo + n]) + bia[l : l + 1, lo : lo + n]
            qc[l, :, lo : lo + n] = q
            v = x0(lo, n) * q + (x0(lo, n) if l == 0 else xr[:, lo : lo + n])
            if l < 2:
                xr[:, lo : lo + n] = v
            xl[l + 1, :, lo : lo + n] = v.astype(BF)
    for i in (-1, 0, 1, 2):
        for o in (0, 1):
            fwd_2(1, i, o)
    core_wait(1)
    for n in range(4):
        c = slice(256 * n, 256 * n + 256)
        a = nt(xl[3], G[8 * n : 8 * n + 8, 48:80, :].reshape(256, LN)) + bia[3:4, c]
        a1[:, c] = a
        h1[:, c] = (a * sig(a)).astype(BF)
    for n in range(4):
        c = slice(256 * n, 256 * n + 256)
        a = nt(h1[...], G[8 * n : 8 * n + 8, 80:112, 0:1024].reshape(256, 1024)) + bia[4:5, c]
        a2[:, c] = a
        h2[:, c] = (a * sig(a)).astype(BF)
    hc = G[:, 80:112, 1024:LN].reshape(1024, 128)
    zl = nn(h2[...], hc) + bia[5:6, 0:128]
    yl = jnp.broadcast_to(R_["lab_v"][...].astype(F32), (128, 384)).T
    lossv = jnp.maximum(zl, 0.0) + jnp.log1p(jnp.exp(-jnp.abs(zl))) - yl * zl
    dz = (sig(zl) - yl) / total
    M[...] = jnp.zeros_like(M)
    M[6:7, 0:128] = jnp.sum(lossv, axis=0, keepdims=True)
    M[7:8, 0:128] = jnp.sum(dz, axis=0, keepdims=True)
    hrow = hc.astype(F32).T[0:1]
    for n in range(8):
        c = slice(128 * n, 128 * n + 128)
        M[5:6, c] = jnp.sum(dz * h2[:, c].astype(F32), axis=0, keepdims=True)
        g = (dz * hrow[:, c] * slope(a2[:, c])).astype(BF)
        d2[:, c] = g
        M[4:5, c] = jnp.sum(g.astype(F32), axis=0, keepdims=True)

    nsem = [0]

    def go(src, dst, dst_dev):
        i = nsem[0]
        nsem[0] += 1
        c = pltpu.make_async_remote_copy(
            src_ref=src, dst_ref=dst, send_sem=R_["rss"].at[i], recv_sem=R_["rrs"].at[i], device_id=dst_dev, device_id_type=MESH)
        c.start()
        sends.append(c)
        return c

    st = {}

    def axes(n):
        return (y, x, ypeer, xpeer) if ITEMS[n][2] else (x, y, xpeer, ypeer)

    def s0(n):
        g = R_["g_" + n]
        st[n] = go(g.at[1 - r], R_["C_" + n], core)

    def s1(n):
        a, b, pa, pb = axes(n)
        st[n].wait_recv()
        g, c = R_["g_" + n], R_["C_" + n]
        g[r, 1 - a] = (g[r, 1 - a].astype(F32) + c[1 - a].astype(F32)).astype(BF)
        st[n] = go(g.at[r, 1 - a], R_["P_" + n], pa)

    def s2(n):
        a, b, pa, pb = axes(n)
        st[n].wait_recv()
        g, c, p = R_["g_" + n], R_["C_" + n], R_["P_" + n]
        g[r, a, 1 - b] = (g[r, a, 1 - b].astype(F32) + c[a, 1 - b].astype(F32) + p[1 - b].astype(F32)).astype(BF)
        st[n] = go(g.at[r, a, 1 - b], R_["Q_" + n], pb)

    def s3(n):
        a, b, pa, pb = axes(n)
        st[n].wait_recv()
        g, c, p, q = R_["g_" + n], R_["C_" + n], R_["P_" + n], R_["Q_" + n]
        st[n] = []
        for i, zz in enumerate(zp):
            g[r, a, b, zz] = (g[r, a, b, zz].astype(F32) + c[a, b, zz].astype(F32) + p[b, zz].astype(F32) + q[zz].astype(F32)).astype(BF)
            st[n].append(go(g.at[r, a, b, zz], R_["T_" + n].at[i], zpeer[i]))

    def s4(n):
        a, b, pa, pb = axes(n)
        for c in st[n]:
            c.wait_recv()
        g, c, p, q, t = R_["g_" + n], R_["C_" + n], R_["P_" + n], R_["Q_" + n], R_["T_" + n]
        R_["o_" + n][...] = (
            g[r, a, b, z].astype(F32) + c[a, b, z].astype(F32) + p[b, z].astype(F32) + q[z].astype(F32)
            + (t[0].astype(F32) + t[1].astype(F32) + t[2].astype(F32)))

    def put(n, base, g):
        nb, _, yfirst = ITEMS[n]
        for i in range(g.shape[0] // nb):
            rep, xx, yy, zz = place(base + i)
            a, b = (yy, xx) if yfirst else (xx, yy)
            R_["g_" + n][rep, a, b, zz] = g[i * nb : i * nb + nb].astype(BF)

    for n in range(4):
        put("m", 8 * n, tn(d2[:, 256 * n : 256 * n + 256], h1[...]))
    s0("m")
    for n in range(4):
        c = slice(256 * n, 256 * n + 256)
        a1[:, c] = nn(d2[...], G[:, 80:112, c].reshape(1024, 256)) * slope(a1[:, c])
    for n in range(4):
        c = slice(256 * n, 256 * n + 256)
        g = a1[:, c].astype(BF)
        d1[:, c] = g
        M[3:4, c] = jnp.sum(g.astype(F32), axis=0, keepdims=True)
    s1("m")
    for n in range(4):
        put("i", 8 * n, tn(d1[:, 256 * n : 256 * n + 256], xl[3]))
    s0("i")
    for lo, n in CH:
        dx[:, lo : lo + n] = nn(d1[...], G[:, 48:80, lo : lo + n].reshape(1024, n))

    def cross_back(l):
        for lo, n in CH:
            g = dx[:, lo : lo + n]
            dq = g * x0(lo, n)
            M[l : l + 1, lo : lo + n] = jnp.sum(dq, axis=0, keepdims=True)
            dql[:, lo : lo + n] = dq.astype(BF)
            e = g * qc[l, :, lo : lo + n]
            d0[:, lo : lo + n] = e if l == 2 else d0[:, lo : lo + n] + e
        dpr[...] = nt(dql[...], UT[l]).astype(BF)
        gr = R_["g_c%d" % l]
        yfirst = ITEMS["c%d" % l][2]
        for lo, n in CH:
            gu = tn(pr[l], dql[:, lo : lo + n]).reshape(32, 8, n)
            gv = tn(dpr[...], xl[l, :, lo : lo + n]).reshape(32, 8, n)
            gg = jnp.concatenate([gv, gu], axis=1).astype(BF)
            for k in range(32):
                rep, xx, yy, zz = place(k)
                a, b = (yy, xx) if yfirst else (xx, yy)
                gr[rep, a, b, zz, :, lo : lo + n] = gg[k]

    def cross_down(l):
        for lo, n in CH:
            v = dx[:, lo : lo + n] + nn(dpr[...], VT[l, :, lo : lo + n])
            if l:
                dx[:, lo : lo + n] = v
            else:
                d0[:, lo : lo + n] = d0[:, lo : lo + n] + v

    cross_back(2)
    s0("c2")
    s1("i")
    cross_down(2)
    cross_back(1)
    s0("c1")
    s1("c2")
    cross_down(1)
    cross_back(0)
    s0("c0")
    cm = go(M, R_["MC"], core)
    s1("c1")
    cross_down(0)
    for i in range(9):
        c = slice(128 * i, 128 * i + 128)
        xT[c, :] = d0[:, c].T
    for t in range(26):
        DE[t] = jnp.concatenate([xT[39 * t : 39 * t + 39, :], jnp.zeros((1, 384), F32)], axis=0)
    DE[26] = jnp.zeros((40, 384), F32)

    def back_rows(d):
        return jnp.concatenate([DE[inv[2 * d]], DE[inv[2 * d + 1]]], axis=0).astype(BF)

    def dstep(i, _):
        d = (me + i) % 16
        eout[d] = back_rows(d)
        dcopy(d, me).start()
        return 0

    lax.fori_loop(1, 16, dstep, 0)
    D[me] = back_rows(me)
    s1("c0")
    MS, MX = R_["MS"], R_["MX"]
    cm.wait_recv()
    MS[0] = M[...] + R_["MC"][...]
    m1 = go(MS.at[0], MX.at[0], xpeer)
    R[...] = jnp.zeros_like(R)

    def one_part(i, s):
        d = (me + i) % 16
        ids = id_rows(d)[s : s + 1]
        lo, hi = ids % 512, ids // 512
        e = D[d].astype(F32)[40 * s : 40 * s + 40]
        lhs = jnp.concatenate([jnp.where(hi == g, e, 0.0) for g in range(8)], axis=0).astype(BF)
        return lhs, one_hot(lo)

    def rows_in(a, b):
        def acc(i2, _):
            for j in range(2):
                i = 2 * i2 + j
                d = (me + i) % 16

                @pl.when(i > 0)
                def _():
                    dcopy(d, d).wait_recv()
            for s in range(2):
                u, v = one_part(2 * i2, s), one_part(2 * i2 + 1, s)
                R[s] += nt(jnp.concatenate([u[0], v[0]], axis=1), jnp.concatenate([u[1], v[1]], axis=1))
            return 0
        lax.fori_loop(a, b, acc, 0)

    s2("m")
    m1.wait_recv()
    MS[1] = MS[0] + MX[0]
    m2 = go(MS.at[1], MX.at[1], ypeer)
    rows_in(0, 1)
    s2("i")
    m2.wait_recv()
    MS[2] = MS[1] + MX[1]
    m3 = [go(MS.at[2], MX.at[2 + i], zpeer[i]) for i in range(3)]
    rows_in(1, 2)
    s2("c2")
    s3("m")
    rows_in(2, 4)
    s2("c1")
    s3("i")
    rows_in(4, 6)
    s2("c0")
    s3("c2")
    rows_in(6, 8)
    for s in range(2):
        for j in range(32):
            g, h = j // 4, j % 4
            gt[pl.ds(2 * j + s, 39, stride=64), :] = R[s, g * 40 : g * 40 + 39, h * 128 : (h + 1) * 128]
    cg = go(gt, gtc, core)
    s3("c1")
    s3("c0")
    for c in m3:
        c.wait_recv()
    pos = [MS[2], MX[2], MX[3], MX[4]]
    u = jnp.where(z % 2 == 0, pos[0], pos[1]) + jnp.where(z % 2 == 0, pos[1], pos[0])
    v = jnp.where(z % 2 == 0, pos[2], pos[3]) + jnp.where(z % 2 == 0, pos[3], pos[2])
    MO[...] = jnp.where(z < 2, u, v) + jnp.where(z < 2, v, u)
    for n in ORDER:
        s4(n)
    cg.wait_recv()

    def dw(i, _):
        d = (me + i) % 16
        dcopy(d, d).wait_send()
        return 0

    lax.fori_loop(1, 16, dw, 0)
    for c in sends:
        c.wait_send()


def mega(total, ts, inv, ids, tab, cr, ti, tm, hd, dns, lab, bia):
    V, S = pltpu.VMEM, jax.ShapeDtypeStruct
    vm, sm, an = pl.BlockSpec(memory_space=pltpu.VMEM), pl.BlockSpec(memory_space=pltpu.SMEM), pl.BlockSpec(memory_space=pl.ANY)
    ins = {"ts": ts, "inv": inv, "bia": bia, "ids": ids, "tab": tab, "cr": cr, "ti": ti, "tm": tm, "hd": hd, "dns": dns, "lab": lab}
    outs = {"gt": S((2496, 128), F32), "gtc": S((2496, 128), F32), "MO": S((8, LN), F32)}
    for n in ORDER:
        outs["o_" + n] = S(ITEMS[n][:2], F32)
    scr = {n + "_v": V(ins[n].shape, ins[n].dtype) for n in ("ids", "tab", "cr", "ti", "tm", "hd", "dns", "lab")}
    scr.update(
        G=V((32, RB, LN), BF), E=V((16, 80, 384), BF), D=V((16, 80, 384), BF), eout=V((16, 80, 384), BF), tabr=V((2, 320, 512), BF),
        xT=V((LN, 384), F32), dx=V((384, LN), F32), xl=V((4, 384, LN), BF), qc=V((3, 384, LN), F32), pr=V((3, 384, 256), BF),
        VT=V((3, 256, LN), BF), UT=V((3, 256, LN), BF), a1=V((384, 1024), F32), a2=V((384, 1024), F32), h1=V((384, 1024), BF), h2=V((384, 1024), BF),
        d0=V((384, LN), F32), dql=V((384, LN), BF), dpr=V((384, 256), BF), DE=V((27, 40, 384), F32), M=V((8, LN), F32), R=V((2, 320, 512), F32),
        MC=V((8, LN), F32), MS=V((3, 8, LN), F32), MX=V((5, 8, LN), F32))
    for n in ORDER:
        nb, L, _ = ITEMS[n]
        scr["g_" + n] = V((2, 2, 2, 4, nb, L), BF)
        scr["C_" + n] = V((2, 2, 4, nb, L), BF)
        scr["P_" + n] = V((2, 4, nb, L), BF)
        scr["Q_" + n] = V((4, nb, L), BF)
        scr["T_" + n] = V((3, nb, L), BF)
    dma = pltpu.SemaphoreType.DMA
    scr.update(lsem=dma((8,)), wss=dma((2, 32)), wrs=dma((2, 32)), ess=dma((16,)), ers=dma((16,)), dss=dma((16,)), drs=dma((16,)), rss=dma((40,)), rrs=dma((40,)))
    res = pl.pallas_call(
        functools.partial(mega_body, total, list(ins), list(outs), list(scr)), name="train_step",
        out_shape=tuple(outs.values()), in_specs=[sm, sm, vm] + [an] * 8, out_specs=(vm,) * len(outs),
        scratch_shapes=list(scr.values()),
        compiler_params=pltpu.CompilerParams(collective_id=0, has_side_effects=True, vmem_limit_bytes=63 << 20),
    )(*ins.values())
    return dict(zip(outs, res))


C5 = 1 - 0.5**5


def adamw(w, m, v, g, rate):
    mn = 0.5 * m + 0.5 * g
    vn = 0.5 * v + 0.5 * g * g
    return w - rate * ((mn / C5) / (jnp.sqrt(vn / C5) + EPSILON) + WEIGHT_DECAY * w), mn, vn


def update_body(names_in, names_out, names_scr, *refs):
    it = iter(refs)
    R_ = {n: next(it) for n in names_in + names_out + names_scr}
    rc, isem, osem = R_["rc"], R_["isem"], R_["osem"]
    order = [k + q for k in "tcim" for q in "wnv"]
    ld = {}
    for i, n in enumerate(order + ["gt", "gtc"]):
        ld[n] = pltpu.make_async_copy(R_[n], R_["v_" + n], isem.at[i])
        ld[n].start()
    outs = []

    def out(name, rows=None):
        i = len(outs)
        s, d = R_["u_" + name], R_["o_" + name]
        if rows is not None:
            s, d = s.at[rows], d.at[rows]
        c = pltpu.make_async_copy(s, d, osem.at[i])
        c.start()
        outs.append(c)

    rows = {"c": [("c0", 0, 16), ("c1", 16, 16), ("c2", 32, 16)], "i": [("i", 0, 32)], "m": [("m", 0, 32)]}
    for k in "imc":
        for q in "wnv":
            ld[k + q].wait()
        for n, lo, nb in rows[k]:
            L = R_["v_" + k + "w"].shape[1]
            at = slice(lo, lo + nb)
            w, m, v = adamw(R_["v_" + k + "w"][at], R_["v_" + k + "n"][at], R_["v_" + k + "v"][at], R_["g_" + n][:, 0:L], RATE_DENSE)
            R_["u_" + k + "w"][at], R_["u_" + k + "n"][at], R_["u_" + k + "v"][at], R_["u_" + k + "l"][at] = w, m, v, w.astype(BF)
        for q in "wnvl":
            out(k + q)
    for n in ("tw", "tn", "tv", "gt", "gtc"):
        ld[n].wait()
    row = lax.broadcasted_iota(jnp.int32, (64, 128), 0)
    lane = lax.broadcasted_iota(jnp.int32, (64, 128), 1)
    use = ((row // 2) * 128 + lane) < jnp.where(row % 2 == 0, rc[0], rc[1])
    for part in range(3):
        def tab(c, _):
            q = pl.ds(pl.multiple_of(c * 64, 64), 64)
            w, m, v = R_["v_tw"][q], R_["v_tn"][q], R_["v_tv"][q]
            nw, nm, nv = adamw(w, m, v, R_["v_gt"][q] + R_["v_gtc"][q], RATE_TABLE)
            nw = jnp.where(use, nw, w)
            R_["u_tw"][q] = nw
            R_["u_tn"][q] = jnp.where(use, nm, m)
            R_["u_tv"][q] = jnp.where(use, nv, v)
            R_["u_tl"][q] = nw.astype(BF)
            return 0
        lax.fori_loop(13 * part, 13 * part + 13, tab, 0)
        for q in "wnvl":
            out("t" + q, pl.ds(832 * part, 832))
    for c in outs:
        c.wait()


def update(rc, g, state):
    V, S = pltpu.VMEM, jax.ShapeDtypeStruct
    vm, sm, an = pl.BlockSpec(memory_space=pltpu.VMEM), pl.BlockSpec(memory_space=pltpu.SMEM), pl.BlockSpec(memory_space=pl.ANY)
    ins, specs = {"rc": rc}, [sm]
    for k in "tcim":
        for q, a in zip("wnv", state[k]):
            ins[k + q] = a
            specs.append(an)
    for n in ("gt", "gtc"):
        ins[n] = g[n]
        specs.append(an)
    for n in ORDER:
        ins["g_" + n] = g["o_" + n]
        specs.append(vm)
    outs, scr = {}, {}
    for k in "tcim":
        for q in "wnvl":
            shape, kind = state[k][0].shape, BF if q == "l" else F32
            outs["o_" + k + q] = S(shape, kind)
            scr["u_" + k + q] = V(shape, kind)
            if q != "l":
                scr["v_" + k + q] = V(shape, kind)
    scr["v_gt"] = V((2496, 128), F32)
    scr["v_gtc"] = V((2496, 128), F32)
    scr["isem"] = pltpu.SemaphoreType.DMA((14,))
    scr["osem"] = pltpu.SemaphoreType.DMA((24,))
    return pl.pallas_call(
        functools.partial(update_body, list(ins), list(outs), list(scr)), name="adamw_step",
        out_shape=tuple(outs.values()), in_specs=specs, out_specs=(an,) * len(outs), scratch_shapes=list(scr.values()),
        compiler_params=pltpu.CompilerParams(vmem_limit_bytes=63 << 20),
    )(*ins.values())


def tab_view(t):
    S, n, C = t.shape
    return jnp.transpose(jnp.transpose(t, (2, 0, 1)).reshape(C, S, n // 128, 128), (0, 2, 1, 3)).reshape(C * S * n // 128, 128)


def tab_unview(v, S=2, n=4096, C=39):
    return jnp.transpose(jnp.transpose(v.reshape(C, n // 128, S, 128), (0, 2, 1, 3)).reshape(C, S, n), (1, 2, 0))


def fast_shards(
    event_ids, row_counts, table_slot, dense_input, labels,
    tables, tables_m, tables_v, cross_uv, cross_m, cross_v,
    tower_in, tower_in_m, tower_in_v, tower_mid, tower_mid_m, tower_mid_v,
    head_weight, head_m, head_v, biases, biases_m, biases_v,
):
    total = float(labels.shape[0] * lax.axis_size("dp") * lax.axis_size("rep"))
    turn = lambda a: jnp.transpose(a, (0, 1, 3, 2)).reshape(48, WIDTH)
    back = lambda a: jnp.transpose(a.reshape(LAYERS, 2, 8, WIDTH), (0, 1, 3, 2))
    state = {
        "t": [tab_view(a) for a in (tables, tables_m, tables_v)],
        "c": [turn(a) for a in (cross_uv, cross_m, cross_v)],
        "i": [a.T for a in (tower_in, tower_in_m, tower_in_v)],
        "m": [a.T for a in (tower_mid, tower_mid_m, tower_mid_v)],
    }
    hits = table_slot[None, :] == jnp.arange(32, dtype=jnp.int32)[:, None]
    inv = TABLES - jnp.sum(hits * (TABLES - jnp.arange(TABLES, dtype=jnp.int32))[None, :], axis=1)
    wide = lambda v: jnp.pad(v, (0, LN - v.shape[0]))
    at = LAYERS * WIDTH
    bia = jnp.stack(
        [wide(biases[WIDTH * i : WIDTH * i + WIDTH]) for i in range(3)]
        + [wide(biases[at : at + 1024]), wide(biases[at + 1024 : at + 2048]),
           jnp.broadcast_to(biases[at + 2048], (LN,)), jnp.zeros((LN,), F32), jnp.zeros((LN,), F32)]
    )
    g = mega(total, table_slot, inv, event_ids, state["t"][0], state["c"][0], state["i"][0], state["m"][0],
             head_weight.reshape(1, 32), dense_input.T, labels.reshape(1, 384), bia)
    o = update(row_counts, g, state)
    MO = g["MO"]
    loss = MO[6, 0]
    g_bias = jnp.concatenate([MO[0, :WIDTH], MO[1, :WIDTH], MO[2, :WIDTH], MO[3, :1024], MO[4, :1024], MO[7, :1]])
    k = lax.axis_index("dp") * 2 + lax.axis_index("rep")
    g_head = lax.dynamic_slice(MO[5], (k * 32,), (32,))
    tail = []
    for w, m, v, gg, rate in ((head_weight, head_m, head_v, g_head, RATE_DENSE), (biases, biases_m, biases_v, g_bias, RATE_BIAS)):
        a, b, c = adamw_update(w, m, v, gg, rate)
        tail += [a, b, c, a.astype(BF)]
    return (
        loss,
        *[tab_unview(a) for a in o[0:4]],
        *[back(a) for a in o[4:8]],
        *[a.T for a in o[8:12]],
        *[a.T for a in o[12:16]],
        *tail,
    )


def solution(mesh):
    placed = (
        P("dp", None),
        P("dp"),
        P(),
        P(("dp", "rep"), None),
        P(("dp", "rep")),
        P("dp", None, None),
        P("dp", None, None),
        P("dp", None, None),
        P(None, None, None, ("dp", "rep")),
        P(None, None, None, ("dp", "rep")),
        P(None, None, None, ("dp", "rep")),
        P(None, ("dp", "rep")),
        P(None, ("dp", "rep")),
        P(None, ("dp", "rep")),
        P(None, ("dp", "rep")),
        P(None, ("dp", "rep")),
        P(None, ("dp", "rep")),
        P(("dp", "rep")),
        P(("dp", "rep")),
        P(("dp", "rep")),
        P(),
        P(),
        P(),
    )
    fits = mesh.shape["dp"] == 16 and mesh.shape["rep"] == 2
    return jax.shard_map(
        fast_shards if fits else shards,
        mesh=mesh,
        in_specs=placed,
        out_specs=(
            P(),
            P("dp", None, None),
            P("dp", None, None),
            P("dp", None, None),
            P("dp", None, None),
            P(None, None, None, ("dp", "rep")),
            P(None, None, None, ("dp", "rep")),
            P(None, None, None, ("dp", "rep")),
            P(None, None, None, ("dp", "rep")),
            P(None, ("dp", "rep")),
            P(None, ("dp", "rep")),
            P(None, ("dp", "rep")),
            P(None, ("dp", "rep")),
            P(None, ("dp", "rep")),
            P(None, ("dp", "rep")),
            P(None, ("dp", "rep")),
            P(None, ("dp", "rep")),
            P(("dp", "rep")),
            P(("dp", "rep")),
            P(("dp", "rep")),
            P(("dp", "rep")),
            P(),
            P(),
            P(),
            P(),
        ),
        check_vma=False,
    )
```

```python
import functools
import math

import jax
import jax.numpy as jnp
from jax import lax
from jax.experimental import pallas as pl
from jax.experimental.pallas import tpu as pltpu
from jax.sharding import PartitionSpec as P

TABLES = 26
EMB = 39
HIDDEN_SIZE = 1024
LAYERS = 3
MICRO = 3
STEP = 5
WIDTH = 1027


BETA_ONE = 0.5
BETA_TWO = 0.5
EPSILON = 1e-10
WEIGHT_DECAY = 0.01
RATE_DENSE = 0.01
RATE_BIAS = 0.05
RATE_TABLE = 0.2
HIGHEST_PRECISION = lax.Precision.HIGHEST


def adamw_update(weight, moment_one, moment_two, gradient, step_rate):
    moment_new = BETA_ONE * moment_one + (1 - BETA_ONE) * gradient
    second = BETA_TWO * moment_two + (1 - BETA_TWO) * gradient * gradient
    scaled_one = moment_new / (1 - BETA_ONE**STEP)
    scaled_two = second / (1 - BETA_TWO**STEP)
    fresh = weight - step_rate * (
        scaled_one / (jnp.sqrt(scaled_two) + EPSILON) + WEIGHT_DECAY * weight
    )
    return (fresh, moment_new, second)


def silu_slope(pre_value):
    sigmoid_value = jax.nn.sigmoid(pre_value)
    return sigmoid_value * (1.0 + pre_value * (1.0 - sigmoid_value))


def contract_rows(left_side, right_side):
    return lax.dot_general(
        left_side, right_side, (((0,), (0,)), ((), ())), preferred_element_type=jnp.float32
    )


def contract_cols(left_side, right_side):
    return lax.dot_general(
        left_side, right_side, (((1,), (1,)), ((), ())), preferred_element_type=jnp.float32
    )


def one_hot_rows(positions, row_total):
    return (positions[:, None] == jnp.arange(row_total, dtype=jnp.int32)[None, :]).astype(
        jnp.bfloat16
    )


def lookup_rows(table_piece, positions):
    count = positions.shape[0]
    block = math.gcd(count, 512)
    blocks = positions.reshape(count // block, block)

    def one_block(block_ids):
        return jnp.dot(
            one_hot_rows(block_ids, table_piece.shape[0]),
            table_piece,
            preferred_element_type=jnp.float32,
        ).astype(jnp.bfloat16)

    return lax.map(one_block, blocks).reshape(count, table_piece.shape[1])


def accumulate_rows(entry_rows, positions, row_total):
    count = positions.shape[0]
    block = math.gcd(count, 512)
    blocks = positions.reshape(count // block, block)
    entry_blocks = entry_rows.reshape(count // block, block, entry_rows.shape[1])

    def add_block(running, pair):
        block_ids, block_rows = pair
        return (running + contract_rows(one_hot_rows(block_ids, row_total), block_rows), None)

    start = jnp.zeros((row_total, entry_rows.shape[1]), jnp.float32)
    summed, unused = lax.scan(add_block, start, (blocks, entry_blocks))
    return summed


def cross_forward(anchor, carried, cross_full, layer_bias, which_layer):
    carried_low = carried.astype(jnp.bfloat16)
    project = jnp.dot(
        carried_low, cross_full[which_layer, 0], preferred_element_type=jnp.float32
    ).astype(jnp.bfloat16)
    crossed = contract_cols(project, cross_full[which_layer, 1])
    return (anchor * (crossed + layer_bias[which_layer]) + carried, (carried_low, project, crossed))


def cross_backward(anchor, grad_carried, saved_values, cross_full, layer_bias, which_layer):
    carried_low, project, crossed = saved_values
    grad_cross = grad_carried * anchor
    bias_grad = jnp.sum(grad_cross, axis=0)
    grad_cross_low = grad_cross.astype(jnp.bfloat16)
    grad_up = contract_rows(grad_cross_low, project)
    grad_project = jnp.dot(
        grad_cross_low, cross_full[which_layer, 1], preferred_element_type=jnp.float32
    ).astype(jnp.bfloat16)
    grad_down = contract_rows(carried_low, grad_project)
    grad_input = contract_cols(grad_project, cross_full[which_layer, 0]) + grad_carried
    extra_grad = grad_carried * (crossed + layer_bias[which_layer])
    return (grad_input, extra_grad, jnp.stack([grad_down, grad_up]), bias_grad)


def micro_step(gathered, biases, emb_flat, dense_rows, target, total_events):
    cross_full, tower_full, mid_full, head_full = gathered
    layer_bias = biases[: LAYERS * WIDTH].reshape(LAYERS, WIDTH)
    bias_one = biases[LAYERS * WIDTH : LAYERS * WIDTH + HIDDEN_SIZE]
    bias_two = biases[LAYERS * WIDTH + HIDDEN_SIZE : LAYERS * WIDTH + 2 * HIDDEN_SIZE]
    bias_out = biases[LAYERS * WIDTH + 2 * HIDDEN_SIZE]
    dense_low = lax.optimization_barrier(dense_rows.astype(jnp.bfloat16)).astype(jnp.float32)
    anchor = jnp.concatenate([emb_flat.astype(jnp.float32), dense_low], axis=1)
    carried = anchor
    saved_all = []
    for which_layer in range(LAYERS):
        carried, saved_values = cross_forward(anchor, carried, cross_full, layer_bias, which_layer)
        saved_all.append(saved_values)
    carried_low = carried.astype(jnp.bfloat16)
    pre_one = jnp.dot(carried_low, tower_full, preferred_element_type=jnp.float32) + bias_one
    hidden_one = jax.nn.silu(pre_one).astype(jnp.bfloat16)
    pre_two = jnp.dot(hidden_one, mid_full, preferred_element_type=jnp.float32) + bias_two
    hidden_two = jax.nn.silu(pre_two).astype(jnp.bfloat16)
    logits = jnp.dot(hidden_two, head_full, preferred_element_type=jnp.float32) + bias_out
    loss_part = jnp.sum(jax.nn.softplus(logits) - target * logits)
    grad_logits = (jax.nn.sigmoid(logits) - target) / total_events
    grad_head = jnp.dot(grad_logits, hidden_two.astype(jnp.float32), precision=HIGHEST_PRECISION)
    grad_hidden_two = grad_logits[:, None] * head_full.astype(jnp.float32)[None, :]
    grad_pre_two = (grad_hidden_two * silu_slope(pre_two)).astype(jnp.bfloat16)
    grad_mid = contract_rows(hidden_one, grad_pre_two)
    grad_hidden_one = contract_cols(grad_pre_two, mid_full)
    grad_pre_one = (grad_hidden_one * silu_slope(pre_one)).astype(jnp.bfloat16)
    grad_tower = contract_rows(carried_low, grad_pre_one)
    grad_carried = contract_cols(grad_pre_one, tower_full)
    grad_anchor = jnp.zeros_like(anchor)
    cross_grads = [None] * LAYERS
    layer_grads = [None] * LAYERS
    for which_layer in reversed(range(LAYERS)):
        grad_carried, extra_grad, grad_pair, bias_grad = cross_backward(
            anchor, grad_carried, saved_all[which_layer], cross_full, layer_bias, which_layer
        )
        grad_anchor = grad_anchor + extra_grad
        cross_grads[which_layer] = grad_pair
        layer_grads[which_layer] = bias_grad
    grad_anchor = grad_anchor + grad_carried
    grad_emb = grad_anchor[:, : TABLES * EMB].astype(jnp.bfloat16)
    bias_grads = jnp.concatenate(
        [
            jnp.stack(layer_grads).reshape(-1),
            jnp.sum(grad_pre_one.astype(jnp.float32), axis=0),
            jnp.sum(grad_pre_two.astype(jnp.float32), axis=0),
            jnp.sum(grad_logits)[None],
        ]
    )
    dense_grads = (jnp.stack(cross_grads), grad_tower, grad_mid, grad_head)
    return (loss_part, grad_emb, dense_grads, bias_grads)


def shards(
    event_ids,
    row_counts,
    table_slot,
    dense_input,
    labels,
    tables,
    tables_m,
    tables_v,
    cross_uv,
    cross_m,
    cross_v,
    tower_in,
    tower_in_m,
    tower_in_v,
    tower_mid,
    tower_mid_m,
    tower_mid_v,
    head_weight,
    head_m,
    head_v,
    biases,
    biases_m,
    biases_v,
):
    dp_count = lax.axis_size("dp")
    rep_count = lax.axis_size("rep")
    rep_index = lax.axis_index("rep")
    slot_count = tables.shape[0]
    row_total = tables.shape[1]
    device_events = labels.shape[0]
    micro_events = device_events // MICRO
    total_events = float(device_events * dp_count * rep_count)
    shard_set = (cross_uv, tower_in, tower_mid, head_weight)
    shard_low = tuple((shard_piece.astype(jnp.bfloat16) for shard_piece in shard_set))
    event_grid = event_ids.reshape(slot_count, dp_count, rep_count, MICRO, micro_events)
    own_ids = lax.dynamic_index_in_dim(event_grid, rep_index, 2, keepdims=False)
    table_low = tables.astype(jnp.bfloat16)
    selector = (
        table_slot[:, None] == jnp.arange(dp_count * slot_count, dtype=jnp.int32)[None, :]
    ).astype(jnp.bfloat16)
    loss_total = jnp.zeros((), jnp.float32)
    bias_total = jnp.zeros(biases.shape, jnp.float32)
    table_grad = jnp.zeros(tables.shape, jnp.float32)
    dense_total = None
    for micro_index in range(MICRO):
        gathered = (
            lax.all_gather(shard_low[0], ("dp", "rep"), axis=3, tiled=True),
            lax.all_gather(shard_low[1], ("dp", "rep"), axis=1, tiled=True),
            lax.all_gather(shard_low[2], ("dp", "rep"), axis=1, tiled=True),
            lax.all_gather(shard_low[3], ("dp", "rep"), axis=0, tiled=True),
        )
        micro_ids = own_ids[:, :, micro_index, :].reshape(slot_count, dp_count * micro_events)
        looked = jax.vmap(lookup_rows)(table_low, micro_ids)
        outgoing = jnp.transpose(
            looked.reshape(slot_count, dp_count, micro_events, EMB), (1, 0, 2, 3)
        )
        arrived = lax.all_to_all(outgoing, "dp", split_axis=0, concat_axis=0, tiled=True)
        by_slot = arrived.reshape(dp_count * slot_count, micro_events, EMB)
        picked = jnp.einsum(
            "ts,sec->tec", selector, by_slot, preferred_element_type=jnp.float32
        ).astype(jnp.bfloat16)
        emb_flat = jnp.transpose(picked, (1, 0, 2)).reshape(micro_events, TABLES * EMB)
        row_lo = micro_index * micro_events
        dense_rows = dense_input[row_lo : row_lo + micro_events]
        target = labels[row_lo : row_lo + micro_events].astype(jnp.float32)
        loss_part, grad_emb, dense_grads, bias_grads = micro_step(
            gathered, biases, emb_flat, dense_rows, target, total_events
        )
        loss_total = loss_total + loss_part
        bias_total = bias_total + bias_grads
        if micro_index == 0:
            dense_total = dense_grads
        else:
            dense_total = tuple(
                (running + fresh_part for running, fresh_part in zip(dense_total, dense_grads))
            )
        grad_tables = jnp.transpose(grad_emb.reshape(micro_events, TABLES, EMB), (1, 0, 2))
        slot_grads = jnp.einsum(
            "ts,tec->sec", selector, grad_tables, preferred_element_type=jnp.float32
        ).astype(jnp.bfloat16)
        returned = lax.all_to_all(
            slot_grads.reshape(dp_count, slot_count, micro_events, EMB),
            "dp",
            split_axis=0,
            concat_axis=0,
            tiled=True,
        )
        entries = jnp.transpose(returned, (1, 0, 2, 3)).reshape(
            slot_count, dp_count * micro_events, EMB
        )
        table_grad = table_grad + jax.vmap(
            lambda entry_rows, positions: accumulate_rows(entry_rows, positions, row_total)
        )(entries, micro_ids)
    dense_total = (
        lax.psum_scatter(dense_total[0], ("dp", "rep"), scatter_dimension=3, tiled=True),
        lax.psum_scatter(dense_total[1], ("dp", "rep"), scatter_dimension=1, tiled=True),
        lax.psum_scatter(dense_total[2], ("dp", "rep"), scatter_dimension=1, tiled=True),
        lax.psum_scatter(dense_total[3], ("dp", "rep"), scatter_dimension=0, tiled=True),
    )
    table_grad = lax.psum(table_grad, "rep")
    bias_total, loss_total = lax.psum((bias_total, loss_total), ("dp", "rep"))
    fresh_tab, fresh_tab_m, fresh_tab_v = adamw_update(
        tables, tables_m, tables_v, table_grad, RATE_TABLE
    )
    in_use = (jnp.arange(row_total, dtype=jnp.int32)[None, :] < row_counts[:, None])[:, :, None]
    fresh_tab = jnp.where(in_use, fresh_tab, tables)
    fresh_tab_m = jnp.where(in_use, fresh_tab_m, tables_m)
    fresh_tab_v = jnp.where(in_use, fresh_tab_v, tables_v)
    weight_set = shard_set + (biases,)
    grad_set = tuple(dense_total) + (bias_total,)
    states = (
        (cross_m, cross_v, RATE_DENSE),
        (tower_in_m, tower_in_v, RATE_DENSE),
        (tower_mid_m, tower_mid_v, RATE_DENSE),
        (head_m, head_v, RATE_DENSE),
        (biases_m, biases_v, RATE_BIAS),
    )
    results = []
    for weight, gradient, state in zip(weight_set, grad_set, states):
        fresh, moment_new, second = adamw_update(weight, state[0], state[1], gradient, state[2])
        results.append((fresh, moment_new, second, fresh.astype(jnp.bfloat16)))
    return (
        loss_total,
        fresh_tab,
        fresh_tab_m,
        fresh_tab_v,
        fresh_tab.astype(jnp.bfloat16),
        results[0][0],
        results[0][1],
        results[0][2],
        results[0][3],
        results[1][0],
        results[1][1],
        results[1][2],
        results[1][3],
        results[2][0],
        results[2][1],
        results[2][2],
        results[2][3],
        results[3][0],
        results[3][1],
        results[3][2],
        results[3][3],
        results[4][0],
        results[4][1],
        results[4][2],
        results[4][3],
    )


MESH = pl.DeviceIdType.MESH
F32 = jnp.float32
BF = jnp.bfloat16
LN = 1152
RB = 112
BIASES = 5130
CH = [(0, 256), (256, 256), (512, 256), (768, 256), (1024, 128)]
ITEMS = {
    "m0": (16, 1024, True, "m", 0),
    "m1": (16, 1024, False, "m", 16),
    "i": (32, LN, True, "i", 0),
    "c2": (16, LN, False, "c2", 0),
    "c1": (16, LN, True, "c1", 0),
    "c0": (16, LN, False, "c0", 0),
}
ORDER = list(ITEMS)
SUMS = {"m": (32, 1024), "i": (32, LN), "c2": (16, LN), "c1": (16, LN), "c0": (16, LN)}
PARTS = {"A": (0, 48, True), "I": (48, 48, False), "U": (96, 16, False)}
LAST_Z = "U"
FORWARD = [
    "ownU", "ownI", "ownA", "prep", "L0", "L1", "f1I-", "f1U-", "corU", "fzI0", "fzA0", "fzI1", "fzA1", "f1A-", "L2", "L3",
    "f2U-1", "f2U-0", "fzI2", "f1A0", "corI", "f1I1", "L4", "L5", "L6", "fzA2", "f1A1", "fzU1", "fzU0", "f2A00", "f2I-0",
    "L7", "L8", "f1I0", "f1I2", "f2I10", "corA", "L9", "fzU2", "f2A20", "L10", "f1A2", "f2A10", "f2A-0", "f2A11", "L11",
    "f2I-1", "f2I20", "L12", "L13", "L14", "f2I01", "f2A-1", "f2A01", "L15", "f2I11", "f2A21", "f2I21", "dei", "f2I00",
    "x0", "cf", "a1", "a2",
]
BACKWARD = [
    "dTm", "dh1", "dx3", "s1m0", "s1m1", "ch2", "cg2", "ch1", "ch0", "cg0", "s2m1", "M1", "D", "dTi", "s3m1", "M2", "s1c2",
    "s1i", "cg1", "s2m0", "M3", "s2i", "s3m0", "s1c0", "s2c2", "s1c1", "s3i", "sc0", "sc1", "s4m1", "sc2", "sc3", "sc4",
    "s4m0", "s3c2", "s2c1", "s2c0", "s3c1", "sc5", "sc6", "s3c0", "sc7", "s4c2", "gt", "M4", "s4c1", "s4i", "gts", "s4c0",
]


def nt(a, b):
    return lax.dot_general(a, b, (((1,), (1,)), ((), ())), preferred_element_type=F32)


def nn(a, b):
    return lax.dot_general(a, b, (((1,), (0,)), ((), ())), preferred_element_type=F32)


def tn(a, b):
    return lax.dot_general(a, b, (((0,), (0,)), ((), ())), preferred_element_type=F32)


def sig(v):
    return 1.0 / (1.0 + jnp.exp(-v))


def slope(v):
    s = sig(v)
    return s * (1.0 + v * (1.0 - s))


def place(k):
    rep, d = k % 2, k // 2
    return rep, d % 2, (d // 2) % 2, d // 4


def mega_body(total, names_in, names_out, names_scr, *refs):
    it = iter(refs)
    R_ = {n: next(it) for n in names_in + names_out + names_scr}
    ts, inv = R_["ts"], R_["inv"]
    G, E, D, eout, tabr = R_["G"], R_["E"], R_["D"], R_["eout"], R_["tabr"]
    xT, dx, xl, qc, pr = R_["xT"], R_["dx"], R_["xl"], R_["qc"], R_["pr"]
    VT, UT, h1, h2 = R_["VT"], R_["UT"], R_["h1"], R_["h2"]
    d0, dql, dpr, DE, M, R = R_["d0"], R_["dql"], R_["dpr"], R_["DE"], R_["M"], R_["R"]
    ids_ref, tab_ref, bia = R_["ids_v"], R_["gg"], R_["bia"]
    xr, a1, a2, d1, d2 = dx, dx, d0, h1, h2
    gt, gg_, gtc, MO = R_["gt"], R_["gg"], R_["gtc"], R_["MO"]
    me = lax.axis_index("dp")
    r = lax.axis_index("rep")
    x, y, z = me % 2, (me // 2) % 2, me // 4
    dev = lambda zz, yy, xx: zz * 4 + yy * 2 + xx
    zp = [z + 1 - 2 * (z % 2), (z + 2) % 4, 3 - z]
    own = me * 2 + r
    xpeer, ypeer, core = (dev(z, y, 1 - x), r), (dev(z, 1 - y, x), r), (me, 1 - r)
    zpeer = [(dev(q, y, x), r) for q in zp]

    loads = {}
    for i, n in enumerate(["cr", "ti", "tm", "hd", "tab", "ids", "dns", "lab", "bi"]):
        c = pltpu.make_async_copy(R_[n], R_["gg" if n == "tab" else n + "_v"], R_["lsem"].at[i])
        c.start()
        loads[n] = c
    bar = pltpu.get_barrier_semaphore()
    for i in range(1, 16):
        pl.semaphore_signal(bar, inc=1, device_id=((me + i) % 16, r), device_id_type=MESH)
    pl.semaphore_signal(bar, inc=1, device_id=core, device_id_type=MESH)

    cr, ti, tm, hd = R_["cr_v"], R_["ti_v"], R_["tm_v"], R_["hd_v"]
    for n in ("cr", "ti", "tm", "hd"):
        loads[n].wait()
    G[own, 0:48, 0:1024] = cr[:, 0:1024].astype(BF)
    G[own, 0:48, 1024:LN] = jnp.concatenate([cr[:, 1024:1027], jnp.zeros((48, 125), F32)], axis=1).astype(BF)
    G[own, 48:80, 0:1024] = ti[:, 0:1024].astype(BF)
    G[own, 48:80, 1024:LN] = jnp.concatenate([ti[:, 1024:1027], jnp.zeros((32, 125), F32)], axis=1).astype(BF)
    G[own, 80:112, 0:1024] = tm[...].astype(BF)
    eye = lax.broadcasted_iota(jnp.int32, (32, 32), 0) == lax.broadcasted_iota(jnp.int32, (32, 32), 1)
    hcol = jnp.sum(jnp.where(eye, jnp.broadcast_to(hd[...].reshape(1, 32), (32, 32)), 0.0), axis=1, keepdims=True)
    G[own, 80:112, 1024:LN] = jnp.broadcast_to(hcol, (32, 128)).astype(BF)
    pl.semaphore_wait(bar, 16)

    cnt = {p: 0 for p in PARTS}
    pnum = {p: i for i, p in enumerate(PARTS)}
    sends = []

    def wcopy(p, k, dst, si):
        lo, n, _ = PARTS[p]
        return pltpu.make_async_remote_copy(
            src_ref=G.at[k, pl.ds(lo, n)], dst_ref=G.at[k, pl.ds(lo, n)],
            send_sem=R_["wss"].at[pnum[p], si], recv_sem=R_["wrs"].at[pnum[p], k], device_id=dst, device_id_type=MESH)

    def wsend(p, k, dst):
        c = wcopy(p, k, dst, cnt[p])
        cnt[p] += 1
        c.start()
        sends.append(c)

    def wwait(p, k):
        wcopy(p, k, core, 0).wait_recv()

    p1 = {p: ypeer if PARTS[p][2] else xpeer for p in PARTS}
    p2 = {p: xpeer if PARTS[p][2] else ypeer for p in PARTS}
    key = lambda zz, yy, xx: dev(zz, yy, xx) * 2 + r
    inner = (z == 1) | (z == 2)
    zq = [zp[0], jnp.where(inner, zp[2], zp[1]), jnp.where(inner, zp[1], zp[2])]
    on_to = [zp[2], zp[0], zp[0]]
    isends = []

    def isend(p, k, zz):
        c = wcopy(p, k, (dev(zz, y, x), r), cnt[p])
        cnt[p] += 1
        isends.append(c)

        @pl.when(inner)
        def _():
            c.start()

    def f_own(p):
        wsend(p, own, (dev(zp[0], y, x), r))
        isend(p, own, zp[2])
        wsend(p, own, p1[p])
        wsend(p, own, p2[p])

    def f_core(p):
        wsend(p, own, core)

    def fwd_z(p, i):
        k = key(zq[i], y, x)
        wwait(p, k)
        isend(p, k, on_to[i])
        wsend(p, k, p1[p])
        wsend(p, k, p2[p])
        wsend(p, k, core)

    def up_down(p, k):
        if p in LAST_Z:
            wsend(p, k, (dev(zp[0], y, x), r))
            isend(p, k, zp[2])

    def fwd_zl(p, i, c):
        k = key(zq[i], (y + c // 2) % 2, (x + c % 2) % 2)
        wwait(p, k)
        isend(p, k, on_to[i])
        wsend(p, k, core)

    def fwd_1(p, i):
        q = z if i < 0 else zq[i]
        k = key(q, 1 - y, x) if PARTS[p][2] else key(q, y, 1 - x)
        wwait(p, k)
        up_down(p, k)
        wsend(p, k, p2[p])
        wsend(p, k, core)

    def fwd_2(p, i, o):
        q = z if i < 0 else zq[i]
        k = key(q, (y + o) % 2, 1 - x) if PARTS[p][2] else key(q, 1 - y, (x + o) % 2)
        wwait(p, k)
        up_down(p, k)
        wsend(p, k, core)

    def core_wait(p):
        def cw(i, _):
            wwait(p, i * 2 + (1 - r))
            return 0
        lax.fori_loop(0, 16, cw, 0)

    def f_prep():
        loads["tab"].wait()
        loads["ids"].wait()
        for s in range(2):
            for j in range(32):
                g, h = j // 4, j % 4
                t = tab_ref[pl.ds(2 * j + s, 39, stride=64), :]
                tabr[s, g * 40 : (g + 1) * 40, h * 128 : (h + 1) * 128] = jnp.concatenate([t, jnp.zeros((1, 128), F32)], axis=0).astype(BF)

    def id_rows(d):
        return ids_ref[:, pl.ds(pl.multiple_of((d * 2 + r) * 384, 128), 384)]

    def one_hot(lo):
        return (lax.broadcasted_iota(jnp.int32, (512, 384), 0) == lo).astype(F32).astype(BF)

    def look(d):
        idv = id_rows(d)
        outs = []
        for s in range(2):
            ids = idv[s : s + 1]
            lo, hi = ids % 512, ids // 512
            res = nn(tabr[s], one_hot(lo))
            e = jnp.zeros((40, 384), F32)
            for g in range(8):
                e = e + jnp.where(hi == g, res[g * 40 : (g + 1) * 40], 0.0)
            outs.append(e)
        return jnp.concatenate(outs, axis=0).astype(BF)

    def ecopy(d, land):
        return pltpu.make_async_remote_copy(
            src_ref=eout.at[d], dst_ref=E.at[land], send_sem=R_["ess"].at[d], recv_sem=R_["ers"].at[land], device_id=(d, r), device_id_type=MESH)

    def dcopy(d, land):
        return pltpu.make_async_remote_copy(
            src_ref=eout.at[d], dst_ref=D.at[land], send_sem=R_["dss"].at[d], recv_sem=R_["drs"].at[land], device_id=(d, r), device_id_type=MESH)

    def nth(i):
        j, w = i // 4, i % 4
        zz = jnp.where(j == 0, zp[1], jnp.where(j == 1, zp[2], jnp.where(j == 2, zp[0], z)))
        return dev(zz, (y + w // 2) % 2, (x + w) % 2)

    def looks(a, b):
        def step(i, _):
            d = nth(i)
            eout[d] = look(d)

            @pl.when(i != 12)
            def _():
                ecopy(d, me).start()
            return 0
        lax.fori_loop(a, b, step, 0)

    x0 = lambda lo, n: xl[0, :, lo : lo + n].astype(F32)

    def f_rows():
        E[me] = eout[me]
        for n in range(32):
            slot_table = jnp.int32(TABLES)
            for t in range(TABLES):
                slot_table = jnp.where(ts[t] == n, t, slot_table)
            inv[n] = slot_table
        loads["bi"].wait()
        bv = R_["bi_v"][...].reshape(1, BIASES)
        bia[...] = jnp.zeros_like(bia)
        for i in range(3):
            bia[i : i + 1, 0:1027] = bv[:, 1027 * i : 1027 * i + 1027]
        bia[3:4, 0:1024] = bv[:, 3081:4105]
        bia[4:5, 0:1024] = bv[:, 4105:5129]
        bia[5:6, :] = jnp.broadcast_to(bv[:, 5129:5130], (1, LN))
        loads["dns"].wait()
        loads["lab"].wait()

        def ew(i, _):
            d = (me + i) % 16
            ecopy(d, d).wait()
            return 0

        lax.fori_loop(1, 16, ew, 0)
        for t in range(26):
            s = ts[t]
            blk = E[s // 2].astype(F32)
            e = jnp.where(s % 2 == 1, blk[40:80], blk[0:40])
            xT[39 * t : 39 * t + 39, :] = e[0:39]
        xT[1014:1027, :] = R_["dns_v"][...].astype(BF).astype(F32)
        xT[1027:LN, :] = jnp.zeros((LN - 1027, 384), F32)
        for i in range(9):
            c = slice(128 * i, 128 * i + 128)
            xl[0, :, c] = xT[c, :].T.astype(BF)

    def f_split():
        core_wait("A")
        for l in range(3):
            for lo, n in CH:
                w = G[:, 16 * l : 16 * l + 16, lo : lo + n].astype(F32).reshape(32, 2, 8, n)
                VT[l, :, lo : lo + n] = w[:, 0].reshape(256, n).astype(BF)
                UT[l, :, lo : lo + n] = w[:, 1].reshape(256, n).astype(BF)

    def f_cross():
        for l in range(3):
            pr[l] = nt(xl[l], VT[l]).astype(BF)
            for lo, n in CH:
                q = nn(pr[l], UT[l, :, lo : lo + n]) + bia[l : l + 1, lo : lo + n]
                qc[l, :, lo : lo + n] = q
                v = x0(lo, n) * q + (x0(lo, n) if l == 0 else xr[:, lo : lo + n])
                if l < 2:
                    xr[:, lo : lo + n] = v
                xl[l + 1, :, lo : lo + n] = v.astype(BF)

    def f_tower_one():
        core_wait("I")
        for n in range(4):
            c = slice(256 * n, 256 * n + 256)
            a = nt(xl[3], G[8 * n : 8 * n + 8, 48:80, :].reshape(256, LN)) + bia[3:4, c]
            a1[:, c] = a
            h1[:, c] = (a * sig(a)).astype(BF)

    def f_tower_two():
        for q in PARTS:
            if q not in "AI":
                core_wait(q)
        for n in range(4):
            c = slice(256 * n, 256 * n + 256)
            a = nt(h1[...], G[8 * n : 8 * n + 8, 80:112, 0:1024].reshape(256, 1024)) + bia[4:5, c]
            a2[:, c] = a
            h2[:, c] = (a * sig(a)).astype(BF)

    plain = {"prep": f_prep, "x0": f_rows, "dei": f_split, "cf": f_cross, "a1": f_tower_one, "a2": f_tower_two}
    step_of = lambda c: -1 if c == "-" else int(c)
    todo = list(FORWARD)
    while todo:
        op = todo.pop(0)
        if op in plain:
            plain[op]()
        elif op[0] == "L":
            a = b = int(op[1:])
            while todo and todo[0][0] == "L":
                b = int(todo.pop(0)[1:])
            looks(a, b + 1)
        elif op[:3] == "own":
            f_own(op[3])
        elif op[:3] == "cor":
            f_core(op[3])
        elif op[:2] == "fz" and op[2] in LAST_Z:
            for c in range(4):
                fwd_zl(op[2], int(op[3]), c)
        elif op[:2] == "fz":
            fwd_z(op[2], int(op[3]))
        elif op[:2] == "f1":
            fwd_1(op[2], step_of(op[3]))
        else:
            fwd_2(op[2], step_of(op[3]), int(op[4]))
    hc = G[:, 80:112, 1024:LN].reshape(1024, 128)
    zl = nn(h2[...], hc) + bia[5:6, 0:128]
    yl = jnp.broadcast_to(R_["lab_v"][...].reshape(1, 384).astype(F32), (128, 384)).T
    lossv = jnp.maximum(zl, 0.0) + jnp.log1p(jnp.exp(-jnp.abs(zl))) - yl * zl
    dz = (sig(zl) - yl) / total
    M[...] = jnp.zeros_like(M)
    M[6:7, 0:128] = jnp.sum(lossv, axis=0, keepdims=True)
    M[7:8, 0:128] = jnp.sum(dz, axis=0, keepdims=True)
    hrow = hc.astype(F32).T[0:1]
    for n in range(8):
        c = slice(128 * n, 128 * n + 128)
        M[5:6, c] = jnp.sum(dz * h2[:, c].astype(F32), axis=0, keepdims=True)
        g = (dz * hrow[:, c] * slope(a2[:, c])).astype(BF)
        d2[:, c] = g
        M[4:5, c] = jnp.sum(g.astype(F32), axis=0, keepdims=True)

    nsem = [0]

    def go(src, dst, dst_dev):
        i = nsem[0]
        nsem[0] += 1
        c = pltpu.make_async_remote_copy(
            src_ref=src, dst_ref=dst, send_sem=R_["rss"].at[i], recv_sem=R_["rrs"].at[i], device_id=dst_dev, device_id_type=MESH)
        c.start()
        sends.append(c)
        return c

    st = {}

    def axes(n):
        return (y, x, ypeer, xpeer) if ITEMS[n][2] else (x, y, xpeer, ypeer)

    def s0(n):
        g = R_["g_" + n]
        st[n] = go(g.at[1 - r], R_["C_" + n], core)

    def s1(n):
        a, b, pa, pb = axes(n)
        st[n].wait_recv()
        g, c = R_["g_" + n], R_["C_" + n]
        st[n] = []
        for bb in (1 - b, b):
            g[r, 1 - a, bb] = (g[r, 1 - a, bb].astype(F32) + c[1 - a, bb].astype(F32)).astype(BF)
            st[n].append(go(g.at[r, 1 - a, bb], R_["P_" + n].at[bb], pa))

    def s2(n):
        a, b, pa, pb = axes(n)
        st[n][0].wait_recv()
        g, c, p = R_["g_" + n], R_["C_" + n], R_["P_" + n]
        g[r, a, 1 - b] = (g[r, a, 1 - b].astype(F32) + c[a, 1 - b].astype(F32) + p[1 - b].astype(F32)).astype(BF)
        st[n].append(go(g.at[r, a, 1 - b], R_["Q_" + n], pb))

    def s3(n):
        a, b, pa, pb = axes(n)
        st[n][1].wait_recv()
        st[n][2].wait_recv()
        g, c, p, q = R_["g_" + n], R_["C_" + n], R_["P_" + n], R_["Q_" + n]
        st[n] = []
        for i, zz in enumerate(zp):
            g[r, a, b, zz] = (g[r, a, b, zz].astype(F32) + c[a, b, zz].astype(F32) + p[b, zz].astype(F32) + q[zz].astype(F32)).astype(BF)
            st[n].append(go(g.at[r, a, b, zz], R_["T_" + n].at[i], zpeer[i]))

    def s4(n):
        a, b, pa, pb = axes(n)
        for c in st[n]:
            c.wait_recv()
        g, c, p, q, t = R_["g_" + n], R_["C_" + n], R_["P_" + n], R_["Q_" + n], R_["T_" + n]
        nb, _, _, out, at = ITEMS[n]
        R_["o_" + out][at : at + nb] = (
            g[r, a, b, z].astype(F32) + c[a, b, z].astype(F32) + p[b, z].astype(F32) + q[z].astype(F32)
            + (t[0].astype(F32) + t[1].astype(F32) + t[2].astype(F32)))

    def parts_of(out):
        return [n for n in ITEMS if ITEMS[n][3] == out]

    def put(out, base, g):
        for n in parts_of(out):
            nb, _, yfirst, _, at = ITEMS[n]
            for i in range(g.shape[0] // 32):
                rep, xx, yy, zz = place(base + i)
                a, b = (yy, xx) if yfirst else (xx, yy)
                R_["g_" + n][rep, a, b, zz] = g[i * 32 + at : i * 32 + at + nb].astype(BF)

    MS, MX = R_["MS"], R_["MX"]

    def grad_mid():
        for n in range(4):
            put("m", 8 * n, tn(d2[:, 256 * n : 256 * n + 256], h1[...]))
        for n in parts_of("m"):
            s0(n)

    def down_one():
        for n in range(4):
            c = slice(256 * n, 256 * n + 256)
            a1[:, c] = nn(d2[...], G[:, 80:112, c].reshape(1024, 256)) * slope(a1[:, c])
        for n in range(4):
            c = slice(256 * n, 256 * n + 256)
            g = a1[:, c].astype(BF)
            d1[:, c] = g
            M[3:4, c] = jnp.sum(g.astype(F32), axis=0, keepdims=True)

    def grad_in():
        for n in range(4):
            put("i", 8 * n, tn(d1[:, 256 * n : 256 * n + 256], xl[3]))
        for n in parts_of("i"):
            s0(n)

    def down_x():
        for lo, n in CH:
            dx[:, lo : lo + n] = nn(d1[...], G[:, 48:80, lo : lo + n].reshape(1024, n))

    def chain(l):
        dq_ref = dql.at[l]
        for lo, n in CH:
            g = dx[:, lo : lo + n]
            dq = g * x0(lo, n)
            M[l : l + 1, lo : lo + n] = jnp.sum(dq, axis=0, keepdims=True)
            dq_ref[:, lo : lo + n] = dq.astype(BF)
            e = g * qc[l, :, lo : lo + n]
            d0[:, lo : lo + n] = e if l == 2 else d0[:, lo : lo + n] + e
        dpr[l] = nt(dq_ref[...], UT[l]).astype(BF)
        for lo, n in CH:
            v = dx[:, lo : lo + n] + nn(dpr[l], VT[l, :, lo : lo + n])
            if l:
                dx[:, lo : lo + n] = v
            else:
                d0[:, lo : lo + n] = d0[:, lo : lo + n] + v
        if l == 0:
            st["M"] = go(M, R_["MC"], core)

    def cross_grads(l):
        gr = R_["g_c%d" % l]
        yfirst = ITEMS["c%d" % l][2]
        for lo, n in CH:
            gu = tn(pr[l], dql[l, :, lo : lo + n]).reshape(32, 8, n)
            gv = tn(dpr[l], xl[l, :, lo : lo + n]).reshape(32, 8, n)
            gg = jnp.concatenate([gv, gu], axis=1).astype(BF)
            for k in range(32):
                rep, xx, yy, zz = place(k)
                a, b = (yy, xx) if yfirst else (xx, yy)
                gr[rep, a, b, zz, :, lo : lo + n] = gg[k]
        s0("c%d" % l)

    def back_rows(d):
        return jnp.concatenate([DE[inv[2 * d]], DE[inv[2 * d + 1]]], axis=0).astype(BF)

    def rows_out():
        for i in range(9):
            c = slice(128 * i, 128 * i + 128)
            xT[c, :] = d0[:, c].T
        for t in range(26):
            DE[t] = jnp.concatenate([xT[39 * t : 39 * t + 39, :], jnp.zeros((1, 384), F32)], axis=0)
        DE[26] = jnp.zeros((40, 384), F32)

        def dstep(i, _):
            d = nth(i)
            eout[d] = back_rows(d)

            @pl.when(i != 12)
            def _():
                dcopy(d, me).start()
            return 0

        lax.fori_loop(0, 16, dstep, 0)
        D[me] = eout[me]

    def one_part(i, s):
        d = nth(15 - i)
        ids = id_rows(d)[s : s + 1]
        lo, hi = ids % 512, ids // 512
        e = D[d].astype(F32)[40 * s : 40 * s + 40]
        lhs = jnp.concatenate([jnp.where(hi == g, e, 0.0) for g in range(8)], axis=0).astype(BF)
        return lhs, one_hot(lo)

    def rows_in(k):
        for i in (2 * k, 2 * k + 1):
            if i != 3:
                d = nth(15 - i)
                dcopy(d, d).wait_recv()
        for s in range(2):
            u, v = one_part(2 * k, s), one_part(2 * k + 1, s)
            p = nt(jnp.concatenate([u[0], v[0]], axis=1), jnp.concatenate([u[1], v[1]], axis=1))
            R[s] = p if k == 0 else R[s] + p

    def table_sum():
        for s in range(2):
            for j in range(32):
                g, h = j // 4, j % 4
                gg_[pl.ds(2 * j + s, 39, stride=64), :] = R[s, g * 40 : g * 40 + 39, h * 128 : (h + 1) * 128]
        st["g"] = go(gg_, gtc, core)

    def table_both():
        st["g"].wait_recv()
        gt[...] = gg_[...] + gtc[...]

    def small(i):
        if i == 1:
            st["M"].wait_recv()
            MS[0] = M[...] + R_["MC"][...]
            st["M"] = go(MS.at[0], MX.at[0], xpeer)
        elif i == 2:
            st["M"].wait_recv()
            MS[1] = MS[0] + MX[0]
            st["M"] = go(MS.at[1], MX.at[1], ypeer)
        elif i == 3:
            st["M"].wait_recv()
            MS[2] = MS[1] + MX[1]
            st["M"] = [go(MS.at[2], MX.at[2 + j], zpeer[j]) for j in range(3)]
        else:
            for c in st["M"]:
                c.wait_recv()
            pos = [MS[2], MX[2], MX[3], MX[4]]
            u = jnp.where(z % 2 == 0, pos[0], pos[1]) + jnp.where(z % 2 == 0, pos[1], pos[0])
            v = jnp.where(z % 2 == 0, pos[2], pos[3]) + jnp.where(z % 2 == 0, pos[3], pos[2])
            MO[...] = jnp.where(z < 2, u, v) + jnp.where(z < 2, v, u)

    stage = {"s1": s1, "s2": s2, "s3": s3, "s4": s4}
    plain = {"dTm": grad_mid, "dh1": down_one, "dTi": grad_in, "dx3": down_x, "D": rows_out, "gt": table_sum, "gts": table_both}
    indexed = {"ch": chain, "cg": cross_grads, "sc": rows_in, "M": small}
    for op in BACKWARD:
        if op in plain:
            plain[op]()
        elif op[:2] in stage:
            stage[op[:2]](op[2:])
        else:
            indexed[op[:-1]](int(op[-1]))

    def dw(i, _):
        d = (me + i) % 16
        dcopy(d, d).wait_send()
        return 0

    lax.fori_loop(1, 16, dw, 0)
    for c in sends:
        c.wait_send()

    @pl.when(inner)
    def _():
        for c in isends:
            c.wait_send()


def mega(total, ts, ids, tab, cr, ti, tm, hd, dns, lab, bi):
    V, S = pltpu.VMEM, jax.ShapeDtypeStruct
    vm, sm, an = pl.BlockSpec(memory_space=pltpu.VMEM), pl.BlockSpec(memory_space=pltpu.SMEM), pl.BlockSpec(memory_space=pl.ANY)
    ins = {"ts": ts, "ids": ids, "tab": tab, "cr": cr, "ti": ti, "tm": tm, "hd": hd, "dns": dns, "lab": lab, "bi": bi}
    outs = {"gt": S((2496, 128), F32), "MO": S((8, LN), F32)}
    for n in SUMS:
        outs["o_" + n] = S(SUMS[n], F32)
    scr = {n + "_v": V(ins[n].shape, ins[n].dtype) for n in ("ids", "cr", "ti", "tm", "hd", "dns", "lab", "bi")}
    scr.update(
        G=V((32, RB, LN), BF), E=V((16, 80, 384), BF), D=V((16, 80, 384), BF), eout=V((16, 80, 384), BF), tabr=V((2, 320, 512), BF),
        xT=V((LN, 384), F32), dx=V((384, LN), F32), xl=V((4, 384, LN), BF), qc=V((3, 384, LN), F32), pr=V((3, 384, 256), BF),
        VT=V((3, 256, LN), BF), UT=V((3, 256, LN), BF), h1=V((384, 1024), BF), h2=V((384, 1024), BF),
        d0=V((384, LN), F32), dql=V((3, 384, LN), BF), dpr=V((3, 384, 256), BF), DE=V((27, 40, 384), F32), M=V((8, LN), F32), R=V((2, 320, 512), F32),
        MC=V((8, LN), F32), MS=V((3, 8, LN), F32), MX=V((5, 8, LN), F32), gg=V((2496, 128), F32), gtc=V((2496, 128), F32), bia=V((8, LN), F32), inv=pltpu.SMEM((32,), jnp.int32))
    for n in ORDER:
        nb, L = ITEMS[n][:2]
        scr["g_" + n] = V((2, 2, 2, 4, nb, L), BF)
        scr["C_" + n] = V((2, 2, 4, nb, L), BF)
        scr["P_" + n] = V((2, 4, nb, L), BF)
        scr["Q_" + n] = V((4, nb, L), BF)
        scr["T_" + n] = V((3, nb, L), BF)
    dma = pltpu.SemaphoreType.DMA
    scr.update(lsem=dma((9,)), wss=dma((3, 40)), wrs=dma((3, 32)), ess=dma((16,)), ers=dma((16,)), dss=dma((16,)), drs=dma((16,)), rss=dma((64,)), rrs=dma((64,)))
    res = pl.pallas_call(
        functools.partial(mega_body, total, list(ins), list(outs), list(scr)), name="train_step",
        out_shape=tuple(outs.values()), in_specs=[sm] + [an] * 9, out_specs=(vm,) * len(outs),
        scratch_shapes=list(scr.values()),
        compiler_params=pltpu.CompilerParams(collective_id=0, has_side_effects=True, vmem_limit_bytes=63 << 20),
    )(*ins.values())
    return dict(zip(outs, res))


C5 = 1 - 0.5**5


def adamw(w, m, v, g, rate):
    mn = 0.5 * m + 0.5 * g
    vn = 0.5 * v + 0.5 * g * g
    return w - rate * ((mn / C5) / (jnp.sqrt(vn / C5) + EPSILON) + WEIGHT_DECAY * w), mn, vn


SMALL = [k + q for k in "hb" for q in "wnv"]


def update_body(names_in, names_out, names_scr, *refs):
    it = iter(refs)
    R_ = {n: next(it) for n in names_in + names_out + names_scr}
    rc, isem, osem = R_["rc"], R_["isem"], R_["osem"]
    order = [k + q for k in "tcim" for q in "wnv"]
    ld = {}
    for n in SMALL + order[3:]:
        ld[n] = pltpu.make_async_copy(R_[n], R_["v_" + n], isem.at[len(ld)])
        ld[n].start()
    for part in range(3):
        for n in ("tw", "tn", "tv", "gt"):
            q = pl.ds(832 * part, 832)
            ld[n, part] = pltpu.make_async_copy(R_[n].at[q], R_["v_" + n].at[q], isem.at[len(ld)])
            ld[n, part].start()
    outs = []

    def out(name, rows=None):
        i = len(outs)
        s, d = R_["u_" + name], R_["o_" + name]
        if rows is not None:
            s, d = s.at[rows], d.at[rows]
        c = pltpu.make_async_copy(s, d, osem.at[i])
        c.start()
        outs.append(c)

    for n in SMALL:
        ld[n].wait()
    MO = R_["MO"]
    R_["o_loss"][0, 0] = jnp.max(MO[6:7, 0:128])
    k = lax.axis_index("dp") * 2 + lax.axis_index("rep")
    gb = jnp.concatenate([MO[0:1, :WIDTH], MO[1:2, :WIDTH], MO[2:3, :WIDTH], MO[3:4, :1024], MO[4:5, :1024], MO[7:8, :1]], axis=1)
    gh = pltpu.roll(MO[5:6, 0:1024], 1024 - 32 * k, 1)[:, 0:32]
    for kk, g, rate in (("h", gh, RATE_DENSE), ("b", gb, RATE_BIAS)):
        n = g.shape[1]
        w, m, v = adamw(*(R_["v_" + kk + q][...].reshape(1, n) for q in "wnv"), g, rate)
        for q, a in (("w", w), ("n", m), ("v", v), ("l", w.astype(BF))):
            R_["u_" + kk + q][...] = a.reshape(n)
            out(kk + q)
    rows = {"c": [("c0", 0, 16), ("c1", 16, 16), ("c2", 32, 16)], "i": [("i", 0, 32)], "m": [("m", 0, 32)]}
    for k in "imc":
        for q in "wnv":
            ld[k + q].wait()
        for n, lo, nb in rows[k]:
            L = R_["v_" + k + "w"].shape[1]
            at = slice(lo, lo + nb)
            w, m, v = adamw(R_["v_" + k + "w"][at], R_["v_" + k + "n"][at], R_["v_" + k + "v"][at], R_["g_" + n][:, 0:L], RATE_DENSE)
            R_["u_" + k + "w"][at], R_["u_" + k + "n"][at], R_["u_" + k + "v"][at], R_["u_" + k + "l"][at] = w, m, v, w.astype(BF)
        for q in "wnvl":
            out(k + q)
    row = lax.broadcasted_iota(jnp.int32, (64, 128), 0)
    lane = lax.broadcasted_iota(jnp.int32, (64, 128), 1)
    use = ((row // 2) * 128 + lane) < jnp.where(row % 2 == 0, rc[0], rc[1])
    for part in range(3):
        for n in ("tw", "tn", "tv", "gt"):
            ld[n, part].wait()

        def tab(c, at):
            q = pl.ds(pl.multiple_of(at + c * 64, 64), 64)
            w, m, v = R_["v_tw"][q], R_["v_tn"][q], R_["v_tv"][q]
            nw, nm, nv = adamw(w, m, v, R_["v_gt"][q], RATE_TABLE)
            nw = jnp.where(use, nw, w)
            R_["u_tw"][q] = nw
            R_["u_tn"][q] = jnp.where(use, nm, m)
            R_["u_tv"][q] = jnp.where(use, nv, v)
            R_["u_tl"][q] = nw.astype(BF)

        for c in range(13):
            tab(c, 832 * part)
        for q in "wnvl":
            out("t" + q, pl.ds(832 * part, 832))
    for c in outs:
        c.wait()


def update(rc, g, state):
    V, S = pltpu.VMEM, jax.ShapeDtypeStruct
    vm, sm, an = pl.BlockSpec(memory_space=pltpu.VMEM), pl.BlockSpec(memory_space=pltpu.SMEM), pl.BlockSpec(memory_space=pl.ANY)
    ins, specs = {"rc": rc}, [sm]
    for k in "tcimhb":
        for q, a in zip("wnv", state[k]):
            ins[k + q] = a
            specs.append(an)
    ins["gt"], ins["MO"] = g["gt"], g["MO"]
    specs += [an, vm]
    for n in SUMS:
        ins["g_" + n] = g["o_" + n]
        specs.append(vm)
    outs, scr = {}, {}
    for k in "tcimhb":
        for q in "wnvl":
            shape, kind = state[k][0].shape, BF if q == "l" else F32
            outs["o_" + k + q] = S(shape, kind)
            scr["u_" + k + q] = V(shape, kind)
            if q != "l":
                scr["v_" + k + q] = V(shape, kind)
    scr["v_gt"] = V((2496, 128), F32)
    outs["o_loss"] = S((1, 1), F32)
    scr["isem"] = pltpu.SemaphoreType.DMA((27,))
    scr["osem"] = pltpu.SemaphoreType.DMA((32,))
    return pl.pallas_call(
        functools.partial(update_body, list(ins), list(outs), list(scr)), name="adamw_step",
        out_shape=tuple(outs.values()), in_specs=specs, out_specs=(an,) * (len(outs) - 1) + (sm,), scratch_shapes=list(scr.values()),
        compiler_params=pltpu.CompilerParams(vmem_limit_bytes=63 << 20),
    )(*ins.values())


def tab_view(t):
    S, n, C = t.shape
    return jnp.transpose(jnp.transpose(t, (2, 0, 1)).reshape(C, S, n // 128, 128), (0, 2, 1, 3)).reshape(C * S * n // 128, 128)


def tab_unview(v, S=2, n=4096, C=39):
    return jnp.transpose(jnp.transpose(v.reshape(C, n // 128, S, 128), (0, 2, 1, 3)).reshape(C, S, n), (1, 2, 0))


def fast_shards(
    event_ids, row_counts, table_slot, dense_input, labels,
    tables, tables_m, tables_v, cross_uv, cross_m, cross_v,
    tower_in, tower_in_m, tower_in_v, tower_mid, tower_mid_m, tower_mid_v,
    head_weight, head_m, head_v, biases, biases_m, biases_v,
):
    total = float(labels.shape[0] * lax.axis_size("dp") * lax.axis_size("rep"))
    turn = lambda a: jnp.transpose(a, (0, 1, 3, 2)).reshape(48, WIDTH)
    back = lambda a: jnp.transpose(a.reshape(LAYERS, 2, 8, WIDTH), (0, 1, 3, 2))
    state = {
        "t": [tab_view(a) for a in (tables, tables_m, tables_v)],
        "c": [turn(a) for a in (cross_uv, cross_m, cross_v)],
        "i": [a.T for a in (tower_in, tower_in_m, tower_in_v)],
        "m": [a.T for a in (tower_mid, tower_mid_m, tower_mid_v)],
    }
    state["h"] = [head_weight, head_m, head_v]
    state["b"] = [biases, biases_m, biases_v]
    g = mega(total, table_slot, event_ids, state["t"][0], state["c"][0], state["i"][0], state["m"][0],
             head_weight, dense_input.T, labels, biases)
    o = update(row_counts, g, state)
    return (
        o[24].reshape(()),
        *[tab_unview(a) for a in o[0:4]],
        *[back(a) for a in o[4:8]],
        *[a.T for a in o[8:12]],
        *[a.T for a in o[12:16]],
        *o[16:24],
    )


def solution(mesh):
    placed = (
        P("dp", None),
        P("dp"),
        P(),
        P(("dp", "rep"), None),
        P(("dp", "rep")),
        P("dp", None, None),
        P("dp", None, None),
        P("dp", None, None),
        P(None, None, None, ("dp", "rep")),
        P(None, None, None, ("dp", "rep")),
        P(None, None, None, ("dp", "rep")),
        P(None, ("dp", "rep")),
        P(None, ("dp", "rep")),
        P(None, ("dp", "rep")),
        P(None, ("dp", "rep")),
        P(None, ("dp", "rep")),
        P(None, ("dp", "rep")),
        P(("dp", "rep")),
        P(("dp", "rep")),
        P(("dp", "rep")),
        P(),
        P(),
        P(),
    )
    fits = mesh.shape["dp"] == 16 and mesh.shape["rep"] == 2
    return jax.shard_map(
        fast_shards if fits else shards,
        mesh=mesh,
        in_specs=placed,
        out_specs=(
            P(),
            P("dp", None, None),
            P("dp", None, None),
            P("dp", None, None),
            P("dp", None, None),
            P(None, None, None, ("dp", "rep")),
            P(None, None, None, ("dp", "rep")),
            P(None, None, None, ("dp", "rep")),
            P(None, None, None, ("dp", "rep")),
            P(None, ("dp", "rep")),
            P(None, ("dp", "rep")),
            P(None, ("dp", "rep")),
            P(None, ("dp", "rep")),
            P(None, ("dp", "rep")),
            P(None, ("dp", "rep")),
            P(None, ("dp", "rep")),
            P(None, ("dp", "rep")),
            P(("dp", "rep")),
            P(("dp", "rep")),
            P(("dp", "rep")),
            P(("dp", "rep")),
            P(),
            P(),
            P(),
            P(),
        ),
        check_vma=False,
    )
```

```python
import functools
import math
import types

import jax
import jax.numpy as jnp
from jax import lax
from jax.experimental import pallas as pl
from jax.experimental.pallas import tpu as pltpu
from jax.sharding import PartitionSpec as P

TABLES = 26
EMB = 39
HIDDEN_SIZE = 1024
LAYERS = 3
MICRO = 3
STEP = 5
WIDTH = 1027


BETA_ONE = 0.5
BETA_TWO = 0.5
EPSILON = 1e-10
WEIGHT_DECAY = 0.01
RATE_DENSE = 0.01
RATE_BIAS = 0.05
RATE_TABLE = 0.2
HIGHEST_PRECISION = lax.Precision.HIGHEST


def adamw_update(weight, moment_one, moment_two, gradient, step_rate):
    moment_new = BETA_ONE * moment_one + (1 - BETA_ONE) * gradient
    second = BETA_TWO * moment_two + (1 - BETA_TWO) * gradient * gradient
    scaled_one = moment_new / (1 - BETA_ONE**STEP)
    scaled_two = second / (1 - BETA_TWO**STEP)
    fresh = weight - step_rate * (
        scaled_one / (jnp.sqrt(scaled_two) + EPSILON) + WEIGHT_DECAY * weight
    )
    return (fresh, moment_new, second)


def silu_slope(pre_value):
    sigmoid_value = jax.nn.sigmoid(pre_value)
    return sigmoid_value * (1.0 + pre_value * (1.0 - sigmoid_value))


def contract_rows(left_side, right_side):
    return lax.dot_general(
        left_side, right_side, (((0,), (0,)), ((), ())), preferred_element_type=jnp.float32
    )


def contract_cols(left_side, right_side):
    return lax.dot_general(
        left_side, right_side, (((1,), (1,)), ((), ())), preferred_element_type=jnp.float32
    )


def one_hot_rows(positions, row_total):
    return (positions[:, None] == jnp.arange(row_total, dtype=jnp.int32)[None, :]).astype(
        jnp.bfloat16
    )


def lookup_rows(table_piece, positions):
    count = positions.shape[0]
    block = math.gcd(count, 512)
    blocks = positions.reshape(count // block, block)

    def one_block(block_ids):
        return jnp.dot(
            one_hot_rows(block_ids, table_piece.shape[0]),
            table_piece,
            preferred_element_type=jnp.float32,
        ).astype(jnp.bfloat16)

    return lax.map(one_block, blocks).reshape(count, table_piece.shape[1])


def accumulate_rows(entry_rows, positions, row_total):
    count = positions.shape[0]
    block = math.gcd(count, 512)
    blocks = positions.reshape(count // block, block)
    entry_blocks = entry_rows.reshape(count // block, block, entry_rows.shape[1])

    def add_block(running, pair):
        block_ids, block_rows = pair
        return (running + contract_rows(one_hot_rows(block_ids, row_total), block_rows), None)

    start = jnp.zeros((row_total, entry_rows.shape[1]), jnp.float32)
    summed, unused = lax.scan(add_block, start, (blocks, entry_blocks))
    return summed


def cross_forward(anchor, carried, cross_full, layer_bias, which_layer):
    carried_low = carried.astype(jnp.bfloat16)
    project = jnp.dot(
        carried_low, cross_full[which_layer, 0], preferred_element_type=jnp.float32
    ).astype(jnp.bfloat16)
    crossed = contract_cols(project, cross_full[which_layer, 1])
    return (anchor * (crossed + layer_bias[which_layer]) + carried, (carried_low, project, crossed))


def cross_backward(anchor, grad_carried, saved_values, cross_full, layer_bias, which_layer):
    carried_low, project, crossed = saved_values
    grad_cross = grad_carried * anchor
    bias_grad = jnp.sum(grad_cross, axis=0)
    grad_cross_low = grad_cross.astype(jnp.bfloat16)
    grad_up = contract_rows(grad_cross_low, project)
    grad_project = jnp.dot(
        grad_cross_low, cross_full[which_layer, 1], preferred_element_type=jnp.float32
    ).astype(jnp.bfloat16)
    grad_down = contract_rows(carried_low, grad_project)
    grad_input = contract_cols(grad_project, cross_full[which_layer, 0]) + grad_carried
    extra_grad = grad_carried * (crossed + layer_bias[which_layer])
    return (grad_input, extra_grad, jnp.stack([grad_down, grad_up]), bias_grad)


def micro_step(gathered, biases, emb_flat, dense_rows, target, total_events):
    cross_full, tower_full, mid_full, head_full = gathered
    layer_bias = biases[: LAYERS * WIDTH].reshape(LAYERS, WIDTH)
    bias_one = biases[LAYERS * WIDTH : LAYERS * WIDTH + HIDDEN_SIZE]
    bias_two = biases[LAYERS * WIDTH + HIDDEN_SIZE : LAYERS * WIDTH + 2 * HIDDEN_SIZE]
    bias_out = biases[LAYERS * WIDTH + 2 * HIDDEN_SIZE]
    dense_low = lax.optimization_barrier(dense_rows.astype(jnp.bfloat16)).astype(jnp.float32)
    anchor = jnp.concatenate([emb_flat.astype(jnp.float32), dense_low], axis=1)
    carried = anchor
    saved_all = []
    for which_layer in range(LAYERS):
        carried, saved_values = cross_forward(anchor, carried, cross_full, layer_bias, which_layer)
        saved_all.append(saved_values)
    carried_low = carried.astype(jnp.bfloat16)
    pre_one = jnp.dot(carried_low, tower_full, preferred_element_type=jnp.float32) + bias_one
    hidden_one = jax.nn.silu(pre_one).astype(jnp.bfloat16)
    pre_two = jnp.dot(hidden_one, mid_full, preferred_element_type=jnp.float32) + bias_two
    hidden_two = jax.nn.silu(pre_two).astype(jnp.bfloat16)
    logits = jnp.dot(hidden_two, head_full, preferred_element_type=jnp.float32) + bias_out
    loss_part = jnp.sum(jax.nn.softplus(logits) - target * logits)
    grad_logits = (jax.nn.sigmoid(logits) - target) / total_events
    grad_head = jnp.dot(grad_logits, hidden_two.astype(jnp.float32), precision=HIGHEST_PRECISION)
    grad_hidden_two = grad_logits[:, None] * head_full.astype(jnp.float32)[None, :]
    grad_pre_two = (grad_hidden_two * silu_slope(pre_two)).astype(jnp.bfloat16)
    grad_mid = contract_rows(hidden_one, grad_pre_two)
    grad_hidden_one = contract_cols(grad_pre_two, mid_full)
    grad_pre_one = (grad_hidden_one * silu_slope(pre_one)).astype(jnp.bfloat16)
    grad_tower = contract_rows(carried_low, grad_pre_one)
    grad_carried = contract_cols(grad_pre_one, tower_full)
    grad_anchor = jnp.zeros_like(anchor)
    cross_grads = [None] * LAYERS
    layer_grads = [None] * LAYERS
    for which_layer in reversed(range(LAYERS)):
        grad_carried, extra_grad, grad_pair, bias_grad = cross_backward(
            anchor, grad_carried, saved_all[which_layer], cross_full, layer_bias, which_layer
        )
        grad_anchor = grad_anchor + extra_grad
        cross_grads[which_layer] = grad_pair
        layer_grads[which_layer] = bias_grad
    grad_anchor = grad_anchor + grad_carried
    grad_emb = grad_anchor[:, : TABLES * EMB].astype(jnp.bfloat16)
    bias_grads = jnp.concatenate(
        [
            jnp.stack(layer_grads).reshape(-1),
            jnp.sum(grad_pre_one.astype(jnp.float32), axis=0),
            jnp.sum(grad_pre_two.astype(jnp.float32), axis=0),
            jnp.sum(grad_logits)[None],
        ]
    )
    dense_grads = (jnp.stack(cross_grads), grad_tower, grad_mid, grad_head)
    return (loss_part, grad_emb, dense_grads, bias_grads)


def shards(
    event_ids,
    row_counts,
    table_slot,
    dense_input,
    labels,
    tables,
    tables_m,
    tables_v,
    cross_uv,
    cross_m,
    cross_v,
    tower_in,
    tower_in_m,
    tower_in_v,
    tower_mid,
    tower_mid_m,
    tower_mid_v,
    head_weight,
    head_m,
    head_v,
    biases,
    biases_m,
    biases_v,
):
    dp_count = lax.axis_size("dp")
    rep_count = lax.axis_size("rep")
    rep_index = lax.axis_index("rep")
    slot_count = tables.shape[0]
    row_total = tables.shape[1]
    device_events = labels.shape[0]
    micro_events = device_events // MICRO
    total_events = float(device_events * dp_count * rep_count)
    shard_set = (cross_uv, tower_in, tower_mid, head_weight)
    shard_low = tuple((shard_piece.astype(jnp.bfloat16) for shard_piece in shard_set))
    event_grid = event_ids.reshape(slot_count, dp_count, rep_count, MICRO, micro_events)
    own_ids = lax.dynamic_index_in_dim(event_grid, rep_index, 2, keepdims=False)
    table_low = tables.astype(jnp.bfloat16)
    selector = (
        table_slot[:, None] == jnp.arange(dp_count * slot_count, dtype=jnp.int32)[None, :]
    ).astype(jnp.bfloat16)
    loss_total = jnp.zeros((), jnp.float32)
    bias_total = jnp.zeros(biases.shape, jnp.float32)
    table_grad = jnp.zeros(tables.shape, jnp.float32)
    dense_total = None
    for micro_index in range(MICRO):
        gathered = (
            lax.all_gather(shard_low[0], ("dp", "rep"), axis=3, tiled=True),
            lax.all_gather(shard_low[1], ("dp", "rep"), axis=1, tiled=True),
            lax.all_gather(shard_low[2], ("dp", "rep"), axis=1, tiled=True),
            lax.all_gather(shard_low[3], ("dp", "rep"), axis=0, tiled=True),
        )
        micro_ids = own_ids[:, :, micro_index, :].reshape(slot_count, dp_count * micro_events)
        looked = jax.vmap(lookup_rows)(table_low, micro_ids)
        outgoing = jnp.transpose(
            looked.reshape(slot_count, dp_count, micro_events, EMB), (1, 0, 2, 3)
        )
        arrived = lax.all_to_all(outgoing, "dp", split_axis=0, concat_axis=0, tiled=True)
        by_slot = arrived.reshape(dp_count * slot_count, micro_events, EMB)
        picked = jnp.einsum(
            "ts,sec->tec", selector, by_slot, preferred_element_type=jnp.float32
        ).astype(jnp.bfloat16)
        emb_flat = jnp.transpose(picked, (1, 0, 2)).reshape(micro_events, TABLES * EMB)
        row_lo = micro_index * micro_events
        dense_rows = dense_input[row_lo : row_lo + micro_events]
        target = labels[row_lo : row_lo + micro_events].astype(jnp.float32)
        loss_part, grad_emb, dense_grads, bias_grads = micro_step(
            gathered, biases, emb_flat, dense_rows, target, total_events
        )
        loss_total = loss_total + loss_part
        bias_total = bias_total + bias_grads
        if micro_index == 0:
            dense_total = dense_grads
        else:
            dense_total = tuple(
                (running + fresh_part for running, fresh_part in zip(dense_total, dense_grads))
            )
        grad_tables = jnp.transpose(grad_emb.reshape(micro_events, TABLES, EMB), (1, 0, 2))
        slot_grads = jnp.einsum(
            "ts,tec->sec", selector, grad_tables, preferred_element_type=jnp.float32
        ).astype(jnp.bfloat16)
        returned = lax.all_to_all(
            slot_grads.reshape(dp_count, slot_count, micro_events, EMB),
            "dp",
            split_axis=0,
            concat_axis=0,
            tiled=True,
        )
        entries = jnp.transpose(returned, (1, 0, 2, 3)).reshape(
            slot_count, dp_count * micro_events, EMB
        )
        table_grad = table_grad + jax.vmap(
            lambda entry_rows, positions: accumulate_rows(entry_rows, positions, row_total)
        )(entries, micro_ids)
    dense_total = (
        lax.psum_scatter(dense_total[0], ("dp", "rep"), scatter_dimension=3, tiled=True),
        lax.psum_scatter(dense_total[1], ("dp", "rep"), scatter_dimension=1, tiled=True),
        lax.psum_scatter(dense_total[2], ("dp", "rep"), scatter_dimension=1, tiled=True),
        lax.psum_scatter(dense_total[3], ("dp", "rep"), scatter_dimension=0, tiled=True),
    )
    table_grad = lax.psum(table_grad, "rep")
    bias_total, loss_total = lax.psum((bias_total, loss_total), ("dp", "rep"))
    fresh_tab, fresh_tab_m, fresh_tab_v = adamw_update(
        tables, tables_m, tables_v, table_grad, RATE_TABLE
    )
    in_use = (jnp.arange(row_total, dtype=jnp.int32)[None, :] < row_counts[:, None])[:, :, None]
    fresh_tab = jnp.where(in_use, fresh_tab, tables)
    fresh_tab_m = jnp.where(in_use, fresh_tab_m, tables_m)
    fresh_tab_v = jnp.where(in_use, fresh_tab_v, tables_v)
    weight_set = shard_set + (biases,)
    grad_set = tuple(dense_total) + (bias_total,)
    states = (
        (cross_m, cross_v, RATE_DENSE),
        (tower_in_m, tower_in_v, RATE_DENSE),
        (tower_mid_m, tower_mid_v, RATE_DENSE),
        (head_m, head_v, RATE_DENSE),
        (biases_m, biases_v, RATE_BIAS),
    )
    results = []
    for weight, gradient, state in zip(weight_set, grad_set, states):
        fresh, moment_new, second = adamw_update(weight, state[0], state[1], gradient, state[2])
        results.append((fresh, moment_new, second, fresh.astype(jnp.bfloat16)))
    return (
        loss_total,
        fresh_tab,
        fresh_tab_m,
        fresh_tab_v,
        fresh_tab.astype(jnp.bfloat16),
        results[0][0],
        results[0][1],
        results[0][2],
        results[0][3],
        results[1][0],
        results[1][1],
        results[1][2],
        results[1][3],
        results[2][0],
        results[2][1],
        results[2][2],
        results[2][3],
        results[3][0],
        results[3][1],
        results[3][2],
        results[3][3],
        results[4][0],
        results[4][1],
        results[4][2],
        results[4][3],
    )


MESH = pl.DeviceIdType.MESH
F32 = jnp.float32
BF = jnp.bfloat16
LN = 1152
RB = 112
BIASES = 5130
CH = [(0, 256), (256, 256), (512, 256), (768, 256), (1024, 128)]
M0, M1, IN, C2, C1, C0 = range(6)
ITEMS = [
    (16, 1024, True, 0, 0),
    (16, 1024, False, 0, 16),
    (32, LN, True, 1, 0),
    (16, LN, False, 2, 0),
    (16, LN, True, 3, 0),
    (16, LN, False, 4, 0),
]
SUMS = [(32, 1024), (32, LN), (16, LN), (16, LN), (16, LN)]
A, I, U = range(3)
PARTS = [(0, 48, True), (48, 48, False), (96, 16, False)]


def nt(a, b):
    return lax.dot_general(a, b, (((1,), (1,)), ((), ())), preferred_element_type=F32)


def nn(a, b):
    return lax.dot_general(a, b, (((1,), (0,)), ((), ())), preferred_element_type=F32)


def tn(a, b):
    return lax.dot_general(a, b, (((0,), (0,)), ((), ())), preferred_element_type=F32)


def sig(v):
    return 1.0 / (1.0 + jnp.exp(-v))


def slope(v):
    s = sig(v)
    return s * (1.0 + v * (1.0 - s))


def place(k):
    rep, d = k % 2, k // 2
    return rep, d % 2, (d // 2) % 2, d // 4


def mega_body(total, names, *refs):
    B = types.SimpleNamespace(**dict(zip(names, refs)))
    buf = lambda kind, n: getattr(B, kind + str(n))
    ts, inv = B.ts, B.inv
    G, E, D, eout, tabr = B.G, B.E, B.D, B.eout, B.tabr
    xT, dx, xl, qc, pr = B.xT, B.dx, B.xl, B.qc, B.pr
    VT, UT, h1, h2 = B.VT, B.UT, B.h1, B.h2
    d0, dql, dpr, DE, M, R = B.d0, B.dql, B.dpr, B.DE, B.M, B.R
    ids_ref, tab_ref, bia = B.ids_v, B.gg, B.bia
    xr, a1, a2, d1, d2 = dx, dx, d0, h1, h2
    gt, gg_, gtc, MO = B.gt, B.gg, B.gtc, B.MO
    me = lax.axis_index("dp")
    r = lax.axis_index("rep")
    x, y, z = me % 2, (me // 2) % 2, me // 4
    dev = lambda zz, yy, xx: zz * 4 + yy * 2 + xx
    zp = [z + 1 - 2 * (z % 2), (z + 2) % 4, 3 - z]
    own = me * 2 + r
    xpeer, ypeer, core = (dev(z, y, 1 - x), r), (dev(z, 1 - y, x), r), (me, 1 - r)
    zpeer = [(dev(q, y, x), r) for q in zp]

    loads = [
        pltpu.make_async_copy(src, dst, B.lsem.at[i])
        for i, (src, dst) in enumerate(
            ((B.cr, B.cr_v), (B.ti, B.ti_v), (B.tm, B.tm_v), (B.hd, B.hd_v), (B.tab, B.gg),
             (B.ids, B.ids_v), (B.dns, B.dns_v), (B.lab, B.lab_v), (B.bi, B.bi_v)))
    ]
    for c in loads:
        c.start()
    bar = pltpu.get_barrier_semaphore()
    for i in range(1, 16):
        pl.semaphore_signal(bar, inc=1, device_id=((me + i) % 16, r), device_id_type=MESH)
    pl.semaphore_signal(bar, inc=1, device_id=core, device_id_type=MESH)

    cr, ti, tm, hd = B.cr_v, B.ti_v, B.tm_v, B.hd_v
    for c in loads[:4]:
        c.wait()
    G[own, 0:48, 0:1024] = cr[:, 0:1024].astype(BF)
    G[own, 0:48, 1024:LN] = jnp.concatenate([cr[:, 1024:1027], jnp.zeros((48, 125), F32)], axis=1).astype(BF)
    G[own, 48:80, 0:1024] = ti[:, 0:1024].astype(BF)
    G[own, 48:80, 1024:LN] = jnp.concatenate([ti[:, 1024:1027], jnp.zeros((32, 125), F32)], axis=1).astype(BF)
    G[own, 80:112, 0:1024] = tm[...].astype(BF)
    eye = lax.broadcasted_iota(jnp.int32, (32, 32), 0) == lax.broadcasted_iota(jnp.int32, (32, 32), 1)
    hcol = jnp.sum(jnp.where(eye, jnp.broadcast_to(hd[...].reshape(1, 32), (32, 32)), 0.0), axis=1, keepdims=True)
    G[own, 80:112, 1024:LN] = jnp.broadcast_to(hcol, (32, 128)).astype(BF)
    pl.semaphore_wait(bar, 16)

    cnt = [0, 0, 0]
    sends = []

    def wcopy(p, k, dst, si):
        lo, n, _ = PARTS[p]
        return pltpu.make_async_remote_copy(
            src_ref=G.at[k, pl.ds(lo, n)], dst_ref=G.at[k, pl.ds(lo, n)],
            send_sem=B.wss.at[p, si], recv_sem=B.wrs.at[p, k], device_id=dst, device_id_type=MESH)

    def wsend(p, k, dst):
        c = wcopy(p, k, dst, cnt[p])
        cnt[p] += 1
        c.start()
        sends.append(c)

    def wwait(p, k):
        wcopy(p, k, core, 0).wait_recv()

    p1 = [ypeer if p[2] else xpeer for p in PARTS]
    p2 = [xpeer if p[2] else ypeer for p in PARTS]
    key = lambda zz, yy, xx: dev(zz, yy, xx) * 2 + r
    inner = (z == 1) | (z == 2)
    zq = [zp[0], jnp.where(inner, zp[2], zp[1]), jnp.where(inner, zp[1], zp[2])]
    on_to = [zp[2], zp[0], zp[0]]
    isends = []

    def isend(p, k, zz):
        c = wcopy(p, k, (dev(zz, y, x), r), cnt[p])
        cnt[p] += 1
        isends.append(c)

        @pl.when(inner)
        def _():
            c.start()

    def f_own(p):
        wsend(p, own, (dev(zp[0], y, x), r))
        isend(p, own, zp[2])
        wsend(p, own, p1[p])
        wsend(p, own, p2[p])

    def f_core(p):
        wsend(p, own, core)

    def fwd_z(p, i):
        k = key(zq[i], y, x)
        wwait(p, k)
        isend(p, k, on_to[i])
        wsend(p, k, p1[p])
        wsend(p, k, p2[p])
        wsend(p, k, core)

    def up_down(p, k):
        if p == U:
            wsend(p, k, (dev(zp[0], y, x), r))
            isend(p, k, zp[2])

    def fwd_zl(p, i, c):
        k = key(zq[i], (y + c // 2) % 2, (x + c % 2) % 2)
        wwait(p, k)
        isend(p, k, on_to[i])
        wsend(p, k, core)

    def fwd_1(p, i):
        q = z if i < 0 else zq[i]
        k = key(q, 1 - y, x) if PARTS[p][2] else key(q, y, 1 - x)
        wwait(p, k)
        up_down(p, k)
        wsend(p, k, p2[p])
        wsend(p, k, core)

    def fwd_2(p, i, o):
        q = z if i < 0 else zq[i]
        k = key(q, (y + o) % 2, 1 - x) if PARTS[p][2] else key(q, 1 - y, (x + o) % 2)
        wwait(p, k)
        up_down(p, k)
        wsend(p, k, core)

    def core_wait(p):
        def cw(i, _):
            wwait(p, i * 2 + (1 - r))
            return 0
        lax.fori_loop(0, 16, cw, 0)

    def f_prep():
        loads[4].wait()
        loads[5].wait()
        for s in range(2):
            for j in range(32):
                g, h = j // 4, j % 4
                t = tab_ref[pl.ds(2 * j + s, 39, stride=64), :]
                tabr[s, g * 40 : (g + 1) * 40, h * 128 : (h + 1) * 128] = jnp.concatenate([t, jnp.zeros((1, 128), F32)], axis=0).astype(BF)

    def id_rows(d):
        return ids_ref[:, pl.ds(pl.multiple_of((d * 2 + r) * 384, 128), 384)]

    def one_hot(lo):
        return (lax.broadcasted_iota(jnp.int32, (512, 384), 0) == lo).astype(F32).astype(BF)

    def look(d):
        idv = id_rows(d)
        outs = []
        for s in range(2):
            ids = idv[s : s + 1]
            lo, hi = ids % 512, ids // 512
            res = nn(tabr[s], one_hot(lo))
            e = jnp.zeros((40, 384), F32)
            for g in range(8):
                e = e + jnp.where(hi == g, res[g * 40 : (g + 1) * 40], 0.0)
            outs.append(e)
        return jnp.concatenate(outs, axis=0).astype(BF)

    def ecopy(d, land):
        return pltpu.make_async_remote_copy(
            src_ref=eout.at[d], dst_ref=E.at[land], send_sem=B.ess.at[d], recv_sem=B.ers.at[land], device_id=(d, r), device_id_type=MESH)

    def dcopy(d, land):
        return pltpu.make_async_remote_copy(
            src_ref=eout.at[d], dst_ref=D.at[land], send_sem=B.dss.at[d], recv_sem=B.drs.at[land], device_id=(d, r), device_id_type=MESH)

    def nth(i):
        j, w = i // 4, i % 4
        zz = jnp.where(j == 0, zp[1], jnp.where(j == 1, zp[2], jnp.where(j == 2, zp[0], z)))
        return dev(zz, (y + w // 2) % 2, (x + w) % 2)

    def looks(a, b):
        def step(i, _):
            d = nth(i)
            eout[d] = look(d)

            @pl.when(i != 12)
            def _():
                ecopy(d, me).start()
            return 0
        lax.fori_loop(a, b, step, 0)

    x0 = lambda lo, n: xl[0, :, lo : lo + n].astype(F32)

    def f_rows():
        E[me] = eout[me]
        for n in range(32):
            slot_table = jnp.int32(TABLES)
            for t in range(TABLES):
                slot_table = jnp.where(ts[t] == n, t, slot_table)
            inv[n] = slot_table
        loads[8].wait()
        bv = B.bi_v[...].reshape(1, BIASES)
        bia[...] = jnp.zeros_like(bia)
        for i in range(3):
            bia[i : i + 1, 0:1027] = bv[:, 1027 * i : 1027 * i + 1027]
        bia[3:4, 0:1024] = bv[:, 3081:4105]
        bia[4:5, 0:1024] = bv[:, 4105:5129]
        bia[5:6, :] = jnp.broadcast_to(bv[:, 5129:5130], (1, LN))
        loads[6].wait()
        loads[7].wait()

        def ew(i, _):
            d = (me + i) % 16
            ecopy(d, d).wait()
            return 0

        lax.fori_loop(1, 16, ew, 0)
        for t in range(26):
            s = ts[t]
            blk = E[s // 2].astype(F32)
            e = jnp.where(s % 2 == 1, blk[40:80], blk[0:40])
            xT[39 * t : 39 * t + 39, :] = e[0:39]
        xT[1014:1027, :] = B.dns_v[...].astype(BF).astype(F32)
        xT[1027:LN, :] = jnp.zeros((LN - 1027, 384), F32)
        for i in range(9):
            c = slice(128 * i, 128 * i + 128)
            xl[0, :, c] = xT[c, :].T.astype(BF)

    def f_split():
        core_wait(A)
        for l in range(3):
            for lo, n in CH:
                w = G[:, 16 * l : 16 * l + 16, lo : lo + n].astype(F32).reshape(32, 2, 8, n)
                VT[l, :, lo : lo + n] = w[:, 0].reshape(256, n).astype(BF)
                UT[l, :, lo : lo + n] = w[:, 1].reshape(256, n).astype(BF)

    def f_cross():
        for l in range(3):
            pr[l] = nt(xl[l], VT[l]).astype(BF)
            for lo, n in CH:
                q = nn(pr[l], UT[l, :, lo : lo + n]) + bia[l : l + 1, lo : lo + n]
                qc[l, :, lo : lo + n] = q
                v = x0(lo, n) * q + (x0(lo, n) if l == 0 else xr[:, lo : lo + n])
                if l < 2:
                    xr[:, lo : lo + n] = v
                xl[l + 1, :, lo : lo + n] = v.astype(BF)

    def f_tower_one():
        core_wait(I)
        for n in range(4):
            c = slice(256 * n, 256 * n + 256)
            a = nt(xl[3], G[8 * n : 8 * n + 8, 48:80, :].reshape(256, LN)) + bia[3:4, c]
            a1[:, c] = a
            h1[:, c] = (a * sig(a)).astype(BF)

    def f_tower_two():
        core_wait(U)
        for n in range(4):
            c = slice(256 * n, 256 * n + 256)
            a = nt(h1[...], G[8 * n : 8 * n + 8, 80:112, 0:1024].reshape(256, 1024)) + bia[4:5, c]
            a2[:, c] = a
            h2[:, c] = (a * sig(a)).astype(BF)

    f_own(U)
    f_own(I)
    f_own(A)
    f_prep()
    looks(0, 1)
    looks(1, 2)
    fwd_1(I, -1)
    fwd_1(U, -1)
    f_core(U)
    fwd_z(I, 0)
    fwd_z(A, 0)
    fwd_z(I, 1)
    fwd_z(A, 1)
    fwd_1(A, -1)
    looks(2, 3)
    looks(3, 4)
    fwd_2(U, -1, 1)
    fwd_2(U, -1, 0)
    fwd_z(I, 2)
    fwd_1(A, 0)
    f_core(I)
    fwd_1(I, 1)
    looks(4, 5)
    looks(5, 6)
    looks(6, 7)
    fwd_z(A, 2)
    fwd_1(A, 1)
    for c in range(4):
        fwd_zl(U, 1, c)
    for c in range(4):
        fwd_zl(U, 0, c)
    fwd_2(A, 0, 0)
    fwd_2(I, -1, 0)
    looks(7, 8)
    looks(8, 9)
    fwd_1(I, 0)
    fwd_1(I, 2)
    fwd_2(I, 1, 0)
    f_core(A)
    looks(9, 10)
    for c in range(4):
        fwd_zl(U, 2, c)
    fwd_2(A, 2, 0)
    looks(10, 11)
    fwd_1(A, 2)
    fwd_2(A, 1, 0)
    fwd_2(A, -1, 0)
    fwd_2(A, 1, 1)
    looks(11, 12)
    fwd_2(I, -1, 1)
    fwd_2(I, 2, 0)
    looks(12, 13)
    looks(13, 14)
    looks(14, 15)
    fwd_2(I, 0, 1)
    fwd_2(A, -1, 1)
    fwd_2(A, 0, 1)
    looks(15, 16)
    fwd_2(I, 1, 1)
    fwd_2(A, 2, 1)
    fwd_2(I, 2, 1)
    f_split()
    fwd_2(I, 0, 0)
    f_rows()
    f_cross()
    f_tower_one()
    f_tower_two()
    hc = G[:, 80:112, 1024:LN].reshape(1024, 128)
    zl = nn(h2[...], hc) + bia[5:6, 0:128]
    yl = jnp.broadcast_to(B.lab_v[...].reshape(1, 384).astype(F32), (128, 384)).T
    lossv = jnp.maximum(zl, 0.0) + jnp.log1p(jnp.exp(-jnp.abs(zl))) - yl * zl
    dz = (sig(zl) - yl) / total
    M[...] = jnp.zeros_like(M)
    M[6:7, 0:128] = jnp.sum(lossv, axis=0, keepdims=True)
    M[7:8, 0:128] = jnp.sum(dz, axis=0, keepdims=True)
    hrow = hc.astype(F32).T[0:1]
    for n in range(8):
        c = slice(128 * n, 128 * n + 128)
        M[5:6, c] = jnp.sum(dz * h2[:, c].astype(F32), axis=0, keepdims=True)
        g = (dz * hrow[:, c] * slope(a2[:, c])).astype(BF)
        d2[:, c] = g
        M[4:5, c] = jnp.sum(g.astype(F32), axis=0, keepdims=True)

    nsem = [0]

    def go(src, dst, dst_dev):
        i = nsem[0]
        nsem[0] += 1
        c = pltpu.make_async_remote_copy(
            src_ref=src, dst_ref=dst, send_sem=B.rss.at[i], recv_sem=B.rrs.at[i], device_id=dst_dev, device_id_type=MESH)
        c.start()
        sends.append(c)
        return c

    st = {}

    def axes(n):
        return (y, x, ypeer, xpeer) if ITEMS[n][2] else (x, y, xpeer, ypeer)

    def s0(n):
        g = buf("g", n)
        st[n] = go(g.at[1 - r], buf("C", n), core)

    def s1(n):
        a, b, pa, pb = axes(n)
        st[n].wait_recv()
        g, c = buf("g", n), buf("C", n)
        st[n] = []
        for bb in (1 - b, b):
            g[r, 1 - a, bb] = (g[r, 1 - a, bb].astype(F32) + c[1 - a, bb].astype(F32)).astype(BF)
            st[n].append(go(g.at[r, 1 - a, bb], buf("P", n).at[bb], pa))

    def s2(n):
        a, b, pa, pb = axes(n)
        st[n][0].wait_recv()
        g, c, p = buf("g", n), buf("C", n), buf("P", n)
        g[r, a, 1 - b] = (g[r, a, 1 - b].astype(F32) + c[a, 1 - b].astype(F32) + p[1 - b].astype(F32)).astype(BF)
        st[n].append(go(g.at[r, a, 1 - b], buf("Q", n), pb))

    def s3(n):
        a, b, pa, pb = axes(n)
        st[n][1].wait_recv()
        st[n][2].wait_recv()
        g, c, p, q = buf("g", n), buf("C", n), buf("P", n), buf("Q", n)
        st[n] = []
        for i, zz in enumerate(zp):
            g[r, a, b, zz] = (g[r, a, b, zz].astype(F32) + c[a, b, zz].astype(F32) + p[b, zz].astype(F32) + q[zz].astype(F32)).astype(BF)
            st[n].append(go(g.at[r, a, b, zz], buf("T", n).at[i], zpeer[i]))

    writes = []

    def write(src, dst):
        c = pltpu.make_async_copy(src, dst, B.osem.at[len(writes)])
        c.start()
        writes.append(c)

    def s4(n):
        a, b, pa, pb = axes(n)
        for c in st[n]:
            c.wait_recv()
        g, c, p, q, t = buf("g", n), buf("C", n), buf("P", n), buf("Q", n), buf("T", n)
        nb, _, _, out, at = ITEMS[n]
        gradient = (
            g[r, a, b, z].astype(F32) + c[a, b, z].astype(F32) + p[b, z].astype(F32) + q[z].astype(F32)
            + (t[0].astype(F32) + t[1].astype(F32) + t[2].astype(F32)))
        buf("w", out)[at : at + nb] = gradient
        write(buf("w", out).at[pl.ds(at, nb)], buf("o", out).at[pl.ds(at, nb)])

    def parts_of(out):
        return [n for n, item in enumerate(ITEMS) if item[3] == out]

    def put(out, base, g):
        for n in parts_of(out):
            nb, _, yfirst, _, at = ITEMS[n]
            for i in range(g.shape[0] // 32):
                rep, xx, yy, zz = place(base + i)
                a, b = (yy, xx) if yfirst else (xx, yy)
                buf("g", n)[rep, a, b, zz] = g[i * 32 + at : i * 32 + at + nb].astype(BF)

    MS, MX = B.MS, B.MX

    def grad_mid():
        for n in range(4):
            put(0, 8 * n, tn(d2[:, 256 * n : 256 * n + 256], h1[...]))
        for n in parts_of(0):
            s0(n)

    def down_one():
        for n in range(4):
            c = slice(256 * n, 256 * n + 256)
            a1[:, c] = nn(d2[...], G[:, 80:112, c].reshape(1024, 256)) * slope(a1[:, c])
        for n in range(4):
            c = slice(256 * n, 256 * n + 256)
            g = a1[:, c].astype(BF)
            d1[:, c] = g
            M[3:4, c] = jnp.sum(g.astype(F32), axis=0, keepdims=True)

    def grad_in():
        for n in range(4):
            put(1, 8 * n, tn(d1[:, 256 * n : 256 * n + 256], xl[3]))
        for n in parts_of(1):
            s0(n)

    def down_x():
        for lo, n in CH:
            dx[:, lo : lo + n] = nn(d1[...], G[:, 48:80, lo : lo + n].reshape(1024, n))

    def chain(l):
        dq_ref = dql.at[l]
        for lo, n in CH:
            g = dx[:, lo : lo + n]
            dq = g * x0(lo, n)
            M[l : l + 1, lo : lo + n] = jnp.sum(dq, axis=0, keepdims=True)
            dq_ref[:, lo : lo + n] = dq.astype(BF)
            e = g * qc[l, :, lo : lo + n]
            d0[:, lo : lo + n] = e if l == 2 else d0[:, lo : lo + n] + e
        dpr[l] = nt(dq_ref[...], UT[l]).astype(BF)
        for lo, n in CH:
            v = dx[:, lo : lo + n] + nn(dpr[l], VT[l, :, lo : lo + n])
            if l:
                dx[:, lo : lo + n] = v
            else:
                d0[:, lo : lo + n] = d0[:, lo : lo + n] + v
        if l == 0:
            st[-1] = go(M, B.MC, core)

    def cross_grads(l):
        gr = buf("g", C0 - l)
        yfirst = ITEMS[C0 - l][2]
        for lo, n in CH:
            gu = tn(pr[l], dql[l, :, lo : lo + n]).reshape(32, 8, n)
            gv = tn(dpr[l], xl[l, :, lo : lo + n]).reshape(32, 8, n)
            gg = jnp.concatenate([gv, gu], axis=1).astype(BF)
            for k in range(32):
                rep, xx, yy, zz = place(k)
                a, b = (yy, xx) if yfirst else (xx, yy)
                gr[rep, a, b, zz, :, lo : lo + n] = gg[k]
        s0(C0 - l)

    def back_rows(d):
        return jnp.concatenate([DE[inv[2 * d]], DE[inv[2 * d + 1]]], axis=0).astype(BF)

    def rows_out():
        for i in range(9):
            c = slice(128 * i, 128 * i + 128)
            xT[c, :] = d0[:, c].T
        for t in range(26):
            DE[t] = jnp.concatenate([xT[39 * t : 39 * t + 39, :], jnp.zeros((1, 384), F32)], axis=0)
        DE[26] = jnp.zeros((40, 384), F32)

        def dstep(i, _):
            d = nth(i)
            eout[d] = back_rows(d)

            @pl.when(i != 12)
            def _():
                dcopy(d, me).start()
            return 0

        lax.fori_loop(0, 16, dstep, 0)
        D[me] = eout[me]

    def one_part(i, s):
        d = nth(15 - i)
        ids = id_rows(d)[s : s + 1]
        lo, hi = ids % 512, ids // 512
        e = D[d].astype(F32)[40 * s : 40 * s + 40]
        lhs = jnp.concatenate([jnp.where(hi == g, e, 0.0) for g in range(8)], axis=0).astype(BF)
        return lhs, one_hot(lo)

    def rows_in(k):
        for i in (2 * k, 2 * k + 1):
            if i != 3:
                d = nth(15 - i)
                dcopy(d, d).wait_recv()
        for s in range(2):
            u, v = one_part(2 * k, s), one_part(2 * k + 1, s)
            p = nt(jnp.concatenate([u[0], v[0]], axis=1), jnp.concatenate([u[1], v[1]], axis=1))
            R[s] = p if k == 0 else R[s] + p

    def table_sum():
        for s in range(2):
            for j in range(32):
                g, h = j // 4, j % 4
                gg_[pl.ds(2 * j + s, 39, stride=64), :] = R[s, g * 40 : g * 40 + 39, h * 128 : (h + 1) * 128]
        st[-2] = go(gg_, gtc, core)

    def table_both():
        st[-2].wait_recv()
        gtc[...] = gg_[...] + gtc[...]
        write(gtc, gt)

    def small(i):
        if i == 1:
            st[-1].wait_recv()
            MS[0] = M[...] + B.MC[...]
            st[-1] = go(MS.at[0], MX.at[0], xpeer)
        elif i == 2:
            st[-1].wait_recv()
            MS[1] = MS[0] + MX[0]
            st[-1] = go(MS.at[1], MX.at[1], ypeer)
        elif i == 3:
            st[-1].wait_recv()
            MS[2] = MS[1] + MX[1]
            st[-1] = [go(MS.at[2], MX.at[2 + j], zpeer[j]) for j in range(3)]
        else:
            for c in st[-1]:
                c.wait_recv()
            pos = [MS[2], MX[2], MX[3], MX[4]]
            u = jnp.where(z % 2 == 0, pos[0], pos[1]) + jnp.where(z % 2 == 0, pos[1], pos[0])
            v = jnp.where(z % 2 == 0, pos[2], pos[3]) + jnp.where(z % 2 == 0, pos[3], pos[2])
            B.MC[...] = jnp.where(z < 2, u, v) + jnp.where(z < 2, v, u)
            write(B.MC, MO)

    grad_mid()
    down_one()
    down_x()
    s1(M0)
    s1(M1)
    chain(2)
    cross_grads(2)
    chain(1)
    chain(0)
    cross_grads(0)
    s2(M1)
    small(1)
    rows_out()
    grad_in()
    s3(M1)
    small(2)
    s1(C2)
    s1(IN)
    cross_grads(1)
    s2(M0)
    small(3)
    s2(IN)
    s3(M0)
    s1(C0)
    s2(C2)
    s1(C1)
    s3(IN)
    rows_in(0)
    rows_in(1)
    s4(M1)
    rows_in(2)
    rows_in(3)
    rows_in(4)
    s4(M0)
    s3(C2)
    s2(C1)
    s2(C0)
    s3(C1)
    rows_in(5)
    rows_in(6)
    s3(C0)
    rows_in(7)
    s4(C2)
    table_sum()
    small(4)
    s4(C1)
    s4(IN)
    table_both()
    s4(C0)

    def dw(i, _):
        d = (me + i) % 16
        dcopy(d, d).wait_send()
        return 0

    lax.fori_loop(1, 16, dw, 0)
    for c in sends:
        c.wait_send()
    for c in writes:
        c.wait()

    @pl.when(inner)
    def _():
        for c in isends:
            c.wait_send()


def mega(total, ts, ids, tab, cr, ti, tm, hd, dns, lab, bi):
    V, S = pltpu.VMEM, jax.ShapeDtypeStruct
    vm, sm, an = pl.BlockSpec(memory_space=pltpu.VMEM), pl.BlockSpec(memory_space=pltpu.SMEM), pl.BlockSpec(memory_space=pl.ANY)
    ins = dict(ts=ts, ids=ids, tab=tab, cr=cr, ti=ti, tm=tm, hd=hd, dns=dns, lab=lab, bi=bi)
    outs = dict(gt=S((2496, 128), F32), MO=S((8, LN), F32))
    for n, shape in enumerate(SUMS):
        outs["o" + str(n)] = S(shape, F32)
    like = lambda a: V(a.shape, a.dtype)
    dma = pltpu.SemaphoreType.DMA
    scr = dict(
        ids_v=like(ids), cr_v=like(cr), ti_v=like(ti), tm_v=like(tm), hd_v=like(hd), dns_v=like(dns), lab_v=like(lab), bi_v=like(bi),
        G=V((32, RB, LN), BF), E=V((16, 80, 384), BF), D=V((16, 80, 384), BF), eout=V((16, 80, 384), BF), tabr=V((2, 320, 512), BF),
        xT=V((LN, 384), F32), dx=V((384, LN), F32), xl=V((4, 384, LN), BF), qc=V((3, 384, LN), F32), pr=V((3, 384, 256), BF),
        VT=V((3, 256, LN), BF), UT=V((3, 256, LN), BF), h1=V((384, 1024), BF), h2=V((384, 1024), BF),
        d0=V((384, LN), F32), dql=V((3, 384, LN), BF), dpr=V((3, 384, 256), BF), DE=V((27, 40, 384), F32), M=V((8, LN), F32), R=V((2, 320, 512), F32),
        MC=V((8, LN), F32), MS=V((3, 8, LN), F32), MX=V((5, 8, LN), F32), gg=V((2496, 128), F32), gtc=V((2496, 128), F32), bia=V((8, LN), F32),
        inv=pltpu.SMEM((32,), jnp.int32), lsem=dma((9,)), wss=dma((3, 40)), wrs=dma((3, 32)), ess=dma((16,)), ers=dma((16,)), dss=dma((16,)), drs=dma((16,)),
        rss=dma((64,)), rrs=dma((64,)), osem=dma((9,)))
    for n, shape in enumerate(SUMS):
        scr["w" + str(n)] = V(shape, F32)
    for n, (nb, L, *_) in enumerate(ITEMS):
        for kind, lead in (("g", (2, 2, 2, 4)), ("C", (2, 2, 4)), ("P", (2, 4)), ("Q", (4,)), ("T", (3,))):
            scr[kind + str(n)] = V(lead + (nb, L), BF)
    return pl.pallas_call(
        functools.partial(mega_body, total, list(ins) + list(outs) + list(scr)), name="train_step",
        out_shape=tuple(outs.values()), in_specs=[sm] + [an] * 9, out_specs=(an,) * len(outs),
        scratch_shapes=list(scr.values()),
        compiler_params=pltpu.CompilerParams(collective_id=0, has_side_effects=True, vmem_limit_bytes=63 << 20),
    )(*ins.values())


IC5 = 1 / (1 - 0.5**5)


def adamw(w, m, v, g, rate):
    mn = 0.5 * m + 0.5 * g
    vn = 0.5 * v + 0.5 * g * g
    return w - rate * ((mn * IC5) / (jnp.sqrt(vn * IC5) + EPSILON) + WEIGHT_DECAY * w), mn, vn


def update_body(rc, *refs):
    hbm, gt, MO, sums, refs = refs[:18], refs[18], refs[19], refs[20:25], refs[25:]
    dst, loss, vin, vg, vout, refs = refs[:24], refs[24], refs[25:43], refs[43], refs[44:68], refs[68:]
    near, isem, osem = refs[:6], refs[6], refs[7]
    n_in, n_out = [0], [0]

    def load(src, to):
        c = pltpu.make_async_copy(src, to, isem.at[n_in[0]])
        n_in[0] += 1
        c.start()
        return c

    outs = []

    def out(k, rows=None):
        for i in range(4 * k, 4 * k + 4):
            s, d = vout[i], dst[i]
            if rows is not None:
                s, d = s.at[rows], d.at[rows]
            c = pltpu.make_async_copy(s, d, osem.at[n_out[0]])
            n_out[0] += 1
            c.start()
            outs.append(c)

    span = lambda part: pl.ds(832 * part, 832)
    dense = {k: [load(hbm[3 * k + j], vin[3 * k + j]) for j in range(3)] for k in (2, 3, 1)}
    gradients = [load(a, b) for a, b in zip((*sums, MO), near)]
    sums, MO = near[:5], near[5]
    table = [[load(a.at[span(part)], b.at[span(part)]) for a, b in ((hbm[0], vin[0]), (hbm[1], vin[1]), (hbm[2], vin[2]), (gt, vg))] for part in range(3)]
    dense.update({k: [load(hbm[3 * k + j], vin[3 * k + j]) for j in range(3)] for k in (4, 5)})
    for c in gradients:
        c.wait()
    for k, rows in ((2, [(1, 0, 32)]), (3, [(0, 0, 32)]), (1, [(4, 0, 16), (3, 16, 16), (2, 32, 16)])):
        for c in dense[k]:
            c.wait()
        w_in, m_in, v_in = vin[3 * k : 3 * k + 3]
        for n, lo, nb in rows:
            at = slice(lo, lo + nb)
            w, m, v = adamw(w_in[at], m_in[at], v_in[at], sums[n][:, 0 : w_in.shape[1]], RATE_DENSE)
            for o, a in zip(vout[4 * k : 4 * k + 4], (w, m, v, w.astype(BF))):
                o[at] = a
        out(k)
    row = lax.broadcasted_iota(jnp.int32, (64, 128), 0)
    lane = lax.broadcasted_iota(jnp.int32, (64, 128), 1)
    use = ((row // 2) * 128 + lane) < jnp.where(row % 2 == 0, rc[0], rc[1])
    for part in range(3):
        for c in table[part]:
            c.wait()
        for i in range(13):
            q = pl.ds(832 * part + i * 64, 64)
            w, m, v = vin[0][q], vin[1][q], vin[2][q]
            nw, nm, nv = adamw(w, m, v, vg[q], RATE_TABLE)
            nw = jnp.where(use, nw, w)
            vout[0][q] = nw
            vout[1][q] = jnp.where(use, nm, m)
            vout[2][q] = jnp.where(use, nv, v)
            vout[3][q] = nw.astype(BF)
        out(0, span(part))
    loss[0, 0] = jnp.max(MO[6:7, 0:128])
    k = lax.axis_index("dp") * 2 + lax.axis_index("rep")
    gb = jnp.concatenate([MO[0:1, :WIDTH], MO[1:2, :WIDTH], MO[2:3, :WIDTH], MO[3:4, :1024], MO[4:5, :1024], MO[7:8, :1]], axis=1)
    gh = pltpu.roll(MO[5:6, 0:1024], 1024 - 32 * k, 1)[:, 0:32]
    for k, g, rate in ((4, gh, RATE_DENSE), (5, gb, RATE_BIAS)):
        for c in dense[k]:
            c.wait()
        n = g.shape[1]
        w, m, v = adamw(*(a[...].reshape(1, n) for a in vin[3 * k : 3 * k + 3]), g, rate)
        for o, a in zip(vout[4 * k : 4 * k + 4], (w, m, v, w.astype(BF))):
            o[...] = a.reshape(n)
        out(k)
    for c in outs:
        c.wait()


def update(rc, g, state):
    V, S = pltpu.VMEM, jax.ShapeDtypeStruct
    vm, sm, an = pl.BlockSpec(memory_space=pltpu.VMEM), pl.BlockSpec(memory_space=pltpu.SMEM), pl.BlockSpec(memory_space=pl.ANY)
    flat = [a for kind in state for a in kind]
    kinds = [S(kind[0].shape, t) for kind in state for t in (F32, F32, F32, BF)]
    dma = pltpu.SemaphoreType.DMA
    return pl.pallas_call(
        update_body, name="adamw_step", out_shape=tuple(kinds) + (S((1, 1), F32),),
        in_specs=[sm] + [an] * 25, out_specs=(an,) * 24 + (sm,),
        scratch_shapes=[V(a.shape, F32) for a in flat] + [V((2496, 128), F32)] + [V(a.shape, a.dtype) for a in kinds] + [V(shape, F32) for shape in SUMS] + [V((8, LN), F32), dma((33,)), dma((32,))],
        compiler_params=pltpu.CompilerParams(vmem_limit_bytes=63 << 20),
    )(rc, *flat, *g)


def tab_view(t):
    S, n, C = t.shape
    return jnp.transpose(jnp.transpose(t, (2, 0, 1)).reshape(C, S, n // 128, 128), (0, 2, 1, 3)).reshape(C * S * n // 128, 128)


def tab_unview(v, S=2, n=4096, C=39):
    return jnp.transpose(jnp.transpose(v.reshape(C, n // 128, S, 128), (0, 2, 1, 3)).reshape(C, S, n), (1, 2, 0))


def fast_shards(
    event_ids, row_counts, table_slot, dense_input, labels,
    tables, tables_m, tables_v, cross_uv, cross_m, cross_v,
    tower_in, tower_in_m, tower_in_v, tower_mid, tower_mid_m, tower_mid_v,
    head_weight, head_m, head_v, biases, biases_m, biases_v,
):
    total = float(labels.shape[0] * lax.axis_size("dp") * lax.axis_size("rep"))
    turn = lambda a: jnp.transpose(a, (0, 1, 3, 2)).reshape(48, WIDTH)
    back = lambda a: jnp.transpose(a.reshape(LAYERS, 2, 8, WIDTH), (0, 1, 3, 2))
    state = [
        [tab_view(a) for a in (tables, tables_m, tables_v)],
        [turn(a) for a in (cross_uv, cross_m, cross_v)],
        [a.T for a in (tower_in, tower_in_m, tower_in_v)],
        [a.T for a in (tower_mid, tower_mid_m, tower_mid_v)],
        [head_weight, head_m, head_v],
        [biases, biases_m, biases_v],
    ]
    g = mega(total, table_slot, event_ids, *(kind[0] for kind in state[:5]), dense_input.T, labels, biases)
    o = update(row_counts, g, state)
    return (
        o[24].reshape(()),
        *[tab_unview(a) for a in o[0:4]],
        *[back(a) for a in o[4:8]],
        *[a.T for a in o[8:12]],
        *[a.T for a in o[12:16]],
        *o[16:24],
    )


def solution(mesh):
    placed = (
        P("dp", None),
        P("dp"),
        P(),
        P(("dp", "rep"), None),
        P(("dp", "rep")),
        P("dp", None, None),
        P("dp", None, None),
        P("dp", None, None),
        P(None, None, None, ("dp", "rep")),
        P(None, None, None, ("dp", "rep")),
        P(None, None, None, ("dp", "rep")),
        P(None, ("dp", "rep")),
        P(None, ("dp", "rep")),
        P(None, ("dp", "rep")),
        P(None, ("dp", "rep")),
        P(None, ("dp", "rep")),
        P(None, ("dp", "rep")),
        P(("dp", "rep")),
        P(("dp", "rep")),
        P(("dp", "rep")),
        P(),
        P(),
        P(),
    )
    fits = mesh.shape["dp"] == 16 and mesh.shape["rep"] == 2
    return jax.shard_map(
        fast_shards if fits else shards,
        mesh=mesh,
        in_specs=placed,
        out_specs=(
            P(),
            P("dp", None, None),
            P("dp", None, None),
            P("dp", None, None),
            P("dp", None, None),
            P(None, None, None, ("dp", "rep")),
            P(None, None, None, ("dp", "rep")),
            P(None, None, None, ("dp", "rep")),
            P(None, None, None, ("dp", "rep")),
            P(None, ("dp", "rep")),
            P(None, ("dp", "rep")),
            P(None, ("dp", "rep")),
            P(None, ("dp", "rep")),
            P(None, ("dp", "rep")),
            P(None, ("dp", "rep")),
            P(None, ("dp", "rep")),
            P(None, ("dp", "rep")),
            P(("dp", "rep")),
            P(("dp", "rep")),
            P(("dp", "rep")),
            P(("dp", "rep")),
            P(),
            P(),
            P(),
            P(),
        ),
        check_vma=False,
    )
```

```python
import functools
import math
import types

import jax
import jax.numpy as jnp
from jax import lax
from jax.experimental import pallas as pl
from jax.experimental.pallas import tpu as pltpu
from jax.sharding import PartitionSpec as P

TABLES = 26
EMB = 39
HIDDEN_SIZE = 1024
LAYERS = 3
MICRO = 3
STEP = 5
WIDTH = 1027


BETA_ONE = 0.5
BETA_TWO = 0.5
EPSILON = 1e-10
WEIGHT_DECAY = 0.01
RATE_DENSE = 0.01
RATE_BIAS = 0.05
RATE_TABLE = 0.2
HIGHEST_PRECISION = lax.Precision.HIGHEST


def adamw_update(weight, moment_one, moment_two, gradient, step_rate):
    moment_new = BETA_ONE * moment_one + (1 - BETA_ONE) * gradient
    second = BETA_TWO * moment_two + (1 - BETA_TWO) * gradient * gradient
    scaled_one = moment_new / (1 - BETA_ONE**STEP)
    scaled_two = second / (1 - BETA_TWO**STEP)
    fresh = weight - step_rate * (
        scaled_one / (jnp.sqrt(scaled_two) + EPSILON) + WEIGHT_DECAY * weight
    )
    return (fresh, moment_new, second)


def silu_slope(pre_value):
    sigmoid_value = jax.nn.sigmoid(pre_value)
    return sigmoid_value * (1.0 + pre_value * (1.0 - sigmoid_value))


def contract_rows(left_side, right_side):
    return lax.dot_general(
        left_side, right_side, (((0,), (0,)), ((), ())), preferred_element_type=jnp.float32
    )


def contract_cols(left_side, right_side):
    return lax.dot_general(
        left_side, right_side, (((1,), (1,)), ((), ())), preferred_element_type=jnp.float32
    )


def one_hot_rows(positions, row_total):
    return (positions[:, None] == jnp.arange(row_total, dtype=jnp.int32)[None, :]).astype(
        jnp.bfloat16
    )


def lookup_rows(table_piece, positions):
    count = positions.shape[0]
    block = math.gcd(count, 512)
    blocks = positions.reshape(count // block, block)

    def one_block(block_ids):
        return jnp.dot(
            one_hot_rows(block_ids, table_piece.shape[0]),
            table_piece,
            preferred_element_type=jnp.float32,
        ).astype(jnp.bfloat16)

    return lax.map(one_block, blocks).reshape(count, table_piece.shape[1])


def accumulate_rows(entry_rows, positions, row_total):
    count = positions.shape[0]
    block = math.gcd(count, 512)
    blocks = positions.reshape(count // block, block)
    entry_blocks = entry_rows.reshape(count // block, block, entry_rows.shape[1])

    def add_block(running, pair):
        block_ids, block_rows = pair
        return (running + contract_rows(one_hot_rows(block_ids, row_total), block_rows), None)

    start = jnp.zeros((row_total, entry_rows.shape[1]), jnp.float32)
    summed, unused = lax.scan(add_block, start, (blocks, entry_blocks))
    return summed


def cross_forward(anchor, carried, cross_full, layer_bias, which_layer):
    carried_low = carried.astype(jnp.bfloat16)
    project = jnp.dot(
        carried_low, cross_full[which_layer, 0], preferred_element_type=jnp.float32
    ).astype(jnp.bfloat16)
    crossed = contract_cols(project, cross_full[which_layer, 1])
    return (anchor * (crossed + layer_bias[which_layer]) + carried, (carried_low, project, crossed))


def cross_backward(anchor, grad_carried, saved_values, cross_full, layer_bias, which_layer):
    carried_low, project, crossed = saved_values
    grad_cross = grad_carried * anchor
    bias_grad = jnp.sum(grad_cross, axis=0)
    grad_cross_low = grad_cross.astype(jnp.bfloat16)
    grad_up = contract_rows(grad_cross_low, project)
    grad_project = jnp.dot(
        grad_cross_low, cross_full[which_layer, 1], preferred_element_type=jnp.float32
    ).astype(jnp.bfloat16)
    grad_down = contract_rows(carried_low, grad_project)
    grad_input = contract_cols(grad_project, cross_full[which_layer, 0]) + grad_carried
    extra_grad = grad_carried * (crossed + layer_bias[which_layer])
    return (grad_input, extra_grad, jnp.stack([grad_down, grad_up]), bias_grad)


def micro_step(gathered, biases, emb_flat, dense_rows, target, total_events):
    cross_full, tower_full, mid_full, head_full = gathered
    layer_bias = biases[: LAYERS * WIDTH].reshape(LAYERS, WIDTH)
    bias_one = biases[LAYERS * WIDTH : LAYERS * WIDTH + HIDDEN_SIZE]
    bias_two = biases[LAYERS * WIDTH + HIDDEN_SIZE : LAYERS * WIDTH + 2 * HIDDEN_SIZE]
    bias_out = biases[LAYERS * WIDTH + 2 * HIDDEN_SIZE]
    dense_low = lax.optimization_barrier(dense_rows.astype(jnp.bfloat16)).astype(jnp.float32)
    anchor = jnp.concatenate([emb_flat.astype(jnp.float32), dense_low], axis=1)
    carried = anchor
    saved_all = []
    for which_layer in range(LAYERS):
        carried, saved_values = cross_forward(anchor, carried, cross_full, layer_bias, which_layer)
        saved_all.append(saved_values)
    carried_low = carried.astype(jnp.bfloat16)
    pre_one = jnp.dot(carried_low, tower_full, preferred_element_type=jnp.float32) + bias_one
    hidden_one = jax.nn.silu(pre_one).astype(jnp.bfloat16)
    pre_two = jnp.dot(hidden_one, mid_full, preferred_element_type=jnp.float32) + bias_two
    hidden_two = jax.nn.silu(pre_two).astype(jnp.bfloat16)
    logits = jnp.dot(hidden_two, head_full, preferred_element_type=jnp.float32) + bias_out
    loss_part = jnp.sum(jax.nn.softplus(logits) - target * logits)
    grad_logits = (jax.nn.sigmoid(logits) - target) / total_events
    grad_head = jnp.dot(grad_logits, hidden_two.astype(jnp.float32), precision=HIGHEST_PRECISION)
    grad_hidden_two = grad_logits[:, None] * head_full.astype(jnp.float32)[None, :]
    grad_pre_two = (grad_hidden_two * silu_slope(pre_two)).astype(jnp.bfloat16)
    grad_mid = contract_rows(hidden_one, grad_pre_two)
    grad_hidden_one = contract_cols(grad_pre_two, mid_full)
    grad_pre_one = (grad_hidden_one * silu_slope(pre_one)).astype(jnp.bfloat16)
    grad_tower = contract_rows(carried_low, grad_pre_one)
    grad_carried = contract_cols(grad_pre_one, tower_full)
    grad_anchor = jnp.zeros_like(anchor)
    cross_grads = [None] * LAYERS
    layer_grads = [None] * LAYERS
    for which_layer in reversed(range(LAYERS)):
        grad_carried, extra_grad, grad_pair, bias_grad = cross_backward(
            anchor, grad_carried, saved_all[which_layer], cross_full, layer_bias, which_layer
        )
        grad_anchor = grad_anchor + extra_grad
        cross_grads[which_layer] = grad_pair
        layer_grads[which_layer] = bias_grad
    grad_anchor = grad_anchor + grad_carried
    grad_emb = grad_anchor[:, : TABLES * EMB].astype(jnp.bfloat16)
    bias_grads = jnp.concatenate(
        [
            jnp.stack(layer_grads).reshape(-1),
            jnp.sum(grad_pre_one.astype(jnp.float32), axis=0),
            jnp.sum(grad_pre_two.astype(jnp.float32), axis=0),
            jnp.sum(grad_logits)[None],
        ]
    )
    dense_grads = (jnp.stack(cross_grads), grad_tower, grad_mid, grad_head)
    return (loss_part, grad_emb, dense_grads, bias_grads)


def shards(
    event_ids,
    row_counts,
    table_slot,
    dense_input,
    labels,
    tables,
    tables_m,
    tables_v,
    cross_uv,
    cross_m,
    cross_v,
    tower_in,
    tower_in_m,
    tower_in_v,
    tower_mid,
    tower_mid_m,
    tower_mid_v,
    head_weight,
    head_m,
    head_v,
    biases,
    biases_m,
    biases_v,
):
    dp_count = lax.axis_size("dp")
    rep_count = lax.axis_size("rep")
    rep_index = lax.axis_index("rep")
    slot_count = tables.shape[0]
    row_total = tables.shape[1]
    device_events = labels.shape[0]
    micro_events = device_events // MICRO
    total_events = float(device_events * dp_count * rep_count)
    shard_set = (cross_uv, tower_in, tower_mid, head_weight)
    shard_low = tuple((shard_piece.astype(jnp.bfloat16) for shard_piece in shard_set))
    event_grid = event_ids.reshape(slot_count, dp_count, rep_count, MICRO, micro_events)
    own_ids = lax.dynamic_index_in_dim(event_grid, rep_index, 2, keepdims=False)
    table_low = tables.astype(jnp.bfloat16)
    selector = (
        table_slot[:, None] == jnp.arange(dp_count * slot_count, dtype=jnp.int32)[None, :]
    ).astype(jnp.bfloat16)
    loss_total = jnp.zeros((), jnp.float32)
    bias_total = jnp.zeros(biases.shape, jnp.float32)
    table_grad = jnp.zeros(tables.shape, jnp.float32)
    dense_total = None
    for micro_index in range(MICRO):
        gathered = (
            lax.all_gather(shard_low[0], ("dp", "rep"), axis=3, tiled=True),
            lax.all_gather(shard_low[1], ("dp", "rep"), axis=1, tiled=True),
            lax.all_gather(shard_low[2], ("dp", "rep"), axis=1, tiled=True),
            lax.all_gather(shard_low[3], ("dp", "rep"), axis=0, tiled=True),
        )
        micro_ids = own_ids[:, :, micro_index, :].reshape(slot_count, dp_count * micro_events)
        looked = jax.vmap(lookup_rows)(table_low, micro_ids)
        outgoing = jnp.transpose(
            looked.reshape(slot_count, dp_count, micro_events, EMB), (1, 0, 2, 3)
        )
        arrived = lax.all_to_all(outgoing, "dp", split_axis=0, concat_axis=0, tiled=True)
        by_slot = arrived.reshape(dp_count * slot_count, micro_events, EMB)
        picked = jnp.einsum(
            "ts,sec->tec", selector, by_slot, preferred_element_type=jnp.float32
        ).astype(jnp.bfloat16)
        emb_flat = jnp.transpose(picked, (1, 0, 2)).reshape(micro_events, TABLES * EMB)
        row_lo = micro_index * micro_events
        dense_rows = dense_input[row_lo : row_lo + micro_events]
        target = labels[row_lo : row_lo + micro_events].astype(jnp.float32)
        loss_part, grad_emb, dense_grads, bias_grads = micro_step(
            gathered, biases, emb_flat, dense_rows, target, total_events
        )
        loss_total = loss_total + loss_part
        bias_total = bias_total + bias_grads
        if micro_index == 0:
            dense_total = dense_grads
        else:
            dense_total = tuple(
                (running + fresh_part for running, fresh_part in zip(dense_total, dense_grads))
            )
        grad_tables = jnp.transpose(grad_emb.reshape(micro_events, TABLES, EMB), (1, 0, 2))
        slot_grads = jnp.einsum(
            "ts,tec->sec", selector, grad_tables, preferred_element_type=jnp.float32
        ).astype(jnp.bfloat16)
        returned = lax.all_to_all(
            slot_grads.reshape(dp_count, slot_count, micro_events, EMB),
            "dp",
            split_axis=0,
            concat_axis=0,
            tiled=True,
        )
        entries = jnp.transpose(returned, (1, 0, 2, 3)).reshape(
            slot_count, dp_count * micro_events, EMB
        )
        table_grad = table_grad + jax.vmap(
            lambda entry_rows, positions: accumulate_rows(entry_rows, positions, row_total)
        )(entries, micro_ids)
    dense_total = (
        lax.psum_scatter(dense_total[0], ("dp", "rep"), scatter_dimension=3, tiled=True),
        lax.psum_scatter(dense_total[1], ("dp", "rep"), scatter_dimension=1, tiled=True),
        lax.psum_scatter(dense_total[2], ("dp", "rep"), scatter_dimension=1, tiled=True),
        lax.psum_scatter(dense_total[3], ("dp", "rep"), scatter_dimension=0, tiled=True),
    )
    table_grad = lax.psum(table_grad, "rep")
    bias_total, loss_total = lax.psum((bias_total, loss_total), ("dp", "rep"))
    fresh_tab, fresh_tab_m, fresh_tab_v = adamw_update(
        tables, tables_m, tables_v, table_grad, RATE_TABLE
    )
    in_use = (jnp.arange(row_total, dtype=jnp.int32)[None, :] < row_counts[:, None])[:, :, None]
    fresh_tab = jnp.where(in_use, fresh_tab, tables)
    fresh_tab_m = jnp.where(in_use, fresh_tab_m, tables_m)
    fresh_tab_v = jnp.where(in_use, fresh_tab_v, tables_v)
    weight_set = shard_set + (biases,)
    grad_set = tuple(dense_total) + (bias_total,)
    states = (
        (cross_m, cross_v, RATE_DENSE),
        (tower_in_m, tower_in_v, RATE_DENSE),
        (tower_mid_m, tower_mid_v, RATE_DENSE),
        (head_m, head_v, RATE_DENSE),
        (biases_m, biases_v, RATE_BIAS),
    )
    results = []
    for weight, gradient, state in zip(weight_set, grad_set, states):
        fresh, moment_new, second = adamw_update(weight, state[0], state[1], gradient, state[2])
        results.append((fresh, moment_new, second, fresh.astype(jnp.bfloat16)))
    return (
        loss_total,
        fresh_tab,
        fresh_tab_m,
        fresh_tab_v,
        fresh_tab.astype(jnp.bfloat16),
        results[0][0],
        results[0][1],
        results[0][2],
        results[0][3],
        results[1][0],
        results[1][1],
        results[1][2],
        results[1][3],
        results[2][0],
        results[2][1],
        results[2][2],
        results[2][3],
        results[3][0],
        results[3][1],
        results[3][2],
        results[3][3],
        results[4][0],
        results[4][1],
        results[4][2],
        results[4][3],
    )


MESH = pl.DeviceIdType.MESH
F32 = jnp.float32
BF = jnp.bfloat16
LN = 1152
RB = 112
BIASES = 5130
CH = [(0, 256), (256, 256), (512, 256), (768, 256), (1024, 128)]
M0, M1, IN, C2, C1, C0 = range(6)
ITEMS = [
    (16, 1024, True, 0, 0),
    (16, 1024, False, 0, 16),
    (32, 1024, True, 1, 0),
    (16, LN, True, 2, 0),
    (16, LN, False, 3, 0),
    (16, LN, False, 4, 0),
]
SUMS = [(32, 1024), (32, 1024), (16, LN), (16, LN), (16, LN)]
A, I, U = range(3)
PARTS = [(0, 48, True), (48, 48, False), (96, 16, False)]


def nt(a, b):
    return lax.dot_general(a, b, (((1,), (1,)), ((), ())), preferred_element_type=F32)


def nn(a, b):
    return lax.dot_general(a, b, (((1,), (0,)), ((), ())), preferred_element_type=F32)


def tn(a, b):
    return lax.dot_general(a, b, (((0,), (0,)), ((), ())), preferred_element_type=F32)


def sig(v):
    return 1.0 / (1.0 + jnp.exp(-v))


def slope(v):
    s = sig(v)
    return s * (1.0 + v * (1.0 - s))


def place(k):
    rep, d = k % 2, k // 2
    return rep, d % 2, (d // 2) % 2, d // 4


def mega_body(total, names, *refs):
    B = types.SimpleNamespace(**dict(zip(names, refs)))
    buf = lambda kind, n: getattr(B, kind + str(n))
    ts, inv = B.ts, B.inv
    G, E, D, eout, tabr = B.G, B.E, B.D, B.eout, B.tabr
    xT, dx, xl, qc, pr = B.xT, B.dx, B.xl, B.qc, B.pr
    VT, UT, h1, h2 = B.VT, B.UT, B.h1, B.h2
    d0, dql, dpr, DE, M, R = B.d0, B.dql, B.dpr, B.DE, B.M, B.R
    ids_ref, tab_ref, bia = B.ids_v, B.gg, B.bia
    xr, a1, a2, d1, d2 = dx, dx, d0, h1, h2
    gt, gg_, gtc, MO = B.gt, B.gg, B.gtc, B.MO
    me = lax.axis_index("dp")
    r = lax.axis_index("rep")
    x, y, z = me % 2, (me // 2) % 2, me // 4
    dev = lambda zz, yy, xx: zz * 4 + yy * 2 + xx
    zp = [z + 1 - 2 * (z % 2), (z + 2) % 4, 3 - z]
    own = me * 2 + r
    xpeer, ypeer, core = (dev(z, y, 1 - x), r), (dev(z, 1 - y, x), r), (me, 1 - r)
    zpeer = [(dev(q, y, x), r) for q in zp]

    loads = [
        pltpu.make_async_copy(src, dst, B.lsem.at[i])
        for i, (src, dst) in enumerate(
            ((B.cr, B.cr_v), (B.ti, B.ti_v), (B.tm, B.tm_v), (B.hd, B.hd_v), (B.tab, B.gg),
             (B.ids, B.ids_v), (B.dns, B.dns_v), (B.lab, B.lab_v), (B.bi, B.bi_v)))
    ]
    for c in loads:
        c.start()
    bar = pltpu.get_barrier_semaphore()
    for i in range(1, 16):
        pl.semaphore_signal(bar, inc=1, device_id=((me + i) % 16, r), device_id_type=MESH)
    pl.semaphore_signal(bar, inc=1, device_id=core, device_id_type=MESH)

    cr, ti, tm, hd = B.cr_v, B.ti_v, B.tm_v, B.hd_v
    for c in loads[:4]:
        c.wait()
    G[own, 0:48, 0:1024] = cr[:, 0:1024].astype(BF)
    G[own, 48:80, 0:1024] = ti[:, 0:1024].astype(BF)
    G[own, 80:112, 0:1024] = tm[...].astype(BF)
    eye = lax.broadcasted_iota(jnp.int32, (32, 32), 0) == lax.broadcasted_iota(jnp.int32, (32, 32), 1)
    hcol = jnp.sum(jnp.where(eye, jnp.broadcast_to(hd[...].reshape(1, 32), (32, 32)), 0.0), axis=1, keepdims=True)
    more = jnp.concatenate([jnp.zeros((32, 3), F32), ti[:, 1024:1027], jnp.zeros((32, 58), F32), jnp.broadcast_to(hcol, (32, 64))], axis=1)
    ends = jnp.concatenate([cr[:, 1024:1027], jnp.zeros((48, 125), F32)], axis=1) + jnp.concatenate([more, jnp.zeros((16, 128), F32)], axis=0)
    G[own, 0:48, 1024:LN] = ends.astype(BF)
    pl.semaphore_wait(bar, 16)

    cnt = [0, 0, 0]
    sends = []

    def wcopy(p, k, dst, si):
        lo, n, _ = PARTS[p]
        at = (k, pl.ds(lo, n), pl.ds(0, LN if p == A else 1024))
        return pltpu.make_async_remote_copy(
            src_ref=G.at[at], dst_ref=G.at[at],
            send_sem=B.wss.at[p, si], recv_sem=B.wrs.at[p, k], device_id=dst, device_id_type=MESH)

    def wsend(p, k, dst):
        c = wcopy(p, k, dst, cnt[p])
        cnt[p] += 1
        c.start()
        sends.append(c)

    def wwait(p, k):
        wcopy(p, k, core, 0).wait_recv()

    p1 = [ypeer if p[2] else xpeer for p in PARTS]
    p2 = [xpeer if p[2] else ypeer for p in PARTS]
    key = lambda zz, yy, xx: dev(zz, yy, xx) * 2 + r
    inner = (z == 1) | (z == 2)
    zq = [zp[0], jnp.where(inner, zp[2], zp[1]), jnp.where(inner, zp[1], zp[2])]
    on_to = [zp[2], zp[0], zp[0]]
    isends = []

    def isend(p, k, zz):
        c = wcopy(p, k, (dev(zz, y, x), r), cnt[p])
        cnt[p] += 1
        isends.append(c)

        @pl.when(inner)
        def _():
            c.start()

    def f_own(p):
        wsend(p, own, (dev(zp[0], y, x), r))
        isend(p, own, zp[2])
        wsend(p, own, p1[p])
        wsend(p, own, p2[p])

    def f_core(p):
        wsend(p, own, core)

    def fwd_z(p, i):
        k = key(zq[i], y, x)
        wwait(p, k)
        isend(p, k, on_to[i])
        wsend(p, k, p1[p])
        wsend(p, k, p2[p])
        wsend(p, k, core)

    def up_down(p, k):
        if p == U:
            wsend(p, k, (dev(zp[0], y, x), r))
            isend(p, k, zp[2])

    def fwd_zl(p, i, c):
        k = key(zq[i], (y + c // 2) % 2, (x + c % 2) % 2)
        wwait(p, k)
        isend(p, k, on_to[i])
        wsend(p, k, core)

    def fwd_1(p, i):
        q = z if i < 0 else zq[i]
        k = key(q, 1 - y, x) if PARTS[p][2] else key(q, y, 1 - x)
        wwait(p, k)
        up_down(p, k)
        wsend(p, k, p2[p])
        wsend(p, k, core)

    def fwd_2(p, i, o):
        q = z if i < 0 else zq[i]
        k = key(q, (y + o) % 2, 1 - x) if PARTS[p][2] else key(q, 1 - y, (x + o) % 2)
        wwait(p, k)
        up_down(p, k)
        wsend(p, k, core)

    def core_wait(p):
        def cw(i, _):
            wwait(p, i * 2 + (1 - r))
            return 0
        lax.fori_loop(0, 16, cw, 0)

    def f_prep():
        loads[4].wait()
        loads[5].wait()
        for s in range(2):
            for j in range(32):
                g, h = j // 4, j % 4
                t = tab_ref[pl.ds(2 * j + s, 39, stride=64), :]
                tabr[s, g * 40 : (g + 1) * 40, h * 128 : (h + 1) * 128] = jnp.concatenate([t, jnp.zeros((1, 128), F32)], axis=0).astype(BF)

    def id_rows(d):
        return ids_ref[:, pl.ds(pl.multiple_of((d * 2 + r) * 384, 128), 384)]

    def one_hot(lo):
        return (lax.broadcasted_iota(jnp.int32, (512, 384), 0) == lo).astype(F32).astype(BF)

    def look(d):
        idv = id_rows(d)
        outs = []
        for s in range(2):
            ids = idv[s : s + 1]
            lo, hi = ids % 512, ids // 512
            res = nn(tabr[s], one_hot(lo))
            e = jnp.zeros((40, 384), F32)
            for g in range(8):
                e = e + jnp.where(hi == g, res[g * 40 : (g + 1) * 40], 0.0)
            outs.append(e)
        return jnp.concatenate(outs, axis=0).astype(BF)

    def ecopy(d, land):
        return pltpu.make_async_remote_copy(
            src_ref=eout.at[d], dst_ref=E.at[land], send_sem=B.ess.at[d], recv_sem=B.ers.at[land], device_id=(d, r), device_id_type=MESH)

    def dcopy(d, land):
        return pltpu.make_async_remote_copy(
            src_ref=eout.at[d], dst_ref=D.at[land], send_sem=B.dss.at[d], recv_sem=B.drs.at[land], device_id=(d, r), device_id_type=MESH)

    def nth(i):
        j, w = i // 4, i % 4
        zz = jnp.where(j == 0, zp[1], jnp.where(j == 1, zp[2], jnp.where(j == 2, zp[0], z)))
        return dev(zz, (y + w // 2) % 2, (x + w) % 2)

    def looks(a, b):
        def step(i, _):
            d = nth(i)
            eout[d] = look(d)

            @pl.when(i != 12)
            def _():
                ecopy(d, me).start()
            return 0
        lax.fori_loop(a, b, step, 0)

    x0 = lambda lo, n: xl[0, :, lo : lo + n].astype(F32)

    def f_rows():
        E[me] = eout[me]
        for n in range(32):
            slot_table = jnp.int32(TABLES)
            for t in range(TABLES):
                slot_table = jnp.where(ts[t] == n, t, slot_table)
            inv[n] = slot_table
        loads[8].wait()
        bv = B.bi_v[...].reshape(1, BIASES)
        bia[...] = jnp.zeros_like(bia)
        for i in range(3):
            bia[i : i + 1, 0:1027] = bv[:, 1027 * i : 1027 * i + 1027]
        bia[3:4, 0:1024] = bv[:, 3081:4105]
        bia[4:5, 0:1024] = bv[:, 4105:5129]
        bia[5:6, :] = jnp.broadcast_to(bv[:, 5129:5130], (1, LN))
        loads[6].wait()
        loads[7].wait()

        def ew(i, _):
            d = (me + i) % 16
            ecopy(d, d).wait()
            return 0

        lax.fori_loop(1, 16, ew, 0)
        for t in range(26):
            s = ts[t]
            blk = E[s // 2].astype(F32)
            e = jnp.where(s % 2 == 1, blk[40:80], blk[0:40])
            xT[39 * t : 39 * t + 39, :] = e[0:39]
        xT[1014:1027, :] = B.dns_v[...].astype(BF).astype(F32)
        xT[1027:LN, :] = jnp.zeros((LN - 1027, 384), F32)
        for i in range(9):
            c = slice(128 * i, 128 * i + 128)
            xl[0, :, c] = xT[c, :].T.astype(BF)

    def f_split():
        core_wait(A)
        for l in range(3):
            for lo, n in CH:
                w = G[:, 16 * l : 16 * l + 16, lo : lo + n].astype(F32).reshape(32, 2, 8, n)
                if lo == 1024:
                    w = jnp.where(lax.broadcasted_iota(jnp.int32, w.shape, 3) < 3, w, 0.0)
                VT[l, :, lo : lo + n] = w[:, 0].reshape(256, n).astype(BF)
                UT[l, :, lo : lo + n] = w[:, 1].reshape(256, n).astype(BF)

    def f_cross():
        for l in range(3):
            pr[l] = nt(xl[l], VT[l]).astype(BF)
            for lo, n in CH:
                q = nn(pr[l], UT[l, :, lo : lo + n]) + bia[l : l + 1, lo : lo + n]
                qc[l, :, lo : lo + n] = q
                v = x0(lo, n) * q + (x0(lo, n) if l == 0 else xr[:, lo : lo + n])
                if l < 2:
                    xr[:, lo : lo + n] = v
                xl[l + 1, :, lo : lo + n] = v.astype(BF)

    def f_tower_one():
        core_wait(I)
        x_end = pltpu.roll(xl[3, :, 1024:LN].astype(F32), 3, 1).astype(BF)
        for n in range(4):
            c = slice(256 * n, 256 * n + 256)
            a = nt(xl[3, :, 0:1024], G[8 * n : 8 * n + 8, 48:80, 0:1024].reshape(256, 1024)) + bia[3:4, c]
            a = a + nt(x_end, G[8 * n : 8 * n + 8, 0:32, 1024:LN].reshape(256, 128))
            a1[:, c] = a
            h1[:, c] = (a * sig(a)).astype(BF)

    def f_tower_two():
        core_wait(U)
        for n in range(4):
            c = slice(256 * n, 256 * n + 256)
            a = nt(h1[...], G[8 * n : 8 * n + 8, 80:112, 0:1024].reshape(256, 1024)) + bia[4:5, c]
            a2[:, c] = a
            h2[:, c] = (a * sig(a)).astype(BF)

    f_own(I)
    f_prep()
    looks(0, 1)
    f_core(U)
    f_own(A)
    f_own(U)
    fwd_z(I, 0)
    looks(1, 2)
    fwd_1(A, -1)
    fwd_2(U, -1, 0)
    fwd_1(I, -1)
    fwd_z(A, 0)
    fwd_1(U, -1)
    fwd_z(I, 1)
    fwd_z(A, 1)
    fwd_1(A, 0)
    fwd_2(I, -1, 0)
    fwd_1(I, 0)
    fwd_z(I, 2)
    fwd_2(A, -1, 1)
    looks(2, 3)
    fwd_2(A, 0, 0)
    f_core(I)
    f_core(A)
    fwd_2(U, -1, 1)
    fwd_2(I, -1, 1)
    looks(3, 4)
    fwd_z(A, 2)
    looks(4, 5)
    looks(5, 6)
    for c in range(4):
        fwd_zl(U, 1, c)
    looks(6, 7)
    fwd_2(A, 0, 1)
    fwd_1(I, 2)
    fwd_1(A, 1)
    fwd_2(I, 1, 0)
    fwd_2(A, 1, 0)
    fwd_1(I, 1)
    looks(7, 8)
    looks(8, 9)
    fwd_2(A, -1, 0)
    fwd_2(A, 2, 0)
    fwd_1(A, 2)
    looks(9, 10)
    for c in range(4):
        fwd_zl(U, 0, c)
    fwd_2(I, 0, 0)
    looks(10, 11)
    looks(11, 12)
    looks(12, 13)
    looks(13, 14)
    fwd_2(I, 2, 1)
    fwd_2(A, 1, 1)
    looks(14, 15)
    fwd_2(I, 0, 1)
    looks(15, 16)
    fwd_2(I, 2, 0)
    for c in range(4):
        fwd_zl(U, 2, c)
    fwd_2(A, 2, 1)
    fwd_2(I, 1, 1)
    f_split()
    f_rows()
    f_cross()
    f_tower_one()
    f_tower_two()
    hc = G[:, 0:32, 1024:LN].reshape(1024, 128)
    zl = nn(h2[...], hc)
    zl = jnp.where(lax.broadcasted_iota(jnp.int32, zl.shape, 1) < 64, pltpu.roll(zl, 64, 1), zl) + bia[5:6, 0:128]
    yl = jnp.broadcast_to(B.lab_v[...].reshape(1, 384).astype(F32), (128, 384)).T
    lossv = jnp.maximum(zl, 0.0) + jnp.log1p(jnp.exp(-jnp.abs(zl))) - yl * zl
    dz = (sig(zl) - yl) / total
    M[...] = jnp.zeros_like(M)
    M[6:7, 0:128] = jnp.sum(lossv, axis=0, keepdims=True)
    M[7:8, 0:128] = jnp.sum(dz, axis=0, keepdims=True)
    hrow = hc.astype(F32).T[64:65]
    for n in range(8):
        c = slice(128 * n, 128 * n + 128)
        M[5:6, c] = jnp.sum(dz * h2[:, c].astype(F32), axis=0, keepdims=True)
        g = (dz * hrow[:, c] * slope(a2[:, c])).astype(BF)
        d2[:, c] = g
        M[4:5, c] = jnp.sum(g.astype(F32), axis=0, keepdims=True)

    nsem = [0]

    def go(src, dst, dst_dev):
        i = nsem[0]
        nsem[0] += 1
        c = pltpu.make_async_remote_copy(
            src_ref=src, dst_ref=dst, send_sem=B.rss.at[i], recv_sem=B.rrs.at[i], device_id=dst_dev, device_id_type=MESH)
        c.start()
        sends.append(c)
        return c

    st = {}

    def axes(n):
        return (y, x, ypeer, xpeer) if ITEMS[n][2] else (x, y, xpeer, ypeer)

    def s0(n):
        g = buf("g", n)
        st[n] = go(g.at[1 - r], buf("C", n), core)

    def s1(n):
        a, b, pa, pb = axes(n)
        st[n].wait_recv()
        g, c = buf("g", n), buf("C", n)
        st[n] = []
        for bb in (1 - b, b):
            g[r, 1 - a, bb] = (g[r, 1 - a, bb].astype(F32) + c[1 - a, bb].astype(F32)).astype(BF)
            st[n].append(go(g.at[r, 1 - a, bb], buf("P", n).at[bb], pa))

    def s2(n):
        a, b, pa, pb = axes(n)
        st[n][0].wait_recv()
        g, c, p = buf("g", n), buf("C", n), buf("P", n)
        g[r, a, 1 - b] = (g[r, a, 1 - b].astype(F32) + c[a, 1 - b].astype(F32) + p[1 - b].astype(F32)).astype(BF)
        st[n].append(go(g.at[r, a, 1 - b], buf("Q", n), pb))

    def s3(n):
        a, b, pa, pb = axes(n)
        st[n][1].wait_recv()
        st[n][2].wait_recv()
        g, c, p, q = buf("g", n), buf("C", n), buf("P", n), buf("Q", n)
        st[n] = []
        for i, zz in enumerate(zp):
            g[r, a, b, zz] = (g[r, a, b, zz].astype(F32) + c[a, b, zz].astype(F32) + p[b, zz].astype(F32) + q[zz].astype(F32)).astype(BF)
            st[n].append(go(g.at[r, a, b, zz], buf("T", n).at[i], zpeer[i]))

    writes = []

    def write(src, dst):
        c = pltpu.make_async_copy(src, dst, B.osem.at[len(writes)])
        c.start()
        writes.append(c)

    def s4(n):
        a, b, pa, pb = axes(n)
        for c in st[n]:
            c.wait_recv()
        g, c, p, q, t = buf("g", n), buf("C", n), buf("P", n), buf("Q", n), buf("T", n)
        nb, _, _, out, at = ITEMS[n]
        gradient = (
            g[r, a, b, z].astype(F32) + c[a, b, z].astype(F32) + p[b, z].astype(F32) + q[z].astype(F32)
            + (t[0].astype(F32) + t[1].astype(F32) + t[2].astype(F32)))
        buf("w", out)[at : at + nb] = gradient
        write(buf("w", out).at[pl.ds(at, nb)], buf("o", out).at[pl.ds(at, nb)])

    def parts_of(out):
        return [n for n, item in enumerate(ITEMS) if item[3] == out]

    def put(out, base, g):
        for n in parts_of(out):
            nb, _, yfirst, _, at = ITEMS[n]
            for i in range(g.shape[0] // 32):
                rep, xx, yy, zz = place(base + i)
                a, b = (yy, xx) if yfirst else (xx, yy)
                buf("g", n)[rep, a, b, zz] = g[i * 32 + at : i * 32 + at + nb].astype(BF)

    MS, MX = B.MS, B.MX

    def grad_mid():
        for n in range(4):
            put(0, 8 * n, tn(d2[:, 256 * n : 256 * n + 256], h1[...]))
        for n in parts_of(0):
            s0(n)

    def down_one():
        for n in range(4):
            c = slice(256 * n, 256 * n + 256)
            a1[:, c] = nn(d2[...], G[:, 80:112, c].reshape(1024, 256)) * slope(a1[:, c])
        for n in range(4):
            c = slice(256 * n, 256 * n + 256)
            g = a1[:, c].astype(BF)
            d1[:, c] = g
            M[3:4, c] = jnp.sum(g.astype(F32), axis=0, keepdims=True)

    def grad_in():
        for n in range(4):
            g = d1[:, 256 * n : 256 * n + 256]
            put(1, 8 * n, tn(g, xl[3, :, 0:1024]))
            B.TE[256 * n : 256 * n + 256] = pltpu.roll(tn(g, xl[3, :, 1024:LN]), 3, 1)
        for n in parts_of(1):
            s0(n)

    def down_x():
        for lo, n in CH[:4]:
            dx[:, lo : lo + n] = nn(d1[...], G[:, 48:80, lo : lo + n].reshape(1024, n))
        g = pltpu.roll(nn(d1[...], G[:, 0:32, 1024:LN].reshape(1024, 128)), 125, 1)
        dx[:, 1024:LN] = jnp.where(lax.broadcasted_iota(jnp.int32, g.shape, 1) < 3, g, 0.0)

    def chain(l):
        dq_ref = dql.at[l]
        for lo, n in CH:
            g = dx[:, lo : lo + n]
            dq = g * x0(lo, n)
            M[l : l + 1, lo : lo + n] = jnp.sum(dq, axis=0, keepdims=True)
            dq_ref[:, lo : lo + n] = dq.astype(BF)
            e = g * qc[l, :, lo : lo + n]
            d0[:, lo : lo + n] = e if l == 2 else d0[:, lo : lo + n] + e
        dpr[l] = nt(dq_ref[...], UT[l]).astype(BF)
        for lo, n in CH:
            v = dx[:, lo : lo + n] + nn(dpr[l], VT[l, :, lo : lo + n])
            if l:
                dx[:, lo : lo + n] = v
            else:
                d0[:, lo : lo + n] = d0[:, lo : lo + n] + v
        if l == 0:
            st[-1] = go(M, B.MC, core)

    def cross_grads(l):
        gr = buf("g", C0 - l)
        yfirst = ITEMS[C0 - l][2]
        for lo, n in CH:
            gu = tn(pr[l], dql[l, :, lo : lo + n]).reshape(32, 8, n)
            gv = tn(dpr[l], xl[l, :, lo : lo + n]).reshape(32, 8, n)
            gg = jnp.concatenate([gv, gu], axis=1)
            if lo == 1024 and l:
                te = B.TE[...].reshape(32, 32, 128)
                gg = gg + (te[:, 0:16] if l == 2 else te[:, 16:32])
            gg = gg.astype(BF)
            for k in range(32):
                rep, xx, yy, zz = place(k)
                a, b = (yy, xx) if yfirst else (xx, yy)
                gr[rep, a, b, zz, :, lo : lo + n] = gg[k]
        s0(C0 - l)

    def back_rows(d):
        return jnp.concatenate([DE[inv[2 * d]], DE[inv[2 * d + 1]]], axis=0).astype(BF)

    def rows_out():
        for i in range(9):
            c = slice(128 * i, 128 * i + 128)
            xT[c, :] = d0[:, c].T
        for t in range(26):
            DE[t] = jnp.concatenate([xT[39 * t : 39 * t + 39, :], jnp.zeros((1, 384), F32)], axis=0)
        DE[26] = jnp.zeros((40, 384), F32)

        def dstep(i, _):
            d = nth(i)
            eout[d] = back_rows(d)

            @pl.when(i != 12)
            def _():
                dcopy(d, me).start()
            return 0

        lax.fori_loop(0, 16, dstep, 0)
        D[me] = eout[me]

    def one_part(i, s):
        d = nth(15 - i)
        ids = id_rows(d)[s : s + 1]
        lo, hi = ids % 512, ids // 512
        e = D[d].astype(F32)[40 * s : 40 * s + 40]
        lhs = jnp.concatenate([jnp.where(hi == g, e, 0.0) for g in range(8)], axis=0).astype(BF)
        return lhs, one_hot(lo)

    def rows_in(k):
        for i in (2 * k, 2 * k + 1):
            if i != 3:
                d = nth(15 - i)
                dcopy(d, d).wait_recv()
        for s in range(2):
            u, v = one_part(2 * k, s), one_part(2 * k + 1, s)
            p = nt(jnp.concatenate([u[0], v[0]], axis=1), jnp.concatenate([u[1], v[1]], axis=1))
            R[s] = p if k == 0 else R[s] + p

    def table_sum():
        for s in range(2):
            for j in range(32):
                g, h = j // 4, j % 4
                gg_[pl.ds(2 * j + s, 39, stride=64), :] = R[s, g * 40 : g * 40 + 39, h * 128 : (h + 1) * 128]
        st[-2] = go(gg_, gtc, core)

    def table_both():
        st[-2].wait_recv()
        gtc[...] = gg_[...] + gtc[...]
        write(gtc, gt)

    def small(i):
        if i == 1:
            st[-1].wait_recv()
            MS[0] = M[...] + B.MC[...]
            st[-1] = go(MS.at[0], MX.at[0], xpeer)
        elif i == 2:
            st[-1].wait_recv()
            MS[1] = MS[0] + MX[0]
            st[-1] = go(MS.at[1], MX.at[1], ypeer)
        elif i == 3:
            st[-1].wait_recv()
            MS[2] = MS[1] + MX[1]
            st[-1] = [go(MS.at[2], MX.at[2 + j], zpeer[j]) for j in range(3)]
        else:
            for c in st[-1]:
                c.wait_recv()
            pos = [MS[2], MX[2], MX[3], MX[4]]
            u = jnp.where(z % 2 == 0, pos[0], pos[1]) + jnp.where(z % 2 == 0, pos[1], pos[0])
            v = jnp.where(z % 2 == 0, pos[2], pos[3]) + jnp.where(z % 2 == 0, pos[3], pos[2])
            B.MC[...] = jnp.where(z < 2, u, v) + jnp.where(z < 2, v, u)
            write(B.MC, MO)

    grad_mid()
    down_one()
    down_x()
    s1(M0)
    s1(M1)
    chain(2)
    grad_in()
    chain(1)
    chain(0)
    s2(M1)
    s2(M0)
    rows_out()
    cross_grads(0)
    s1(IN)
    cross_grads(2)
    rows_in(0)
    cross_grads(1)
    small(1)
    s1(C0)
    rows_in(1)
    rows_in(2)
    s3(M1)
    small(2)
    rows_in(3)
    rows_in(4)
    s2(IN)
    rows_in(5)
    s2(C0)
    s1(C2)
    rows_in(6)
    s3(M0)
    rows_in(7)
    s4(M1)
    s1(C1)
    small(3)
    s3(IN)
    s2(C1)
    table_sum()
    s2(C2)
    small(4)
    s3(C0)
    s3(C2)
    table_both()
    s4(IN)
    s3(C1)
    s4(C0)
    s4(M0)
    s4(C2)
    s4(C1)

    def dw(i, _):
        d = (me + i) % 16
        dcopy(d, d).wait_send()
        return 0

    lax.fori_loop(1, 16, dw, 0)
    for c in sends:
        c.wait_send()
    for c in writes:
        c.wait()

    @pl.when(inner)
    def _():
        for c in isends:
            c.wait_send()


def mega(total, ts, ids, tab, cr, ti, tm, hd, dns, lab, bi):
    V, S = pltpu.VMEM, jax.ShapeDtypeStruct
    vm, sm, an = pl.BlockSpec(memory_space=pltpu.VMEM), pl.BlockSpec(memory_space=pltpu.SMEM), pl.BlockSpec(memory_space=pl.ANY)
    ins = dict(ts=ts, ids=ids, tab=tab, cr=cr, ti=ti, tm=tm, hd=hd, dns=dns, lab=lab, bi=bi)
    outs = dict(gt=S((2496, 128), F32), MO=S((8, LN), F32))
    for n, shape in enumerate(SUMS):
        outs["o" + str(n)] = S(shape, F32)
    like = lambda a: V(a.shape, a.dtype)
    dma = pltpu.SemaphoreType.DMA
    scr = dict(
        ids_v=like(ids), cr_v=like(cr), ti_v=like(ti), tm_v=like(tm), hd_v=like(hd), dns_v=like(dns), lab_v=like(lab), bi_v=like(bi),
        G=V((32, RB, LN), BF), E=V((16, 80, 384), BF), D=V((16, 80, 384), BF), eout=V((16, 80, 384), BF), tabr=V((2, 320, 512), BF),
        xT=V((LN, 384), F32), dx=V((384, LN), F32), xl=V((4, 384, LN), BF), qc=V((3, 384, LN), F32), pr=V((3, 384, 256), BF),
        VT=V((3, 256, LN), BF), UT=V((3, 256, LN), BF), h1=V((384, 1024), BF), h2=V((384, 1024), BF),
        d0=V((384, LN), F32), dql=V((3, 384, LN), BF), dpr=V((3, 384, 256), BF), DE=V((27, 40, 384), F32), M=V((8, LN), F32), R=V((2, 320, 512), F32),
        MC=V((8, LN), F32), MS=V((3, 8, LN), F32), MX=V((5, 8, LN), F32), TE=V((1024, 128), F32), gg=V((2496, 128), F32), gtc=V((2496, 128), F32), bia=V((8, LN), F32),
        inv=pltpu.SMEM((32,), jnp.int32), lsem=dma((9,)), wss=dma((3, 40)), wrs=dma((3, 32)), ess=dma((16,)), ers=dma((16,)), dss=dma((16,)), drs=dma((16,)),
        rss=dma((64,)), rrs=dma((64,)), osem=dma((9,)))
    for n, shape in enumerate(SUMS):
        scr["w" + str(n)] = V(shape, F32)
    for n, (nb, L, *_) in enumerate(ITEMS):
        for kind, lead in (("g", (2, 2, 2, 4)), ("C", (2, 2, 4)), ("P", (2, 4)), ("Q", (4,)), ("T", (3,))):
            scr[kind + str(n)] = V(lead + (nb, L), BF)
    return pl.pallas_call(
        functools.partial(mega_body, total, list(ins) + list(outs) + list(scr)), name="train_step",
        out_shape=tuple(outs.values()), in_specs=[sm] + [an] * 9, out_specs=(an,) * len(outs),
        scratch_shapes=list(scr.values()),
        compiler_params=pltpu.CompilerParams(collective_id=0, has_side_effects=True, vmem_limit_bytes=63 << 20),
    )(*ins.values())


IC5 = 1 / (1 - 0.5**5)


def adamw(w, m, v, g, rate):
    mn = 0.5 * m + 0.5 * g
    vn = 0.5 * v + 0.5 * g * g
    return w - rate * ((mn * IC5) / (jnp.sqrt(vn * IC5) + EPSILON) + WEIGHT_DECAY * w), mn, vn


def update_body(rc, *refs):
    hbm, gt, MO, sums, refs = refs[:18], refs[18], refs[19], refs[20:25], refs[25:]
    dst, loss, vin, vg, vout, refs = refs[:24], refs[24], refs[25:43], refs[43], refs[44:68], refs[68:]
    near, isem, osem = refs[:6], refs[6], refs[7]
    n_in, n_out = [0], [0]

    def load(src, to):
        c = pltpu.make_async_copy(src, to, isem.at[n_in[0]])
        n_in[0] += 1
        c.start()
        return c

    outs = []

    def out(k, rows=None):
        for i in range(4 * k, 4 * k + 4):
            s, d = vout[i], dst[i]
            if rows is not None:
                s, d = s.at[rows], d.at[rows]
            c = pltpu.make_async_copy(s, d, osem.at[n_out[0]])
            n_out[0] += 1
            c.start()
            outs.append(c)

    span = lambda part: pl.ds(832 * part, 832)
    dense = {k: [load(hbm[3 * k + j], vin[3 * k + j]) for j in range(3)] for k in (2, 3, 1)}
    gradients = [load(a, b) for a, b in zip((*sums, MO), near)]
    sums, MO = near[:5], near[5]
    table = [[load(a.at[span(part)], b.at[span(part)]) for a, b in ((hbm[0], vin[0]), (hbm[1], vin[1]), (hbm[2], vin[2]), (gt, vg))] for part in range(3)]
    dense.update({k: [load(hbm[3 * k + j], vin[3 * k + j]) for j in range(3)] for k in (4, 5)})
    for c in gradients:
        c.wait()
    for k, rows in ((2, [(1, 0, 32)]), (3, [(0, 0, 32)]), (1, [(4, 0, 16), (3, 16, 16), (2, 32, 16)])):
        for c in dense[k]:
            c.wait()
        w_in, m_in, v_in = vin[3 * k : 3 * k + 3]
        for n, lo, nb in rows:
            g = sums[n][:, 0 : w_in.shape[1]]
            if k == 2:
                ends = [a[:, WIDTH : WIDTH + 3] for a in (sums[2], sums[3])]
                g = jnp.concatenate([g, jnp.concatenate(ends, axis=0)], axis=1)
            at = slice(lo, lo + nb)
            w, m, v = adamw(w_in[at], m_in[at], v_in[at], g, RATE_DENSE)
            for o, a in zip(vout[4 * k : 4 * k + 4], (w, m, v, w.astype(BF))):
                o[at] = a
        out(k)
    row = lax.broadcasted_iota(jnp.int32, (64, 128), 0)
    lane = lax.broadcasted_iota(jnp.int32, (64, 128), 1)
    use = ((row // 2) * 128 + lane) < jnp.where(row % 2 == 0, rc[0], rc[1])
    for part in range(3):
        for c in table[part]:
            c.wait()
        for i in range(13):
            q = pl.ds(832 * part + i * 64, 64)
            w, m, v = vin[0][q], vin[1][q], vin[2][q]
            nw, nm, nv = adamw(w, m, v, vg[q], RATE_TABLE)
            nw = jnp.where(use, nw, w)
            vout[0][q] = nw
            vout[1][q] = jnp.where(use, nm, m)
            vout[2][q] = jnp.where(use, nv, v)
            vout[3][q] = nw.astype(BF)
        out(0, span(part))
    loss[0, 0] = jnp.max(MO[6:7, 0:128])
    k = lax.axis_index("dp") * 2 + lax.axis_index("rep")
    gb = jnp.concatenate([MO[0:1, :WIDTH], MO[1:2, :WIDTH], MO[2:3, :WIDTH], MO[3:4, :1024], MO[4:5, :1024], MO[7:8, :1]], axis=1)
    gh = pltpu.roll(MO[5:6, 0:1024], 1024 - 32 * k, 1)[:, 0:32]
    for k, g, rate in ((4, gh, RATE_DENSE), (5, gb, RATE_BIAS)):
        for c in dense[k]:
            c.wait()
        n = g.shape[1]
        w, m, v = adamw(*(a[...].reshape(1, n) for a in vin[3 * k : 3 * k + 3]), g, rate)
        for o, a in zip(vout[4 * k : 4 * k + 4], (w, m, v, w.astype(BF))):
            o[...] = a.reshape(n)
        out(k)
    for c in outs:
        c.wait()


def update(rc, g, state):
    V, S = pltpu.VMEM, jax.ShapeDtypeStruct
    vm, sm, an = pl.BlockSpec(memory_space=pltpu.VMEM), pl.BlockSpec(memory_space=pltpu.SMEM), pl.BlockSpec(memory_space=pl.ANY)
    flat = [a for kind in state for a in kind]
    kinds = [S(kind[0].shape, t) for kind in state for t in (F32, F32, F32, BF)]
    dma = pltpu.SemaphoreType.DMA
    return pl.pallas_call(
        update_body, name="adamw_step", out_shape=tuple(kinds) + (S((1, 1), F32),),
        in_specs=[sm] + [an] * 25, out_specs=(an,) * 24 + (sm,),
        scratch_shapes=[V(a.shape, F32) for a in flat] + [V((2496, 128), F32)] + [V(a.shape, a.dtype) for a in kinds] + [V(shape, F32) for shape in SUMS] + [V((8, LN), F32), dma((33,)), dma((32,))],
        compiler_params=pltpu.CompilerParams(vmem_limit_bytes=63 << 20),
    )(rc, *flat, *g)


def tab_view(t):
    S, n, C = t.shape
    return jnp.transpose(jnp.transpose(t, (2, 0, 1)).reshape(C, S, n // 128, 128), (0, 2, 1, 3)).reshape(C * S * n // 128, 128)


def tab_unview(v, S=2, n=4096, C=39):
    return jnp.transpose(jnp.transpose(v.reshape(C, n // 128, S, 128), (0, 2, 1, 3)).reshape(C, S, n), (1, 2, 0))


def fast_shards(
    event_ids, row_counts, table_slot, dense_input, labels,
    tables, tables_m, tables_v, cross_uv, cross_m, cross_v,
    tower_in, tower_in_m, tower_in_v, tower_mid, tower_mid_m, tower_mid_v,
    head_weight, head_m, head_v, biases, biases_m, biases_v,
):
    total = float(labels.shape[0] * lax.axis_size("dp") * lax.axis_size("rep"))
    turn = lambda a: jnp.transpose(a, (0, 1, 3, 2)).reshape(48, WIDTH)
    back = lambda a: jnp.transpose(a.reshape(LAYERS, 2, 8, WIDTH), (0, 1, 3, 2))
    state = [
        [tab_view(a) for a in (tables, tables_m, tables_v)],
        [turn(a) for a in (cross_uv, cross_m, cross_v)],
        [a.T for a in (tower_in, tower_in_m, tower_in_v)],
        [a.T for a in (tower_mid, tower_mid_m, tower_mid_v)],
        [head_weight, head_m, head_v],
        [biases, biases_m, biases_v],
    ]
    g = mega(total, table_slot, event_ids, *(kind[0] for kind in state[:5]), dense_input.T, labels, biases)
    o = update(row_counts, g, state)
    return (
        o[24].reshape(()),
        *[tab_unview(a) for a in o[0:4]],
        *[back(a) for a in o[4:8]],
        *[a.T for a in o[8:12]],
        *[a.T for a in o[12:16]],
        *o[16:24],
    )


def solution(mesh):
    placed = (
        P("dp", None),
        P("dp"),
        P(),
        P(("dp", "rep"), None),
        P(("dp", "rep")),
        P("dp", None, None),
        P("dp", None, None),
        P("dp", None, None),
        P(None, None, None, ("dp", "rep")),
        P(None, None, None, ("dp", "rep")),
        P(None, None, None, ("dp", "rep")),
        P(None, ("dp", "rep")),
        P(None, ("dp", "rep")),
        P(None, ("dp", "rep")),
        P(None, ("dp", "rep")),
        P(None, ("dp", "rep")),
        P(None, ("dp", "rep")),
        P(("dp", "rep")),
        P(("dp", "rep")),
        P(("dp", "rep")),
        P(),
        P(),
        P(),
    )
    fits = mesh.shape["dp"] == 16 and mesh.shape["rep"] == 2
    return jax.shard_map(
        fast_shards if fits else shards,
        mesh=mesh,
        in_specs=placed,
        out_specs=(
            P(),
            P("dp", None, None),
            P("dp", None, None),
            P("dp", None, None),
            P("dp", None, None),
            P(None, None, None, ("dp", "rep")),
            P(None, None, None, ("dp", "rep")),
            P(None, None, None, ("dp", "rep")),
            P(None, None, None, ("dp", "rep")),
            P(None, ("dp", "rep")),
            P(None, ("dp", "rep")),
            P(None, ("dp", "rep")),
            P(None, ("dp", "rep")),
            P(None, ("dp", "rep")),
            P(None, ("dp", "rep")),
            P(None, ("dp", "rep")),
            P(None, ("dp", "rep")),
            P(("dp", "rep")),
            P(("dp", "rep")),
            P(("dp", "rep")),
            P(("dp", "rep")),
            P(),
            P(),
            P(),
            P(),
        ),
        check_vma=False,
    )
```

```python
import functools
import math
import types

import jax
import jax.numpy as jnp
from jax import lax
from jax.experimental import pallas as pl
from jax.experimental.pallas import tpu as pltpu
from jax.sharding import PartitionSpec as P

TABLES = 26
EMB = 39
HIDDEN_SIZE = 1024
LAYERS = 3
MICRO = 3
STEP = 5
WIDTH = 1027


BETA_ONE = 0.5
BETA_TWO = 0.5
EPSILON = 1e-10
WEIGHT_DECAY = 0.01
RATE_DENSE = 0.01
RATE_BIAS = 0.05
RATE_TABLE = 0.2
HIGHEST_PRECISION = lax.Precision.HIGHEST


def adamw_update(weight, moment_one, moment_two, gradient, step_rate):
    moment_new = BETA_ONE * moment_one + (1 - BETA_ONE) * gradient
    second = BETA_TWO * moment_two + (1 - BETA_TWO) * gradient * gradient
    scaled_one = moment_new / (1 - BETA_ONE**STEP)
    scaled_two = second / (1 - BETA_TWO**STEP)
    fresh = weight - step_rate * (
        scaled_one / (jnp.sqrt(scaled_two) + EPSILON) + WEIGHT_DECAY * weight
    )
    return (fresh, moment_new, second)


def silu_slope(pre_value):
    sigmoid_value = jax.nn.sigmoid(pre_value)
    return sigmoid_value * (1.0 + pre_value * (1.0 - sigmoid_value))


def contract_rows(left_side, right_side):
    return lax.dot_general(
        left_side, right_side, (((0,), (0,)), ((), ())), preferred_element_type=jnp.float32
    )


def contract_cols(left_side, right_side):
    return lax.dot_general(
        left_side, right_side, (((1,), (1,)), ((), ())), preferred_element_type=jnp.float32
    )


def one_hot_rows(positions, row_total):
    return (positions[:, None] == jnp.arange(row_total, dtype=jnp.int32)[None, :]).astype(
        jnp.bfloat16
    )


def lookup_rows(table_piece, positions):
    count = positions.shape[0]
    block = math.gcd(count, 512)
    blocks = positions.reshape(count // block, block)

    def one_block(block_ids):
        return jnp.dot(
            one_hot_rows(block_ids, table_piece.shape[0]),
            table_piece,
            preferred_element_type=jnp.float32,
        ).astype(jnp.bfloat16)

    return lax.map(one_block, blocks).reshape(count, table_piece.shape[1])


def accumulate_rows(entry_rows, positions, row_total):
    count = positions.shape[0]
    block = math.gcd(count, 512)
    blocks = positions.reshape(count // block, block)
    entry_blocks = entry_rows.reshape(count // block, block, entry_rows.shape[1])

    def add_block(running, pair):
        block_ids, block_rows = pair
        return (running + contract_rows(one_hot_rows(block_ids, row_total), block_rows), None)

    start = jnp.zeros((row_total, entry_rows.shape[1]), jnp.float32)
    summed, unused = lax.scan(add_block, start, (blocks, entry_blocks))
    return summed


def cross_forward(anchor, carried, cross_full, layer_bias, which_layer):
    carried_low = carried.astype(jnp.bfloat16)
    project = jnp.dot(
        carried_low, cross_full[which_layer, 0], preferred_element_type=jnp.float32
    ).astype(jnp.bfloat16)
    crossed = contract_cols(project, cross_full[which_layer, 1])
    return (anchor * (crossed + layer_bias[which_layer]) + carried, (carried_low, project, crossed))


def cross_backward(anchor, grad_carried, saved_values, cross_full, layer_bias, which_layer):
    carried_low, project, crossed = saved_values
    grad_cross = grad_carried * anchor
    bias_grad = jnp.sum(grad_cross, axis=0)
    grad_cross_low = grad_cross.astype(jnp.bfloat16)
    grad_up = contract_rows(grad_cross_low, project)
    grad_project = jnp.dot(
        grad_cross_low, cross_full[which_layer, 1], preferred_element_type=jnp.float32
    ).astype(jnp.bfloat16)
    grad_down = contract_rows(carried_low, grad_project)
    grad_input = contract_cols(grad_project, cross_full[which_layer, 0]) + grad_carried
    extra_grad = grad_carried * (crossed + layer_bias[which_layer])
    return (grad_input, extra_grad, jnp.stack([grad_down, grad_up]), bias_grad)


def micro_step(gathered, biases, emb_flat, dense_rows, target, total_events):
    cross_full, tower_full, mid_full, head_full = gathered
    layer_bias = biases[: LAYERS * WIDTH].reshape(LAYERS, WIDTH)
    bias_one = biases[LAYERS * WIDTH : LAYERS * WIDTH + HIDDEN_SIZE]
    bias_two = biases[LAYERS * WIDTH + HIDDEN_SIZE : LAYERS * WIDTH + 2 * HIDDEN_SIZE]
    bias_out = biases[LAYERS * WIDTH + 2 * HIDDEN_SIZE]
    dense_low = lax.optimization_barrier(dense_rows.astype(jnp.bfloat16)).astype(jnp.float32)
    anchor = jnp.concatenate([emb_flat.astype(jnp.float32), dense_low], axis=1)
    carried = anchor
    saved_all = []
    for which_layer in range(LAYERS):
        carried, saved_values = cross_forward(anchor, carried, cross_full, layer_bias, which_layer)
        saved_all.append(saved_values)
    carried_low = carried.astype(jnp.bfloat16)
    pre_one = jnp.dot(carried_low, tower_full, preferred_element_type=jnp.float32) + bias_one
    hidden_one = jax.nn.silu(pre_one).astype(jnp.bfloat16)
    pre_two = jnp.dot(hidden_one, mid_full, preferred_element_type=jnp.float32) + bias_two
    hidden_two = jax.nn.silu(pre_two).astype(jnp.bfloat16)
    logits = jnp.dot(hidden_two, head_full, preferred_element_type=jnp.float32) + bias_out
    loss_part = jnp.sum(jax.nn.softplus(logits) - target * logits)
    grad_logits = (jax.nn.sigmoid(logits) - target) / total_events
    grad_head = jnp.dot(grad_logits, hidden_two.astype(jnp.float32), precision=HIGHEST_PRECISION)
    grad_hidden_two = grad_logits[:, None] * head_full.astype(jnp.float32)[None, :]
    grad_pre_two = (grad_hidden_two * silu_slope(pre_two)).astype(jnp.bfloat16)
    grad_mid = contract_rows(hidden_one, grad_pre_two)
    grad_hidden_one = contract_cols(grad_pre_two, mid_full)
    grad_pre_one = (grad_hidden_one * silu_slope(pre_one)).astype(jnp.bfloat16)
    grad_tower = contract_rows(carried_low, grad_pre_one)
    grad_carried = contract_cols(grad_pre_one, tower_full)
    grad_anchor = jnp.zeros_like(anchor)
    cross_grads = [None] * LAYERS
    layer_grads = [None] * LAYERS
    for which_layer in reversed(range(LAYERS)):
        grad_carried, extra_grad, grad_pair, bias_grad = cross_backward(
            anchor, grad_carried, saved_all[which_layer], cross_full, layer_bias, which_layer
        )
        grad_anchor = grad_anchor + extra_grad
        cross_grads[which_layer] = grad_pair
        layer_grads[which_layer] = bias_grad
    grad_anchor = grad_anchor + grad_carried
    grad_emb = grad_anchor[:, : TABLES * EMB].astype(jnp.bfloat16)
    bias_grads = jnp.concatenate(
        [
            jnp.stack(layer_grads).reshape(-1),
            jnp.sum(grad_pre_one.astype(jnp.float32), axis=0),
            jnp.sum(grad_pre_two.astype(jnp.float32), axis=0),
            jnp.sum(grad_logits)[None],
        ]
    )
    dense_grads = (jnp.stack(cross_grads), grad_tower, grad_mid, grad_head)
    return (loss_part, grad_emb, dense_grads, bias_grads)


def shards(
    event_ids,
    row_counts,
    table_slot,
    dense_input,
    labels,
    tables,
    tables_m,
    tables_v,
    cross_uv,
    cross_m,
    cross_v,
    tower_in,
    tower_in_m,
    tower_in_v,
    tower_mid,
    tower_mid_m,
    tower_mid_v,
    head_weight,
    head_m,
    head_v,
    biases,
    biases_m,
    biases_v,
):
    dp_count = lax.axis_size("dp")
    rep_count = lax.axis_size("rep")
    rep_index = lax.axis_index("rep")
    slot_count = tables.shape[0]
    row_total = tables.shape[1]
    device_events = labels.shape[0]
    micro_events = device_events // MICRO
    total_events = float(device_events * dp_count * rep_count)
    shard_set = (cross_uv, tower_in, tower_mid, head_weight)
    shard_low = tuple((shard_piece.astype(jnp.bfloat16) for shard_piece in shard_set))
    event_grid = event_ids.reshape(slot_count, dp_count, rep_count, MICRO, micro_events)
    own_ids = lax.dynamic_index_in_dim(event_grid, rep_index, 2, keepdims=False)
    table_low = tables.astype(jnp.bfloat16)
    selector = (
        table_slot[:, None] == jnp.arange(dp_count * slot_count, dtype=jnp.int32)[None, :]
    ).astype(jnp.bfloat16)
    loss_total = jnp.zeros((), jnp.float32)
    bias_total = jnp.zeros(biases.shape, jnp.float32)
    table_grad = jnp.zeros(tables.shape, jnp.float32)
    dense_total = None
    for micro_index in range(MICRO):
        gathered = (
            lax.all_gather(shard_low[0], ("dp", "rep"), axis=3, tiled=True),
            lax.all_gather(shard_low[1], ("dp", "rep"), axis=1, tiled=True),
            lax.all_gather(shard_low[2], ("dp", "rep"), axis=1, tiled=True),
            lax.all_gather(shard_low[3], ("dp", "rep"), axis=0, tiled=True),
        )
        micro_ids = own_ids[:, :, micro_index, :].reshape(slot_count, dp_count * micro_events)
        looked = jax.vmap(lookup_rows)(table_low, micro_ids)
        outgoing = jnp.transpose(
            looked.reshape(slot_count, dp_count, micro_events, EMB), (1, 0, 2, 3)
        )
        arrived = lax.all_to_all(outgoing, "dp", split_axis=0, concat_axis=0, tiled=True)
        by_slot = arrived.reshape(dp_count * slot_count, micro_events, EMB)
        picked = jnp.einsum(
            "ts,sec->tec", selector, by_slot, preferred_element_type=jnp.float32
        ).astype(jnp.bfloat16)
        emb_flat = jnp.transpose(picked, (1, 0, 2)).reshape(micro_events, TABLES * EMB)
        row_lo = micro_index * micro_events
        dense_rows = dense_input[row_lo : row_lo + micro_events]
        target = labels[row_lo : row_lo + micro_events].astype(jnp.float32)
        loss_part, grad_emb, dense_grads, bias_grads = micro_step(
            gathered, biases, emb_flat, dense_rows, target, total_events
        )
        loss_total = loss_total + loss_part
        bias_total = bias_total + bias_grads
        if micro_index == 0:
            dense_total = dense_grads
        else:
            dense_total = tuple(
                (running + fresh_part for running, fresh_part in zip(dense_total, dense_grads))
            )
        grad_tables = jnp.transpose(grad_emb.reshape(micro_events, TABLES, EMB), (1, 0, 2))
        slot_grads = jnp.einsum(
            "ts,tec->sec", selector, grad_tables, preferred_element_type=jnp.float32
        ).astype(jnp.bfloat16)
        returned = lax.all_to_all(
            slot_grads.reshape(dp_count, slot_count, micro_events, EMB),
            "dp",
            split_axis=0,
            concat_axis=0,
            tiled=True,
        )
        entries = jnp.transpose(returned, (1, 0, 2, 3)).reshape(
            slot_count, dp_count * micro_events, EMB
        )
        table_grad = table_grad + jax.vmap(
            lambda entry_rows, positions: accumulate_rows(entry_rows, positions, row_total)
        )(entries, micro_ids)
    dense_total = (
        lax.psum_scatter(dense_total[0], ("dp", "rep"), scatter_dimension=3, tiled=True),
        lax.psum_scatter(dense_total[1], ("dp", "rep"), scatter_dimension=1, tiled=True),
        lax.psum_scatter(dense_total[2], ("dp", "rep"), scatter_dimension=1, tiled=True),
        lax.psum_scatter(dense_total[3], ("dp", "rep"), scatter_dimension=0, tiled=True),
    )
    table_grad = lax.psum(table_grad, "rep")
    bias_total, loss_total = lax.psum((bias_total, loss_total), ("dp", "rep"))
    fresh_tab, fresh_tab_m, fresh_tab_v = adamw_update(
        tables, tables_m, tables_v, table_grad, RATE_TABLE
    )
    in_use = (jnp.arange(row_total, dtype=jnp.int32)[None, :] < row_counts[:, None])[:, :, None]
    fresh_tab = jnp.where(in_use, fresh_tab, tables)
    fresh_tab_m = jnp.where(in_use, fresh_tab_m, tables_m)
    fresh_tab_v = jnp.where(in_use, fresh_tab_v, tables_v)
    weight_set = shard_set + (biases,)
    grad_set = tuple(dense_total) + (bias_total,)
    states = (
        (cross_m, cross_v, RATE_DENSE),
        (tower_in_m, tower_in_v, RATE_DENSE),
        (tower_mid_m, tower_mid_v, RATE_DENSE),
        (head_m, head_v, RATE_DENSE),
        (biases_m, biases_v, RATE_BIAS),
    )
    results = []
    for weight, gradient, state in zip(weight_set, grad_set, states):
        fresh, moment_new, second = adamw_update(weight, state[0], state[1], gradient, state[2])
        results.append((fresh, moment_new, second, fresh.astype(jnp.bfloat16)))
    return (
        loss_total,
        fresh_tab,
        fresh_tab_m,
        fresh_tab_v,
        fresh_tab.astype(jnp.bfloat16),
        results[0][0],
        results[0][1],
        results[0][2],
        results[0][3],
        results[1][0],
        results[1][1],
        results[1][2],
        results[1][3],
        results[2][0],
        results[2][1],
        results[2][2],
        results[2][3],
        results[3][0],
        results[3][1],
        results[3][2],
        results[3][3],
        results[4][0],
        results[4][1],
        results[4][2],
        results[4][3],
    )


MESH = pl.DeviceIdType.MESH
F32 = jnp.float32
BF = jnp.bfloat16
LN = 1152
RB = 112
BIASES = 5130
CH = [(0, 256), (256, 256), (512, 256), (768, 256), (1024, 128)]
M0, M1, IN, C2, C1, C0 = range(6)
ITEMS = [
    (16, 1024, True, 0, 0),
    (16, 1024, False, 0, 16),
    (32, 1024, True, 1, 0),
    (16, LN, True, 2, 0),
    (16, LN, False, 3, 0),
    (16, LN, False, 4, 0),
]
SUMS = [(32, 1024), (32, 1024), (16, LN), (16, LN), (16, LN)]
A, I, U = range(3)
PARTS = [(0, 48, True), (48, 48, False), (96, 16, False)]


def nt(a, b):
    return lax.dot_general(a, b, (((1,), (1,)), ((), ())), preferred_element_type=F32)


def nn(a, b):
    return lax.dot_general(a, b, (((1,), (0,)), ((), ())), preferred_element_type=F32)


def tn(a, b):
    return lax.dot_general(a, b, (((0,), (0,)), ((), ())), preferred_element_type=F32)


def sig(v):
    return 1.0 / (1.0 + jnp.exp(-v))


def slope(v):
    s = sig(v)
    return s * (1.0 + v * (1.0 - s))


def place(k):
    rep, d = k % 2, k // 2
    return rep, d % 2, (d // 2) % 2, d // 4


def mega_body(total, names, *refs):
    B = types.SimpleNamespace(**dict(zip(names, refs)))
    buf = lambda kind, n: getattr(B, kind + str(n))
    ts, inv = B.ts, B.inv
    G, E, D, eout, tabr = B.G, B.E, B.D, B.eout, B.tabr
    xT, dx, xl, qc, pr = B.xT, B.dx, B.xl, B.qc, B.pr
    VT, UT, h1, h2 = B.VT, B.UT, B.h1, B.h2
    d0, dql, dpr, DE, M, R = B.d0, B.dql, B.dpr, B.DE, B.M, B.R
    ids_ref, tab_ref, bia = B.ids_v, B.gg, B.bia
    xr, a1, a2, d1, d2 = dx, dx, d0, h1, h2
    gt, gg_, gtc, MO = B.gt, B.gg, B.gtc, B.MO
    me = lax.axis_index("dp")
    r = lax.axis_index("rep")
    x, y, z = me % 2, (me // 2) % 2, me // 4
    dev = lambda zz, yy, xx: zz * 4 + yy * 2 + xx
    zp = [z + 1 - 2 * (z % 2), (z + 2) % 4, 3 - z]
    own = me * 2 + r
    xpeer, ypeer, core = (dev(z, y, 1 - x), r), (dev(z, 1 - y, x), r), (me, 1 - r)
    zpeer = [(dev(q, y, x), r) for q in zp]

    loads = [
        pltpu.make_async_copy(src, dst, B.lsem.at[i])
        for i, (src, dst) in enumerate(
            ((B.cr, B.cr_v), (B.ti, B.ti_v), (B.tm, B.tm_v), (B.hd, B.hd_v), (B.tab, B.gg),
             (B.ids, B.ids_v), (B.dns, B.dns_v), (B.lab, B.lab_v), (B.bi, B.bi_v)))
    ]
    for c in loads:
        c.start()
    bar = pltpu.get_barrier_semaphore()
    for i in range(1, 16):
        pl.semaphore_signal(bar, inc=1, device_id=((me + i) % 16, r), device_id_type=MESH)
    pl.semaphore_signal(bar, inc=1, device_id=core, device_id_type=MESH)

    cr, ti, tm, hd = B.cr_v, B.ti_v, B.tm_v, B.hd_v
    for c in loads[:4]:
        c.wait()
    G[own, 0:48, 0:1024] = cr[:, 0:1024].astype(BF)
    G[own, 48:80, 0:1024] = ti[:, 0:1024].astype(BF)
    G[own, 80:112, 0:1024] = tm[...].astype(BF)
    eye = lax.broadcasted_iota(jnp.int32, (32, 32), 0) == lax.broadcasted_iota(jnp.int32, (32, 32), 1)
    hcol = jnp.sum(jnp.where(eye, jnp.broadcast_to(hd[...].reshape(1, 32), (32, 32)), 0.0), axis=1, keepdims=True)
    more = jnp.concatenate([jnp.zeros((32, 3), F32), ti[:, 1024:1027], jnp.zeros((32, 58), F32), jnp.broadcast_to(hcol, (32, 64))], axis=1)
    ends = jnp.concatenate([cr[:, 1024:1027], jnp.zeros((48, 125), F32)], axis=1) + jnp.concatenate([more, jnp.zeros((16, 128), F32)], axis=0)
    G[own, 0:48, 1024:LN] = ends.astype(BF)
    pl.semaphore_wait(bar, 16)

    cnt = [0, 0, 0]
    sends = []

    def wcopy(p, k, dst, si):
        lo, n, _ = PARTS[p]
        at = (k, pl.ds(lo, n), pl.ds(0, LN if p == A else 1024))
        return pltpu.make_async_remote_copy(
            src_ref=G.at[at], dst_ref=G.at[at],
            send_sem=B.wss.at[p, si], recv_sem=B.wrs.at[p, k], device_id=dst, device_id_type=MESH)

    def wsend(p, k, dst):
        c = wcopy(p, k, dst, cnt[p])
        cnt[p] += 1
        c.start()
        sends.append(c)

    def wwait(p, k):
        wcopy(p, k, core, 0).wait_recv()

    p1 = [ypeer if p[2] else xpeer for p in PARTS]
    p2 = [xpeer if p[2] else ypeer for p in PARTS]
    key = lambda zz, yy, xx: dev(zz, yy, xx) * 2 + r
    inner = (z == 1) | (z == 2)
    zq = [zp[0], jnp.where(inner, zp[2], zp[1]), jnp.where(inner, zp[1], zp[2])]
    on_to = [zp[2], zp[0], zp[0]]
    isends = []

    def isend(p, k, zz):
        c = wcopy(p, k, (dev(zz, y, x), r), cnt[p])
        cnt[p] += 1
        isends.append(c)

        @pl.when(inner)
        def _():
            c.start()

    def f_own(p):
        wsend(p, own, (dev(zp[0], y, x), r))
        isend(p, own, zp[2])
        wsend(p, own, p1[p])
        wsend(p, own, p2[p])

    def f_core(p):
        wsend(p, own, core)

    def fwd_z(p, i):
        k = key(zq[i], y, x)
        wwait(p, k)
        isend(p, k, on_to[i])
        wsend(p, k, p1[p])
        wsend(p, k, p2[p])
        wsend(p, k, core)

    def up_down(p, k):
        if p == U:
            wsend(p, k, (dev(zp[0], y, x), r))
            isend(p, k, zp[2])

    def fwd_zl(p, i, c):
        k = key(zq[i], (y + c // 2) % 2, (x + c % 2) % 2)
        wwait(p, k)
        isend(p, k, on_to[i])
        wsend(p, k, core)

    def fwd_1(p, i):
        q = z if i < 0 else zq[i]
        k = key(q, 1 - y, x) if PARTS[p][2] else key(q, y, 1 - x)
        wwait(p, k)
        up_down(p, k)
        wsend(p, k, p2[p])
        wsend(p, k, core)

    def fwd_2(p, i, o):
        q = z if i < 0 else zq[i]
        k = key(q, (y + o) % 2, 1 - x) if PARTS[p][2] else key(q, 1 - y, (x + o) % 2)
        wwait(p, k)
        up_down(p, k)
        wsend(p, k, core)

    def core_wait(p):
        def cw(i, _):
            wwait(p, i * 2 + (1 - r))
            return 0
        lax.fori_loop(0, 16, cw, 0)

    def f_prep():
        loads[4].wait()
        loads[5].wait()
        for s in range(2):
            for j in range(32):
                g, h = j // 4, j % 4
                t = tab_ref[pl.ds(2 * j + s, 39, stride=64), :]
                tabr[s, g * 40 : (g + 1) * 40, h * 128 : (h + 1) * 128] = jnp.concatenate([t, jnp.zeros((1, 128), F32)], axis=0).astype(BF)

    def id_rows(d):
        return ids_ref[:, pl.ds(pl.multiple_of((d * 2 + r) * 384, 128), 384)]

    def one_hot(lo):
        return (lax.broadcasted_iota(jnp.int32, (512, 384), 0) == lo).astype(F32).astype(BF)

    def look(d):
        idv = id_rows(d)
        outs = []
        for s in range(2):
            ids = idv[s : s + 1]
            lo, hi = ids % 512, ids // 512
            res = nn(tabr[s], one_hot(lo))
            e = jnp.zeros((40, 384), F32)
            for g in range(8):
                e = e + jnp.where(hi == g, res[g * 40 : (g + 1) * 40], 0.0)
            outs.append(e)
        return jnp.concatenate(outs, axis=0).astype(BF)

    def ecopy(d, land):
        return pltpu.make_async_remote_copy(
            src_ref=eout.at[d], dst_ref=E.at[land], send_sem=B.ess.at[d], recv_sem=B.ers.at[land], device_id=(d, r), device_id_type=MESH)

    def dcopy(d, land):
        return pltpu.make_async_remote_copy(
            src_ref=eout.at[d], dst_ref=D.at[land], send_sem=B.dss.at[d], recv_sem=B.drs.at[land], device_id=(d, r), device_id_type=MESH)

    def nth(i):
        j, w = i // 4, i % 4
        zz = jnp.where(j == 0, zp[1], jnp.where(j == 1, zp[2], jnp.where(j == 2, zp[0], z)))
        return dev(zz, (y + w // 2) % 2, (x + w) % 2)

    def looks(a, b):
        def step(i, _):
            d = nth(i)
            eout[d] = look(d)

            @pl.when(i != 12)
            def _():
                ecopy(d, me).start()
            return 0
        lax.fori_loop(a, b, step, 0)

    x0 = lambda lo, n: xl[0, :, lo : lo + n].astype(F32)

    def f_rows():
        E[me] = eout[me]
        for n in range(32):
            slot_table = jnp.int32(TABLES)
            for t in range(TABLES):
                slot_table = jnp.where(ts[t] == n, t, slot_table)
            inv[n] = slot_table
        loads[8].wait()
        bv = B.bi_v[...].reshape(1, BIASES)
        bia[...] = jnp.zeros_like(bia)
        for i in range(3):
            bia[i : i + 1, 0:1027] = bv[:, 1027 * i : 1027 * i + 1027]
        bia[3:4, 0:1024] = bv[:, 3081:4105]
        bia[4:5, 0:1024] = bv[:, 4105:5129]
        bia[5:6, :] = jnp.broadcast_to(bv[:, 5129:5130], (1, LN))
        loads[6].wait()
        loads[7].wait()

        def ew(i, _):
            d = (me + i) % 16
            ecopy(d, d).wait()
            return 0

        lax.fori_loop(1, 16, ew, 0)
        for t in range(26):
            s = ts[t]
            blk = E[s // 2].astype(F32)
            e = jnp.where(s % 2 == 1, blk[40:80], blk[0:40])
            xT[39 * t : 39 * t + 39, :] = e[0:39]
        xT[1014:1027, :] = B.dns_v[...].astype(BF).astype(F32)
        xT[1027:LN, :] = jnp.zeros((LN - 1027, 384), F32)
        for i in range(9):
            c = slice(128 * i, 128 * i + 128)
            xl[0, :, c] = xT[c, :].T.astype(BF)

    def f_split():
        core_wait(A)
        for l in range(3):
            for lo, n in CH:
                w = G[:, 16 * l : 16 * l + 16, lo : lo + n].astype(F32).reshape(32, 2, 8, n)
                if lo == 1024:
                    w = jnp.where(lax.broadcasted_iota(jnp.int32, w.shape, 3) < 3, w, 0.0)
                VT[l, :, lo : lo + n] = w[:, 0].reshape(256, n).astype(BF)
                UT[l, :, lo : lo + n] = w[:, 1].reshape(256, n).astype(BF)

    def f_cross():
        for l in range(3):
            pr[l] = nt(xl[l], VT[l]).astype(BF)
            for lo, n in CH:
                q = nn(pr[l], UT[l, :, lo : lo + n]) + bia[l : l + 1, lo : lo + n]
                qc[l, :, lo : lo + n] = q
                v = x0(lo, n) * q + (x0(lo, n) if l == 0 else xr[:, lo : lo + n])
                if l < 2:
                    xr[:, lo : lo + n] = v
                xl[l + 1, :, lo : lo + n] = v.astype(BF)

    def f_tower_one():
        core_wait(I)
        x_end = pltpu.roll(xl[3, :, 1024:LN].astype(F32), 3, 1).astype(BF)
        for n in range(4):
            c = slice(256 * n, 256 * n + 256)
            a = nt(xl[3, :, 0:1024], G[8 * n : 8 * n + 8, 48:80, 0:1024].reshape(256, 1024)) + bia[3:4, c]
            a = a + nt(x_end, G[8 * n : 8 * n + 8, 0:32, 1024:LN].reshape(256, 128))
            a1[:, c] = a
            h1[:, c] = (a * sig(a)).astype(BF)

    def f_tower_two():
        core_wait(U)
        for n in range(4):
            c = slice(256 * n, 256 * n + 256)
            a = nt(h1[...], G[8 * n : 8 * n + 8, 80:112, 0:1024].reshape(256, 1024)) + bia[4:5, c]
            a2[:, c] = a
            h2[:, c] = (a * sig(a)).astype(BF)

    f_own(I)
    f_own(A)
    f_own(U)
    fwd_z(I, 0)
    fwd_z(I, 1)
    f_prep()
    fwd_z(A, 0)
    fwd_z(A, 1)
    fwd_1(U, -1)
    looks(0, 1)
    fwd_1(I, 0)
    f_core(A)
    fwd_1(A, -1)
    looks(1, 2)
    fwd_2(A, -1, 0)
    looks(2, 3)
    fwd_z(A, 2)
    fwd_1(A, 0)
    fwd_z(I, 2)
    fwd_1(A, 1)
    fwd_2(U, -1, 0)
    fwd_2(U, -1, 1)
    fwd_1(I, 1)
    looks(3, 4)
    fwd_2(I, -1, 0)
    fwd_1(I, -1)
    looks(4, 5)
    fwd_2(A, -1, 1)
    for c in range(4):
        fwd_zl(U, 1, c)
    fwd_1(A, 2)
    looks(5, 6)
    looks(6, 7)
    fwd_1(I, 2)
    fwd_2(I, 2, 0)
    fwd_2(I, 0, 0)
    fwd_2(I, 1, 1)
    fwd_2(A, 0, 0)
    fwd_2(A, 2, 0)
    fwd_2(I, 1, 0)
    fwd_2(A, 1, 0)
    fwd_2(A, 0, 1)
    looks(7, 8)
    looks(8, 9)
    fwd_2(A, 1, 1)
    looks(9, 10)
    looks(10, 11)
    looks(11, 12)
    fwd_2(I, -1, 1)
    looks(12, 13)
    f_core(I)
    looks(13, 14)
    for c in range(4):
        fwd_zl(U, 0, c)
    fwd_2(I, 0, 1)
    looks(14, 15)
    fwd_2(I, 2, 1)
    looks(15, 16)
    fwd_2(A, 2, 1)
    f_core(U)
    f_split()
    for c in range(4):
        fwd_zl(U, 2, c)
    f_rows()
    f_cross()
    f_tower_one()
    f_tower_two()
    hc = G[:, 0:32, 1024:LN].reshape(1024, 128)
    zl = nn(h2[...], hc)
    zl = jnp.where(lax.broadcasted_iota(jnp.int32, zl.shape, 1) < 64, pltpu.roll(zl, 64, 1), zl) + bia[5:6, 0:128]
    yl = jnp.broadcast_to(B.lab_v[...].reshape(1, 384).astype(F32), (128, 384)).T
    lossv = jnp.maximum(zl, 0.0) + jnp.log1p(jnp.exp(-jnp.abs(zl))) - yl * zl
    dz = (sig(zl) - yl) / total
    M[...] = jnp.zeros_like(M)
    M[6:7, 0:128] = jnp.sum(lossv, axis=0, keepdims=True)
    M[7:8, 0:128] = jnp.sum(dz, axis=0, keepdims=True)
    hrow = hc.astype(F32).T[64:65]
    for n in range(8):
        c = slice(128 * n, 128 * n + 128)
        M[5:6, c] = jnp.sum(dz * h2[:, c].astype(F32), axis=0, keepdims=True)
        g = (dz * hrow[:, c] * slope(a2[:, c])).astype(BF)
        d2[:, c] = g
        M[4:5, c] = jnp.sum(g.astype(F32), axis=0, keepdims=True)

    nsem = [0]

    def go(src, dst, dst_dev):
        i = nsem[0]
        nsem[0] += 1
        c = pltpu.make_async_remote_copy(
            src_ref=src, dst_ref=dst, send_sem=B.rss.at[i], recv_sem=B.rrs.at[i], device_id=dst_dev, device_id_type=MESH)
        c.start()
        sends.append(c)
        return c

    st = {}

    def axes(n):
        return (y, x, ypeer, xpeer) if ITEMS[n][2] else (x, y, xpeer, ypeer)

    def s0(n):
        g = buf("g", n)
        st[n] = go(g.at[1 - r], buf("C", n), core)

    def s1(n):
        a, b, pa, pb = axes(n)
        st[n].wait_recv()
        g, c = buf("g", n), buf("C", n)
        st[n] = []
        for bb in (1 - b, b):
            g[r, 1 - a, bb] = (g[r, 1 - a, bb].astype(F32) + c[1 - a, bb].astype(F32)).astype(BF)
            st[n].append(go(g.at[r, 1 - a, bb], buf("P", n).at[bb], pa))

    def s2(n):
        a, b, pa, pb = axes(n)
        st[n][0].wait_recv()
        g, c, p = buf("g", n), buf("C", n), buf("P", n)
        g[r, a, 1 - b] = (g[r, a, 1 - b].astype(F32) + c[a, 1 - b].astype(F32) + p[1 - b].astype(F32)).astype(BF)
        st[n].append(go(g.at[r, a, 1 - b], buf("Q", n), pb))

    def s3(n):
        a, b, pa, pb = axes(n)
        st[n][1].wait_recv()
        st[n][2].wait_recv()
        g, c, p, q = buf("g", n), buf("C", n), buf("P", n), buf("Q", n)
        st[n] = []
        for i, zz in enumerate(zp):
            g[r, a, b, zz] = (g[r, a, b, zz].astype(F32) + c[a, b, zz].astype(F32) + p[b, zz].astype(F32) + q[zz].astype(F32)).astype(BF)
            st[n].append(go(g.at[r, a, b, zz], buf("T", n).at[i], zpeer[i]))

    writes = []

    def write(src, dst):
        c = pltpu.make_async_copy(src, dst, B.osem.at[len(writes)])
        c.start()
        writes.append(c)

    def s4(n):
        a, b, pa, pb = axes(n)
        for c in st[n]:
            c.wait_recv()
        g, c, p, q, t = buf("g", n), buf("C", n), buf("P", n), buf("Q", n), buf("T", n)
        nb, _, _, out, at = ITEMS[n]
        gradient = (
            g[r, a, b, z].astype(F32) + c[a, b, z].astype(F32) + p[b, z].astype(F32) + q[z].astype(F32)
            + (t[0].astype(F32) + t[1].astype(F32) + t[2].astype(F32)))
        buf("w", out)[at : at + nb] = gradient
        write(buf("w", out).at[pl.ds(at, nb)], buf("o", out).at[pl.ds(at, nb)])

    def parts_of(out):
        return [n for n, item in enumerate(ITEMS) if item[3] == out]

    def put(out, base, g):
        for n in parts_of(out):
            nb, _, yfirst, _, at = ITEMS[n]
            for i in range(g.shape[0] // 32):
                rep, xx, yy, zz = place(base + i)
                a, b = (yy, xx) if yfirst else (xx, yy)
                buf("g", n)[rep, a, b, zz] = g[i * 32 + at : i * 32 + at + nb].astype(BF)

    MS, MX = B.MS, B.MX

    def grad_mid():
        for n in range(4):
            put(0, 8 * n, tn(d2[:, 256 * n : 256 * n + 256], h1[...]))
        for n in parts_of(0):
            s0(n)

    def down_one():
        for n in range(4):
            c = slice(256 * n, 256 * n + 256)
            a1[:, c] = nn(d2[...], G[:, 80:112, c].reshape(1024, 256)) * slope(a1[:, c])
        for n in range(4):
            c = slice(256 * n, 256 * n + 256)
            g = a1[:, c].astype(BF)
            d1[:, c] = g
            M[3:4, c] = jnp.sum(g.astype(F32), axis=0, keepdims=True)

    def grad_in():
        for n in range(4):
            g = d1[:, 256 * n : 256 * n + 256]
            put(1, 8 * n, tn(g, xl[3, :, 0:1024]))
            B.TE[256 * n : 256 * n + 256] = pltpu.roll(tn(g, xl[3, :, 1024:LN]), 3, 1)
        for n in parts_of(1):
            s0(n)

    def down_x():
        for lo, n in CH[:4]:
            dx[:, lo : lo + n] = nn(d1[...], G[:, 48:80, lo : lo + n].reshape(1024, n))
        g = pltpu.roll(nn(d1[...], G[:, 0:32, 1024:LN].reshape(1024, 128)), 125, 1)
        dx[:, 1024:LN] = jnp.where(lax.broadcasted_iota(jnp.int32, g.shape, 1) < 3, g, 0.0)

    def chain(l):
        dq_ref = dql.at[l]
        for lo, n in CH:
            g = dx[:, lo : lo + n]
            dq = g * x0(lo, n)
            M[l : l + 1, lo : lo + n] = jnp.sum(dq, axis=0, keepdims=True)
            dq_ref[:, lo : lo + n] = dq.astype(BF)
            e = g * qc[l, :, lo : lo + n]
            d0[:, lo : lo + n] = e if l == 2 else d0[:, lo : lo + n] + e
        dpr[l] = nt(dq_ref[...], UT[l]).astype(BF)
        for lo, n in CH:
            v = dx[:, lo : lo + n] + nn(dpr[l], VT[l, :, lo : lo + n])
            if l:
                dx[:, lo : lo + n] = v
            else:
                d0[:, lo : lo + n] = d0[:, lo : lo + n] + v
        if l == 0:
            st[-1] = go(M, B.MC, core)

    def cross_grads(l):
        gr = buf("g", C0 - l)
        yfirst = ITEMS[C0 - l][2]
        for lo, n in CH:
            gu = tn(pr[l], dql[l, :, lo : lo + n]).reshape(32, 8, n)
            gv = tn(dpr[l], xl[l, :, lo : lo + n]).reshape(32, 8, n)
            gg = jnp.concatenate([gv, gu], axis=1)
            if lo == 1024 and l:
                te = B.TE[...].reshape(32, 32, 128)
                gg = gg + (te[:, 0:16] if l == 2 else te[:, 16:32])
            gg = gg.astype(BF)
            for k in range(32):
                rep, xx, yy, zz = place(k)
                a, b = (yy, xx) if yfirst else (xx, yy)
                gr[rep, a, b, zz, :, lo : lo + n] = gg[k]
        s0(C0 - l)

    def back_rows(d):
        return jnp.concatenate([DE[inv[2 * d]], DE[inv[2 * d + 1]]], axis=0).astype(BF)

    def rows_out():
        for i in range(9):
            c = slice(128 * i, 128 * i + 128)
            xT[c, :] = d0[:, c].T
        for t in range(26):
            DE[t] = jnp.concatenate([xT[39 * t : 39 * t + 39, :], jnp.zeros((1, 384), F32)], axis=0)
        DE[26] = jnp.zeros((40, 384), F32)

        def dstep(i, _):
            d = nth(i)
            eout[d] = back_rows(d)

            @pl.when(i != 12)
            def _():
                dcopy(d, me).start()
            return 0

        lax.fori_loop(0, 16, dstep, 0)
        D[me] = eout[me]

    def one_part(i, s):
        d = nth(15 - i)
        ids = id_rows(d)[s : s + 1]
        lo, hi = ids % 512, ids // 512
        e = D[d].astype(F32)[40 * s : 40 * s + 40]
        lhs = jnp.concatenate([jnp.where(hi == g, e, 0.0) for g in range(8)], axis=0).astype(BF)
        return lhs, one_hot(lo)

    def rows_in(k):
        for i in (2 * k, 2 * k + 1):
            if i != 3:
                d = nth(15 - i)
                dcopy(d, d).wait_recv()
        for s in range(2):
            u, v = one_part(2 * k, s), one_part(2 * k + 1, s)
            p = nt(jnp.concatenate([u[0], v[0]], axis=1), jnp.concatenate([u[1], v[1]], axis=1))
            R[s] = p if k == 0 else R[s] + p

    def table_sum():
        for s in range(2):
            for j in range(32):
                g, h = j // 4, j % 4
                gg_[pl.ds(2 * j + s, 39, stride=64), :] = R[s, g * 40 : g * 40 + 39, h * 128 : (h + 1) * 128]
        st[-2] = go(gg_, gtc, core)

    def table_both():
        st[-2].wait_recv()
        gtc[...] = gg_[...] + gtc[...]
        write(gtc, gt)

    def small(i):
        if i == 1:
            st[-1].wait_recv()
            MS[0] = M[...] + B.MC[...]
            st[-1] = go(MS.at[0], MX.at[0], xpeer)
        elif i == 2:
            st[-1].wait_recv()
            MS[1] = MS[0] + MX[0]
            st[-1] = go(MS.at[1], MX.at[1], ypeer)
        elif i == 3:
            st[-1].wait_recv()
            MS[2] = MS[1] + MX[1]
            st[-1] = [go(MS.at[2], MX.at[2 + j], zpeer[j]) for j in range(3)]
        else:
            for c in st[-1]:
                c.wait_recv()
            pos = [MS[2], MX[2], MX[3], MX[4]]
            u = jnp.where(z % 2 == 0, pos[0], pos[1]) + jnp.where(z % 2 == 0, pos[1], pos[0])
            v = jnp.where(z % 2 == 0, pos[2], pos[3]) + jnp.where(z % 2 == 0, pos[3], pos[2])
            B.MC[...] = jnp.where(z < 2, u, v) + jnp.where(z < 2, v, u)
            write(B.MC, MO)

    grad_mid()
    down_one()
    down_x()
    s1(M0)
    s1(M1)
    chain(2)
    grad_in()
    chain(1)
    chain(0)
    s2(M1)
    s2(M0)
    rows_out()
    cross_grads(0)
    s1(IN)
    cross_grads(2)
    rows_in(0)
    cross_grads(1)
    small(1)
    s1(C0)
    rows_in(1)
    rows_in(2)
    s3(M1)
    small(2)
    rows_in(3)
    rows_in(4)
    s2(IN)
    rows_in(5)
    s2(C0)
    s1(C2)
    rows_in(6)
    s3(M0)
    rows_in(7)
    s4(M1)
    s1(C1)
    small(3)
    s3(IN)
    s2(C1)
    table_sum()
    s2(C2)
    small(4)
    s3(C0)
    s3(C2)
    table_both()
    s4(IN)
    s3(C1)
    s4(C0)
    s4(M0)
    s4(C2)
    s4(C1)

    def dw(i, _):
        d = (me + i) % 16
        dcopy(d, d).wait_send()
        return 0

    lax.fori_loop(1, 16, dw, 0)
    for c in sends:
        c.wait_send()
    for c in writes:
        c.wait()

    @pl.when(inner)
    def _():
        for c in isends:
            c.wait_send()


def mega(total, ts, ids, tab, cr, ti, tm, hd, dns, lab, bi):
    V, S = pltpu.VMEM, jax.ShapeDtypeStruct
    vm, sm, an = pl.BlockSpec(memory_space=pltpu.VMEM), pl.BlockSpec(memory_space=pltpu.SMEM), pl.BlockSpec(memory_space=pl.ANY)
    ins = dict(ts=ts, ids=ids, tab=tab, cr=cr, ti=ti, tm=tm, hd=hd, dns=dns, lab=lab, bi=bi)
    outs = dict(gt=S((2496, 128), F32), MO=S((8, LN), F32))
    for n, shape in enumerate(SUMS):
        outs["o" + str(n)] = S(shape, F32)
    like = lambda a: V(a.shape, a.dtype)
    dma = pltpu.SemaphoreType.DMA
    scr = dict(
        ids_v=like(ids), cr_v=like(cr), ti_v=like(ti), tm_v=like(tm), hd_v=like(hd), dns_v=like(dns), lab_v=like(lab), bi_v=like(bi),
        G=V((32, RB, LN), BF), E=V((16, 80, 384), BF), D=V((16, 80, 384), BF), eout=V((16, 80, 384), BF), tabr=V((2, 320, 512), BF),
        xT=V((LN, 384), F32), dx=V((384, LN), F32), xl=V((4, 384, LN), BF), qc=V((3, 384, LN), F32), pr=V((3, 384, 256), BF),
        VT=V((3, 256, LN), BF), UT=V((3, 256, LN), BF), h1=V((384, 1024), BF), h2=V((384, 1024), BF),
        d0=V((384, LN), F32), dql=V((3, 384, LN), BF), dpr=V((3, 384, 256), BF), DE=V((27, 40, 384), F32), M=V((8, LN), F32), R=V((2, 320, 512), F32),
        MC=V((8, LN), F32), MS=V((3, 8, LN), F32), MX=V((5, 8, LN), F32), TE=V((1024, 128), F32), gg=V((2496, 128), F32), gtc=V((2496, 128), F32), bia=V((8, LN), F32),
        inv=pltpu.SMEM((32,), jnp.int32), lsem=dma((9,)), wss=dma((3, 40)), wrs=dma((3, 32)), ess=dma((16,)), ers=dma((16,)), dss=dma((16,)), drs=dma((16,)),
        rss=dma((64,)), rrs=dma((64,)), osem=dma((9,)))
    for n, shape in enumerate(SUMS):
        scr["w" + str(n)] = V(shape, F32)
    for n, (nb, L, *_) in enumerate(ITEMS):
        for kind, lead in (("g", (2, 2, 2, 4)), ("C", (2, 2, 4)), ("P", (2, 4)), ("Q", (4,)), ("T", (3,))):
            scr[kind + str(n)] = V(lead + (nb, L), BF)
    return pl.pallas_call(
        functools.partial(mega_body, total, list(ins) + list(outs) + list(scr)), name="train_step",
        out_shape=tuple(outs.values()), in_specs=[sm] + [an] * 9, out_specs=(an,) * len(outs),
        scratch_shapes=list(scr.values()),
        compiler_params=pltpu.CompilerParams(collective_id=0, has_side_effects=True, vmem_limit_bytes=63 << 20),
    )(*ins.values())


IC5 = 1 / (1 - 0.5**5)


def adamw(w, m, v, g, rate):
    mn = 0.5 * m + 0.5 * g
    vn = 0.5 * v + 0.5 * g * g
    return w - rate * ((mn * IC5) / (jnp.sqrt(vn * IC5) + EPSILON) + WEIGHT_DECAY * w), mn, vn


def update_body(rc, *refs):
    hbm, gt, MO, sums, refs = refs[:18], refs[18], refs[19], refs[20:25], refs[25:]
    dst, loss, vin, vg, vout, refs = refs[:24], refs[24], refs[25:43], refs[43], refs[44:68], refs[68:]
    near, isem, osem = refs[:6], refs[6], refs[7]
    n_in, n_out = [0], [0]

    def load(src, to):
        c = pltpu.make_async_copy(src, to, isem.at[n_in[0]])
        n_in[0] += 1
        c.start()
        return c

    outs = []

    def out(k, rows=None):
        for i in range(4 * k, 4 * k + 4):
            s, d = vout[i], dst[i]
            if rows is not None:
                s, d = s.at[rows], d.at[rows]
            c = pltpu.make_async_copy(s, d, osem.at[n_out[0]])
            n_out[0] += 1
            c.start()
            outs.append(c)

    span = lambda part: pl.ds(832 * part, 832)
    third = lambda part: [load(a.at[span(part)], b.at[span(part)]) for a, b in ((hbm[0], vin[0]), (hbm[1], vin[1]), (hbm[2], vin[2]), (gt, vg))]
    table = [third(0), third(1)]
    dense = {k: [load(hbm[3 * k + j], vin[3 * k + j]) for j in range(3)] for k in (2, 3, 1)}
    gradients = [load(a, b) for a, b in zip((*sums, MO), near)]
    sums, MO = near[:5], near[5]
    table.append(third(2))
    dense.update({k: [load(hbm[3 * k + j], vin[3 * k + j]) for j in range(3)] for k in (4, 5)})
    row = lax.broadcasted_iota(jnp.int32, (64, 128), 0)
    lane = lax.broadcasted_iota(jnp.int32, (64, 128), 1)
    use = ((row // 2) * 128 + lane) < jnp.where(row % 2 == 0, rc[0], rc[1])
    def update_third(part):
        for c in table[part]:
            c.wait()
        for i in range(13):
            q = pl.ds(832 * part + i * 64, 64)
            w, m, v = vin[0][q], vin[1][q], vin[2][q]
            nw, nm, nv = adamw(w, m, v, vg[q], RATE_TABLE)
            nw = jnp.where(use, nw, w)
            vout[0][q] = nw
            vout[1][q] = jnp.where(use, nm, m)
            vout[2][q] = jnp.where(use, nv, v)
            vout[3][q] = nw.astype(BF)
        out(0, span(part))

    update_third(0)
    update_third(1)
    for c in gradients:
        c.wait()
    for k, rows in ((2, [(1, 0, 32)]), (3, [(0, 0, 32)]), (1, [(4, 0, 16), (3, 16, 16), (2, 32, 16)])):
        for c in dense[k]:
            c.wait()
        w_in, m_in, v_in = vin[3 * k : 3 * k + 3]
        for n, lo, nb in rows:
            g = sums[n][:, 0 : w_in.shape[1]]
            if k == 2:
                ends = [a[:, WIDTH : WIDTH + 3] for a in (sums[2], sums[3])]
                g = jnp.concatenate([g, jnp.concatenate(ends, axis=0)], axis=1)
            at = slice(lo, lo + nb)
            w, m, v = adamw(w_in[at], m_in[at], v_in[at], g, RATE_DENSE)
            for o, a in zip(vout[4 * k : 4 * k + 4], (w, m, v, w.astype(BF))):
                o[at] = a
        out(k)
    update_third(2)
    loss[0, 0] = jnp.max(MO[6:7, 0:128])
    k = lax.axis_index("dp") * 2 + lax.axis_index("rep")
    gb = jnp.concatenate([MO[0:1, :WIDTH], MO[1:2, :WIDTH], MO[2:3, :WIDTH], MO[3:4, :1024], MO[4:5, :1024], MO[7:8, :1]], axis=1)
    gh = pltpu.roll(MO[5:6, 0:1024], 1024 - 32 * k, 1)[:, 0:32]
    for k, g, rate in ((4, gh, RATE_DENSE), (5, gb, RATE_BIAS)):
        for c in dense[k]:
            c.wait()
        n = g.shape[1]
        w, m, v = adamw(*(a[...].reshape(1, n) for a in vin[3 * k : 3 * k + 3]), g, rate)
        for o, a in zip(vout[4 * k : 4 * k + 4], (w, m, v, w.astype(BF))):
            o[...] = a.reshape(n)
        out(k)
    for c in outs:
        c.wait()


def update(rc, g, state):
    V, S = pltpu.VMEM, jax.ShapeDtypeStruct
    vm, sm, an = pl.BlockSpec(memory_space=pltpu.VMEM), pl.BlockSpec(memory_space=pltpu.SMEM), pl.BlockSpec(memory_space=pl.ANY)
    flat = [a for kind in state for a in kind]
    kinds = [S(kind[0].shape, t) for kind in state for t in (F32, F32, F32, BF)]
    dma = pltpu.SemaphoreType.DMA
    return pl.pallas_call(
        update_body, name="adamw_step", out_shape=tuple(kinds) + (S((1, 1), F32),),
        in_specs=[sm] + [an] * 25, out_specs=(an,) * 24 + (sm,),
        scratch_shapes=[V(a.shape, F32) for a in flat] + [V((2496, 128), F32)] + [V(a.shape, a.dtype) for a in kinds] + [V(shape, F32) for shape in SUMS] + [V((8, LN), F32), dma((33,)), dma((32,))],
        compiler_params=pltpu.CompilerParams(vmem_limit_bytes=63 << 20),
    )(rc, *flat, *g)


def tab_view(t):
    S, n, C = t.shape
    return jnp.transpose(jnp.transpose(t, (2, 0, 1)).reshape(C, S, n // 128, 128), (0, 2, 1, 3)).reshape(C * S * n // 128, 128)


def tab_unview(v, S=2, n=4096, C=39):
    return jnp.transpose(jnp.transpose(v.reshape(C, n // 128, S, 128), (0, 2, 1, 3)).reshape(C, S, n), (1, 2, 0))


def fast_shards(
    event_ids, row_counts, table_slot, dense_input, labels,
    tables, tables_m, tables_v, cross_uv, cross_m, cross_v,
    tower_in, tower_in_m, tower_in_v, tower_mid, tower_mid_m, tower_mid_v,
    head_weight, head_m, head_v, biases, biases_m, biases_v,
):
    total = float(labels.shape[0] * lax.axis_size("dp") * lax.axis_size("rep"))
    turn = lambda a: jnp.transpose(a, (0, 1, 3, 2)).reshape(48, WIDTH)
    back = lambda a: jnp.transpose(a.reshape(LAYERS, 2, 8, WIDTH), (0, 1, 3, 2))
    state = [
        [tab_view(a) for a in (tables, tables_m, tables_v)],
        [turn(a) for a in (cross_uv, cross_m, cross_v)],
        [a.T for a in (tower_in, tower_in_m, tower_in_v)],
        [a.T for a in (tower_mid, tower_mid_m, tower_mid_v)],
        [head_weight, head_m, head_v],
        [biases, biases_m, biases_v],
    ]
    g = mega(total, table_slot, event_ids, *(kind[0] for kind in state[:5]), dense_input.T, labels, biases)
    o = update(row_counts, g, state)
    return (
        o[24].reshape(()),
        *[tab_unview(a) for a in o[0:4]],
        *[back(a) for a in o[4:8]],
        *[a.T for a in o[8:12]],
        *[a.T for a in o[12:16]],
        *o[16:24],
    )


def solution(mesh):
    placed = (
        P("dp", None),
        P("dp"),
        P(),
        P(("dp", "rep"), None),
        P(("dp", "rep")),
        P("dp", None, None),
        P("dp", None, None),
        P("dp", None, None),
        P(None, None, None, ("dp", "rep")),
        P(None, None, None, ("dp", "rep")),
        P(None, None, None, ("dp", "rep")),
        P(None, ("dp", "rep")),
        P(None, ("dp", "rep")),
        P(None, ("dp", "rep")),
        P(None, ("dp", "rep")),
        P(None, ("dp", "rep")),
        P(None, ("dp", "rep")),
        P(("dp", "rep")),
        P(("dp", "rep")),
        P(("dp", "rep")),
        P(),
        P(),
        P(),
    )
    fits = mesh.shape["dp"] == 16 and mesh.shape["rep"] == 2
    return jax.shard_map(
        fast_shards if fits else shards,
        mesh=mesh,
        in_specs=placed,
        out_specs=(
            P(),
            P("dp", None, None),
            P("dp", None, None),
            P("dp", None, None),
            P("dp", None, None),
            P(None, None, None, ("dp", "rep")),
            P(None, None, None, ("dp", "rep")),
            P(None, None, None, ("dp", "rep")),
            P(None, None, None, ("dp", "rep")),
            P(None, ("dp", "rep")),
            P(None, ("dp", "rep")),
            P(None, ("dp", "rep")),
            P(None, ("dp", "rep")),
            P(None, ("dp", "rep")),
            P(None, ("dp", "rep")),
            P(None, ("dp", "rep")),
            P(None, ("dp", "rep")),
            P(("dp", "rep")),
            P(("dp", "rep")),
            P(("dp", "rep")),
            P(("dp", "rep")),
            P(),
            P(),
            P(),
            P(),
        ),
        check_vma=False,
    )
```
